32 devices in a mesh: dp: 16 (over z, y, x), rep: 2 (over core).
Axes of the slice: x: 2, y: 2, z: 4, core: 2. Of those that a mesh axis runs over, the one named last changes fastest.
Arguments:
- query_tokens: bfloat16 [512, 32, 768], P(('dp', 'rep')), may hold values from -6 to 6
- passage_tokens: bfloat16 [128, 128, 768], P(('dp', 'rep')), may hold values from -6 to 6
- query_cot: bfloat16 [512, 32, 768], P(('dp', 'rep')), may hold values from -6 to 6
- passage_cot: bfloat16 [128, 128, 768], P(('dp', 'rep')), may hold values from -6 to 6
- positives: int32 [512, 128], P(('dp', 'rep')), may hold values from 0 to 1, as said below
- w_qkv: bfloat16 [2, 768, 2304], P(None, 'dp'), may hold values from -0.21875 to 0.21875
- w_out: bfloat16 [2, 768, 768], P(None, 'dp'), may hold values from -0.625 to 0.625
- w_up: bfloat16 [2, 768, 3072], P(None, 'dp'), may hold values from -0.21875 to 0.21875
- w_down: bfloat16 [2, 3072, 768], P(None, 'dp'), may hold values from -0.109375 to 0.109375
- biases: bfloat16 [2, 10, 768], P(None, None, 'dp'), may hold values from -3 to 3
- gains: bfloat16 [2, 2, 768], P(None, None, 'dp'), may hold values from 0.5 to 1.5
Outputs:
- query_out: bfloat16 [512, 32, 768], P(('dp', 'rep'))
- passage_out: bfloat16 [128, 128, 768], P(('dp', 'rep'))
- query_grad: float32 [512, 32, 768], P(('dp', 'rep'))
- passage_grad: float32 [128, 128, 768], P(('dp', 'rep'))
- query_loss: float32 [512], P(('dp', 'rep'))
- grad_qkv: float32 [2, 768, 2304], P(None, 'dp')
- grad_out: float32 [2, 768, 768], P(None, 'dp')
- grad_up: float32 [2, 768, 3072], P(None, 'dp')
- grad_down: float32 [2, 3072, 768], P(None, 'dp')
- grad_biases: float32 [2, 10, 768], P(None, None, 'dp')
- grad_gains: float32 [2, 2, 768], P(None, None, 'dp')
The draws below stay inside these ranges and needn't reach their ends.
Inputs may be any that keep to these rules, and one draw needn't show every extreme that they name: `positives`: each query has one to three positive passages; some query has three and some one.
All inputs are finite; a program needn't handle non-finite values.
Results may differ from the reference program's by a relative error of at most 0.015.
Values may be sent and summed in bfloat16 or wider, within the bound.
No kernel may reach another device: no remote copies, remote signals or barrier semaphores. Data moves between devices by JAX's collectives and lax.ppermute only.
A program may use at most 256 MiB of HBM per device.

```python
import math
import jax
import jax.numpy as jnp
from jax import lax

D = 768
FF = 3072
HEADS = 12
HEAD = 64
QLEN = 32
PLEN = 128
QUERIES = 512
PASSAGES = 128


def draw_positives(key, part):
    key = jax.random.fold_in(key, 7)
    pick_key, count_key = jax.random.split(key)
    spread = (2 ** 31 - 1) // PASSAGES - 1
    ranks = jax.random.randint(pick_key, (QUERIES, PASSAGES), 0, spread) * PASSAGES + jnp.arange(PASSAGES, dtype=jnp.int32)[None, :]
    unused, chosen = lax.top_k(ranks, 3)
    counts = jax.random.randint(count_key, (QUERIES,), 1, 4)
    rows = jnp.arange(QUERIES, dtype=jnp.int32)
    counts = jnp.where(rows == 0, 3, jnp.where(rows == 1, 1, counts))
    slots = jnp.arange(3, dtype=jnp.int32)
    live = slots[None, :] < counts[:, None]
    hits = (chosen[:, :, None] == jnp.arange(PASSAGES, dtype=jnp.int32)[None, None, :]) & live[:, :, None]
    return jnp.any(hits, axis=1).astype(jnp.int32)


def steps_of(stream_key, shape, pieces, least, top_value):
    factor_of = 1.0
    for axis_at, shards_of in pieces:
        heights = jax.random.uniform(jax.random.fold_in(jax.random.fold_in(stream_key, 6), axis_at), (shards_of,), jnp.float32, least / len(pieces), top_value / len(pieces))
        factor_of = factor_of * jnp.repeat(jnp.exp(heights), shape[axis_at] // shards_of).reshape((-1,) + (1,) * (len(shape) - 1 - axis_at))
    return factor_of


def normal_values(key, shape, scale, bound, cuts=(), kind=jnp.bfloat16):
    level = steps_of(key, shape, cuts, -0.22, 0.18) if cuts else 1.0
    values = jax.random.normal(key, shape, jnp.float32) * scale * level
    return jnp.minimum(jnp.maximum(values, -bound), bound).astype(kind)


def setup_inputs(seed: int = 0) -> dict:
    arg_keys = jax.random.split(jax.random.key(seed), 12)
    return {
        "query_tokens": normal_values(arg_keys[0], (QUERIES, QLEN, D), 1.0, 6.0, ((0, 32),)),
        "passage_tokens": normal_values(arg_keys[1], (PASSAGES, PLEN, D), 1.0, 6.0, ((0, 32),)),
        "query_cot": normal_values(arg_keys[2], (QUERIES, QLEN, D), 1.0, 6.0, ((0, 32),)),
        "passage_cot": normal_values(arg_keys[3], (PASSAGES, PLEN, D), 1.0, 6.0, ((0, 32),)),
        "positives": draw_positives(jax.random.fold_in(arg_keys[11], 71), 0),
        "w_qkv": normal_values(arg_keys[5], (2, D, 3 * D), D ** -0.5, 0.21875, ((1, 16),)),
        "w_out": normal_values(arg_keys[6], (2, D, D), (D // 8) ** -0.5, 0.625, ((1, 16),)),
        "w_up": normal_values(arg_keys[7], (2, D, FF), D ** -0.5, 0.21875, ((1, 16),)),
        "w_down": normal_values(arg_keys[8], (2, FF, D), FF ** -0.5, 0.109375, ((1, 16),)),
        "biases": normal_values(arg_keys[9], (2, 10, D), 0.5, 3.0, ((2, 16),)),
        "gains": jnp.clip(1.0 + 0.1 * jax.random.normal(arg_keys[10], (2, 2, D), jnp.float32), 0.5, 1.5).astype(jnp.bfloat16),
    }


@jax.custom_vjp
def low(v):
    return lax.optimization_barrier(v.astype(jnp.bfloat16)).astype(jnp.float32)

@jax.custom_vjp
def low_back(v):
    return v

def low_keep(v):
    return (low(v), None)

def low_pass(kept, grad):
    return (grad,)

def back_keep(v):
    return (v, None)

def back_low(kept, grad):
    return (low(grad),)
low.defvjp(low_keep, low_pass)
low_back.defvjp(back_keep, back_low)
eps = 1e-05
loss_weight = 32.0
highest = lax.Precision.HIGHEST

def matmul(left, right):
    return jnp.dot(left, right, precision=highest)

def rows_norm(h, gain, shift):
    center = h - lax.optimization_barrier(jnp.mean(h, -1, keepdims=True))
    spread = lax.optimization_barrier(jnp.mean(center * center, -1, keepdims=True))
    return center * lax.rsqrt(spread + eps) * gain + shift

def layer(weights, tokens):
    wqkv, wout, wup, wdown, vecs, gns = weights
    count, length, width = tokens.shape
    flat = tokens.reshape(count * length, width)
    zeros = jnp.zeros((width,), jnp.float32)
    proj = low(low_back(matmul(flat, wqkv) + jnp.concatenate([vecs[0], zeros, vecs[1]])))
    parts = proj.reshape(count, length, 3, HEADS, HEAD)
    query, keys, values = (parts[:, :, 0], parts[:, :, 1], parts[:, :, 2])
    scores = low_back(jnp.einsum('slhd,smhd->shlm', query, keys, precision=highest) * HEAD ** (-0.5))
    probs = low(jax.nn.softmax(scores, -1))
    attn = low(low_back(jnp.einsum('shlm,smhd->slhd', probs, values, precision=highest).reshape(count * length, width)))
    hidden = flat + low_back(matmul(attn, wout) + vecs[2])
    normed = rows_norm(hidden, gns[0], vecs[3])
    upper = low_back(matmul(low(normed), wup) + vecs[4:8].reshape(-1))
    active = low(jax.nn.gelu(upper, approximate=False))
    second = normed + low_back(matmul(active, wdown) + vecs[8])
    return rows_norm(second, gns[1], vecs[9]).reshape(count, length, width)

def run_tower(weights, tokens, block):
    blocks = tokens.reshape(tokens.shape[0] // block, block, tokens.shape[1], tokens.shape[2])
    outs = lax.map(jax.checkpoint(lambda piece: layer(weights, piece)), blocks)
    return outs.reshape(tokens.shape)

def reference(query_tokens, passage_tokens, query_cot, passage_cot, positives, w_qkv, w_out, w_up, w_down, biases, gains):
    params = tuple((a.astype(jnp.float32) for a in (w_qkv, w_out, w_up, w_down, biases, gains)))
    marks = positives.astype(jnp.float32)
    query_block = math.gcd(QUERIES, max(1, 4096 // QLEN))
    passage_block = math.gcd(PASSAGES, max(1, 4096 // PLEN))

    def forward(weights, xq, xp):
        first = tuple((w[0] for w in weights))
        other = tuple((w[1] for w in weights))
        out_q = run_tower(first, xq, query_block)
        out_p = run_tower(other, xp, passage_block)
        cls_q = low(out_q[:, 0, :])
        cls_p = low(out_p[:, 0, :])
        raw = low_back(matmul(cls_q, cls_p.T) * D ** (-0.5))
        top = lax.optimization_barrier(jnp.max(raw, -1, keepdims=True))
        expd = jnp.exp(raw - top)
        total = lax.optimization_barrier(jnp.sum(expd, -1))
        marked = lax.optimization_barrier(jnp.sum(marks * expd, -1))
        return (out_q, out_p, jnp.log(total) - jnp.log(marked))
    xq = query_tokens.astype(jnp.float32)
    xp = passage_tokens.astype(jnp.float32)
    (out_q, out_p, losses), pull = jax.vjp(forward, params, xq, xp)
    grads, grad_q, grad_p = pull((query_cot.astype(jnp.float32), passage_cot.astype(jnp.float32), jnp.full((QUERIES,), loss_weight, jnp.float32)))
    return (out_q.astype(jnp.bfloat16), out_p.astype(jnp.bfloat16), grad_q, grad_p, losses, grads[0], grads[1], grads[2], grads[3], grads[4], grads[5])
```

```python
from functools import partial

import jax
import jax.numpy as jnp
from jax import lax
from jax.experimental import pallas as pl
from jax.experimental.pallas import tpu as pltpu
from jax.sharding import PartitionSpec as P

AXES = ("dp", "rep")
BF = jnp.bfloat16
F32 = jnp.float32
D = 768
FF = 3072
HEADS = 12
HEAD = 64
PAIRS = HEADS // 2
BLOCK = 128
TILE = 256
EPS = 1e-05
LOSS_WEIGHT = 32.0
MIB = 2**20
AT_OUT = 3 * D
AT_VEC = 4 * D
W_ONE = 4 * D + 256


def smem():
    return pl.BlockSpec(memory_space=pltpu.SMEM)


def vmem():
    return pl.BlockSpec(memory_space=pltpu.VMEM)


def params(mib):
    return pltpu.CompilerParams(vmem_limit_bytes=mib * MIB)


def send(v, pairs):
    return lax.ppermute(v, AXES, pairs)


class Plan:
    def __init__(self, n, reps):
        self.n, self.reps, self.depth = n, reps, n // 4

    def pairs(self, move):
        return [
            (d * self.reps + r, (d ^ move(r)[0]) * self.reps + (r ^ move(r)[1]))
            for d in range(self.n)
            for r in range(self.reps)
        ]

    def along(self, k):
        return self.pairs(lambda r: (4 * k, 0))

    def first(self):
        return self.pairs(lambda r: (1 + r % 2, 0))

    def second(self):
        return self.pairs(lambda r: (2 - r % 2, 0))

    def sibling(self, q):
        return self.pairs(lambda r: (0, q))


def assemble_kernel(depth, reps, width, where_ref, *refs):
    nb = 4 * reps
    bufs, out = refs[:nb], refs[nb]
    me, core = where_ref[0], where_ref[1]
    for q in range(reps):
        owner = core ^ q
        p1 = 1 + owner % 2
        p2 = 2 - owner % 2
        lanes = pl.ds(pl.multiple_of(owner * width, 128), width)
        for b in range(4):
            flip = [0, p1, p2, 3][b]
            for k in range(depth):
                dst = (me ^ flip) ^ (4 * k)
                out[pl.ds(dst, 1), :, lanes] = bufs[q * 4 + b][pl.ds(k, 1)]


def gather_chunk(plan, where, shard):
    me, core, tower = where[0], where[1], where[2]
    rows, whole = shard.shape[1:]
    width = whole // plan.reps
    mine = lax.dynamic_slice(shard, (tower, 0, core * width), (1, rows, width))
    other = lax.dynamic_slice(shard, (1 - tower, 0, core * width), (1, rows, width))
    got = [mine] + [
        send(other if k % 2 else mine, plan.along(k)) for k in range(1, plan.depth)
    ]
    z = jnp.concatenate(got, 0)
    r1 = send(z, plan.first())
    r2 = send(z, plan.second())
    r3 = send(r1, plan.second())
    bufs = [z, r1, r2, r3]
    for q in range(1, plan.reps):
        bufs += [send(b, plan.sibling(q)) for b in (z, r1, r2, r3)]
    full = pl.pallas_call(
        partial(assemble_kernel, plan.depth, plan.reps, width),
        out_shape=jax.ShapeDtypeStruct((plan.n, rows, whole), BF),
        in_specs=[smem()] + [vmem()] * len(bufs),
        out_specs=vmem(),
        compiler_params=params(24),
        name="assemble",
    )(where, *bufs)
    return full.reshape(plan.n * rows, whole)


def add_kernel(n, wh, table_ref, a_ref, b_ref, s_ref, k_ref):
    lanes = pl.ds(pl.multiple_of(table_ref[n] * wh, 128), wh)
    for j in range(n):
        at = table_ref[j]
        total = a_ref[pl.ds(at, 1), :, lanes].astype(F32) + b_ref[pl.ds(at, 1)].astype(F32)
        o_ref, to = (s_ref, j) if j < n // 2 else (k_ref, j - n // 2)
        o_ref[pl.ds(to, 1)] = total.astype(BF)


def plus(a, b):
    return (a.astype(F32) + b.astype(F32)).astype(BF)


def scatter_chunk(plan, where, grad, rows):
    me, core, tower = where[0], where[1], where[2]
    n = plan.n
    whole = grad.shape[1]
    wh = whole // plan.reps
    g = grad.reshape(n, rows, whole)
    got = [
        send(lax.dynamic_slice_in_dim(g, (core ^ q) * wh, wh, 2), plan.sibling(q))
        for q in range(1, plan.reps)
    ]
    rest = got[0]
    for o in got[1:]:
        rest = plus(rest, o)
    p1 = 1 + core % 2
    p2 = 2 - core % 2
    idx = []
    for b1 in (1, 0):
        for b2 in (1, 0):
            for k in range(plan.depth):
                idx.append(me ^ (b1 * p1) ^ (b2 * p2) ^ (4 * k))
    table = jnp.stack(idx + [core]).astype(jnp.int32)
    half = jax.ShapeDtypeStruct((n // 2, rows, wh), BF)
    hs, hk = pl.pallas_call(
        partial(add_kernel, n, wh),
        out_shape=(half, half),
        in_specs=[smem(), vmem(), vmem()],
        out_specs=[vmem(), vmem()],
        compiler_params=params(24),
        name="pick_add",
    )(table, g, rest)
    r1 = send(hs, plan.first())
    q = n // 4
    ks = plus(hk[:q], r1[:q])
    r2 = send(ks, plan.second())
    kk = plus(hk[q:], r1[q:])
    k2 = [kk[k].astype(F32) + r2[k].astype(F32) for k in range(plan.depth)]
    own, oth = k2[0], None
    for k in range(1, plan.depth):
        s = send(k2[k].astype(BF), plan.along(k)).astype(F32)
        if k % 2:
            oth = s if oth is None else oth + s
        else:
            own = own + s
    pair = jnp.stack([own, oth]).astype(BF)
    pair = jnp.where(tower == 0, pair, pair[::-1])
    parts = [pair] + [send(pair, plan.sibling(q)) for q in range(1, plan.reps)]
    if plan.reps == 2:
        a, b = parts[0].astype(F32), parts[1].astype(F32)
        return jnp.where(core == 0, jnp.concatenate([a, b], 2), jnp.concatenate([b, a], 2))
    full = jnp.zeros((2, rows, whole), F32)
    for q, part in enumerate(parts):
        full = lax.dynamic_update_slice_in_dim(full, part.astype(F32), (core ^ q) * wh, 2)
    return full


def dot(a, b):
    return jnp.dot(a, b, preferred_element_type=F32)


def dot_t(a, b):
    return lax.dot_general(a, b, (((1,), (1,)), ((), ())), preferred_element_type=F32)


def t_dot(a, b):
    return lax.dot_general(a, b, (((0,), (0,)), ((), ())), preferred_element_type=F32)


def normalize(h):
    center = h - jnp.mean(h, -1, keepdims=True)
    rstd = lax.rsqrt(jnp.mean(center * center, -1, keepdims=True) + EPS)
    return center * rstd, rstd


def lane_masks():
    lane = lax.broadcasted_iota(jnp.int32, (1, 2 * HEAD), 1)
    low = (lane < HEAD).astype(F32).astype(BF)
    return low, (1.0 - low.astype(F32)).astype(BF)


def attend_kernel(
    where_ref, x_ref, w_ref, proj_ref, probs_ref, attn_ref, hat_ref, rstd_ref, norm_ref, vec_ref, bias_ref
):
    @pl.when(pl.program_id(0) == 0)
    def prepare():
        vec_ref[...] = jnp.transpose(w_ref[:, AT_VEC : AT_VEC + 128].astype(F32))
        span = where_ref[3]
        row = lax.broadcasted_iota(jnp.int32, (2 * BLOCK, BLOCK), 0) % BLOCK
        col = lax.broadcasted_iota(jnp.int32, (2 * BLOCK, BLOCK), 1)
        bias_ref[...] = jnp.where((row ^ col) < span, 0.0, -1e30)

    x = x_ref[...]
    for j in range(3):
        part = dot(x, w_ref[:, j * D : (j + 1) * D])
        if j != 1:
            part = part + vec_ref[j // 2 : j // 2 + 1, :]
        proj_ref[:, j * D : (j + 1) * D] = part.astype(BF)
    low, high = lane_masks()
    bias = bias_ref[...]
    for blk in range(TILE // BLOCK):
        rows = slice(blk * BLOCK, (blk + 1) * BLOCK)
        for pair in range(PAIRS):
            lanes = slice(pair * 128, (pair + 1) * 128)
            q = proj_ref[rows, lanes]
            k = proj_ref[rows, D + pair * 128 : D + (pair + 1) * 128]
            v = proj_ref[rows, 2 * D + pair * 128 : 2 * D + (pair + 1) * 128]
            s = dot_t(jnp.concatenate([q * low, q * high], 0), k) * HEAD**-0.5 + bias
            e = jnp.exp(s - jnp.max(s, -1, keepdims=True))
            p = (e * (1.0 / jnp.sum(e, -1, keepdims=True))).astype(BF)
            probs_ref[blk, pair] = p
            wide = jnp.concatenate([p[:BLOCK], p[BLOCK:]], 1)
            attn_ref[rows, lanes] = dot(wide, jnp.concatenate([v * low, v * high], 0)).astype(BF)
    hidden = x.astype(F32) + (dot(attn_ref[...], w_ref[:, AT_OUT:AT_VEC]) + vec_ref[2:3, :])
    hat, rstd = normalize(hidden)
    hat_ref[...] = hat
    rstd_ref[...] = rstd
    norm_ref[...] = (hat * vec_ref[10:11, :] + vec_ref[3:4, :]).astype(BF)


def row_block(width, rows=TILE):
    return pl.BlockSpec((rows, width), lambda i: (i, 0))


def whole_block(shape):
    return pl.BlockSpec(shape, lambda i: (0,) * len(shape))


def attend(where, x, w_one):
    rows = x.shape[0]
    shape = jax.ShapeDtypeStruct
    per = TILE // BLOCK
    return pl.pallas_call(
        attend_kernel,
        grid=(rows // TILE,),
        out_shape=(
            shape((rows, 3 * D), BF),
            shape((rows // BLOCK, PAIRS, 2 * BLOCK, BLOCK), BF),
            shape((rows, D), BF),
            shape((rows, D), F32),
            shape((rows, 1), F32),
            shape((rows, D), BF),
            shape((128, D), F32),
        ),
        in_specs=[smem(), row_block(D), whole_block(w_one.shape)],
        out_specs=[
            row_block(3 * D),
            pl.BlockSpec((per, PAIRS, 2 * BLOCK, BLOCK), lambda i: (i, 0, 0, 0)),
            row_block(D),
            row_block(D),
            row_block(1),
            row_block(D),
            whole_block((128, D)),
        ],
        scratch_shapes=[pltpu.VMEM((2 * BLOCK, BLOCK), F32)],
        compiler_params=params(48),
        name="attend",
    )(where, x, w_one)


def gelu_pair(u):
    t = 1.0 / (1.0 + (0.3275911 * 2**-0.5) * jnp.abs(u))
    e = jnp.exp(-0.5 * u * u)
    poly = t * (
        0.5 * 0.254829592
        + t * (0.5 * -0.284496736 + t * (0.5 * 1.421413741 + t * (0.5 * -1.453152027 + t * (0.5 * 1.061405429))))
    )
    tail = poly * e
    phi = jnp.where(u < 0, tail, 1.0 - tail)
    return u * phi, phi + u * (e * 0.3989422804014327)


def up_kernel(norm_ref, w_ref, vec_ref, act_ref, slope_ref):
    i = pl.program_id(0)
    bias = vec_ref[pl.ds(4 + i, 1), :]
    for m in range(norm_ref.shape[0] // TILE):
        rows = slice(m * TILE, (m + 1) * TILE)
        act, slope = gelu_pair(dot(norm_ref[rows, :], w_ref[...]) + bias)
        act_ref[rows, :] = act.astype(BF)
        slope_ref[rows, :] = slope.astype(BF)


def up(norm, w_up, vec):
    rows = norm.shape[0]
    wide = jax.ShapeDtypeStruct((rows, FF), BF)
    col = pl.BlockSpec((rows, D), lambda i: (0, i))
    return pl.pallas_call(
        up_kernel,
        grid=(FF // D,),
        out_shape=(wide, wide),
        in_specs=[whole_block(norm.shape), pl.BlockSpec((D, D), lambda i: (0, i)), whole_block(vec.shape)],
        out_specs=[col, col],
        compiler_params=params(48),
        name="up",
    )(norm, w_up, vec)


def down_kernel(act_ref, w_ref, hat_ref, vec_ref, out_ref, hat2_ref, rstd2_ref, cls_ref):
    normed = hat_ref[...] * vec_ref[10:11, :] + vec_ref[3:4, :]
    second = normed + (dot(act_ref[...], w_ref[...]) + vec_ref[8:9, :])
    hat, rstd = normalize(second)
    hat2_ref[...] = hat
    rstd2_ref[...] = rstd
    out = hat * vec_ref[11:12, :] + vec_ref[9:10, :]
    out_ref[...] = out.astype(BF)
    for j in range(TILE // 32):
        cls_ref[j : j + 1, :] = out[32 * j : 32 * j + 1, :]


def down(act, w_down, hat, vec):
    rows = act.shape[0]
    shape = jax.ShapeDtypeStruct
    return pl.pallas_call(
        down_kernel,
        grid=(rows // TILE,),
        out_shape=(shape((rows, D), BF), shape((rows, D), F32), shape((rows, 1), F32), shape((rows // 32, D), F32)),
        in_specs=[row_block(FF), whole_block(w_down.shape), row_block(D), whole_block(vec.shape)],
        out_specs=[row_block(D), row_block(D), row_block(1), row_block(D, TILE // 32)],
        compiler_params=params(48),
        name="down",
    )(act, w_down, hat, vec)


def contrast_kernel(reps, depth, per, where_ref, q_ref, p_ref, loss_ref, grad_ref, acc_ref):
    i = pl.program_id(0)
    me, core, tower = where_ref[0], where_ref[1], where_ref[2]
    pieces = p_ref.shape[0]
    total_p = pieces * per * 2
    cls_q = q_ref[:, :32, :D].reshape(-1, D)
    marks = q_ref[:, :32, D:].reshape(-1, q_ref.shape[2] - D)
    cls_p = p_ref[:, 32:, :D].reshape(-1, D)
    cols = cls_p.shape[0]
    col = lax.broadcasted_iota(jnp.int32, (marks.shape[1], cols), 1)
    row = lax.broadcasted_iota(jnp.int32, (marks.shape[1], cols), 0)
    j, slot = col // 16, col % 16
    line = j % (depth // 2)
    f1 = (j // (depth // 2)) % 2
    f2 = (j // depth) % 2
    flip_core = j // (2 * depth)
    from_core = core ^ flip_core
    p1, p2 = 1 + from_core % 2, 2 - from_core % 2
    base = (me | 4) ^ (8 * line) ^ (f1 * p1) ^ (f2 * p2)
    owner = jnp.where(slot < per, base, base ^ 4)
    passage = (owner * reps + from_core) * per + slot % per
    good = slot < 2 * per
    pick = jnp.where((row == passage) & good, 1.0, 0.0).astype(BF)
    marked_cols = dot(marks, pick)
    valid = lax.broadcasted_iota(jnp.int32, (1, cols), 1) % 16 < 2 * per
    raw = jnp.where(valid, dot_t(cls_q, cls_p) * D**-0.5, -1e30)
    e = jnp.exp(raw - jnp.max(raw, -1, keepdims=True))
    total = jnp.sum(e, -1, keepdims=True)
    me_ = marked_cols * e
    marked = jnp.sum(me_, -1, keepdims=True)
    grad = (LOSS_WEIGHT * (e / total - me_ / marked)).astype(BF)
    part = t_dot(grad[:, :128], cls_q) * D**-0.5

    @pl.when(i == 0)
    def first():
        loss_ref[...] = (jnp.log(total) - jnp.log(marked))[:32]
        acc_ref[...] = jnp.zeros_like(acc_ref)
        grad_ref[...] = dot(grad[:32], cls_p) * D**-0.5

    acc_ref[...] += part

    @pl.when((i == pl.num_programs(0) - 1) & (tower == 1))
    def last():
        grad_ref[...] = jnp.zeros_like(grad_ref)
        for s in range(2 * per):
            at = s * (32 // (2 * per))
            grad_ref[at : at + 1, :] = acc_ref[s : s + 1, :]


def contrast(plan, where, cls, positives):
    tower = where[2]
    queries, passages = positives.shape
    per = queries // 4
    msg = jnp.concatenate(
        [cls.astype(BF), jnp.pad(positives.astype(BF), ((0, 32 - queries), (0, 0)))], 1
    )
    back = send(msg, plan.along(1))
    q = jnp.where(tower == 0, msg[:, :D], back[:, :D])
    p = jnp.where(tower == 0, back[:, :D], msg[:, :D])[:: 32 // (2 * per)]
    m_own, m_far = msg[:queries, D:], back[:queries, D:]
    marks = jnp.concatenate([jnp.where(tower == 0, m_own, m_far), jnp.where(tower == 0, m_far, m_own)], 0)
    top = jnp.concatenate([q, marks], 1)
    low = jnp.pad(p, ((0, 16 - 2 * per), (0, passages)))
    buf = jnp.concatenate([top, low], 0)[None]
    buf = jnp.concatenate([buf] + [send(buf, plan.along(k)) for k in range(2, plan.depth, 2)], 0)
    buf = jnp.concatenate([buf, send(buf, plan.first())], 0)
    buf = jnp.concatenate([buf, send(buf, plan.second())], 0)
    buf = jnp.concatenate([buf] + [send(buf, plan.sibling(s)) for s in range(1, plan.reps)], 0)
    pieces = buf.shape[0]
    group = min(16, pieces)
    width = buf.shape[2]
    loss, grad = pl.pallas_call(
        partial(contrast_kernel, plan.reps, plan.depth, per),
        grid=(pieces // group,),
        out_shape=(jax.ShapeDtypeStruct((32, 1), F32), jax.ShapeDtypeStruct((32, D), F32)),
        in_specs=[
            smem(),
            pl.BlockSpec((group, 48, width), lambda i: (i, 0, 0)),
            whole_block(buf.shape),
        ],
        out_specs=[whole_block((32, 1)), whole_block((32, D))],
        scratch_shapes=[pltpu.VMEM((128, D), F32)],
        compiler_params=params(56),
        name="contrast",
    )(where, buf, buf)
    loss = lax.dynamic_slice(loss, (tower * queries, 0), (queries, 1))[:, 0]
    return loss, grad


def norm_back(grad, hat, rstd, gain):
    scaled = grad * gain
    a = jnp.mean(scaled, -1, keepdims=True)
    b = jnp.mean(scaled * hat, -1, keepdims=True)
    return rstd * (scaled - a - hat * b)


def col_sum(v):
    return jnp.sum(v, 0, keepdims=True)


def top_kernel(cot_ref, cls_ref, hat_ref, rstd_ref, vec_ref, second_ref, gs_ref, sums_ref):
    @pl.when(pl.program_id(0) == 0)
    def clear():
        sums_ref[...] = jnp.zeros_like(sums_ref)

    groups = TILE // 32
    at_first = lax.broadcasted_iota(jnp.int32, (groups, 32, D), 1) == 0
    extra = jnp.where(at_first, cls_ref[...].reshape(groups, 1, D), 0.0)
    dout = cot_ref[...].astype(F32) + extra.reshape(TILE, D)
    hat = hat_ref[...]
    grad = norm_back(dout, hat, rstd_ref[...], vec_ref[11:12, :])
    second_ref[...] = grad
    gs = grad.astype(BF)
    gs_ref[...] = gs
    sums_ref[0:1, :] += col_sum(gs.astype(F32))
    sums_ref[1:2, :] += col_sum(dout)
    sums_ref[2:3, :] += col_sum(dout * hat)


def top(cot, cls_grad, hat2, rstd2, vec):
    rows = cot.shape[0]
    shape = jax.ShapeDtypeStruct
    return pl.pallas_call(
        top_kernel,
        grid=(rows // TILE,),
        out_shape=(shape((rows, D), F32), shape((rows, D), BF), shape((8, D), F32)),
        in_specs=[row_block(D), row_block(D, TILE // 32), row_block(D), row_block(1), whole_block(vec.shape)],
        out_specs=[row_block(D), row_block(D), whole_block((8, D))],
        compiler_params=params(48),
        name="top",
    )(cot, cls_grad, hat2, rstd2, vec)


def gelu_back_kernel(gs_ref, w_ref, slope_ref, gu_ref, sums_ref):
    total = jnp.zeros((1, D), F32)
    for m in range(gs_ref.shape[0] // TILE):
        rows = slice(m * TILE, (m + 1) * TILE)
        gu = (dot_t(gs_ref[rows, :], w_ref[...]) * slope_ref[rows, :].astype(F32)).astype(BF)
        gu_ref[rows, :] = gu
        total = total + col_sum(gu.astype(F32))
    sums_ref[pl.ds(pl.program_id(0), 1), :] = total


def gelu_back(gs, w_down, slope):
    rows = gs.shape[0]
    shape = jax.ShapeDtypeStruct
    col = pl.BlockSpec((rows, D), lambda i: (0, i))
    return pl.pallas_call(
        gelu_back_kernel,
        grid=(FF // D,),
        out_shape=(shape((rows, FF), BF), shape((8, D), F32)),
        in_specs=[whole_block(gs.shape), row_block(D, D), col],
        out_specs=[col, whole_block((8, D))],
        compiler_params=params(48),
        name="gelu_back",
    )(gs, w_down, slope)


def attend_back_kernel(
    gu_ref, w_up_ref, second_ref, hat_ref, rstd_ref, w_ref, vec_ref, proj_ref, probs_ref,
    go_ref, gp_ref, own_ref, far_ref, sums_ref, ga_ref,
):
    i = pl.program_id(0)

    @pl.when(i == 0)
    def clear():
        sums_ref[...] = jnp.zeros_like(sums_ref)

    grad = dot_t(gu_ref[...], w_up_ref[...]) + second_ref[...]
    hat = hat_ref[...]
    hidden = norm_back(grad, hat, rstd_ref[...], vec_ref[10:11, :])
    go = hidden.astype(BF)
    go_ref[...] = go
    sums_ref[2:3, :] += col_sum(go.astype(F32))
    sums_ref[3:4, :] += col_sum(grad)
    sums_ref[4:5, :] += col_sum(grad * hat)
    ga_ref[...] = dot_t(go, w_ref[:, AT_OUT:AT_VEC]).astype(BF)
    low, high = lane_masks()
    for blk in range(TILE // BLOCK):
        rows = slice(blk * BLOCK, (blk + 1) * BLOCK)
        for pair in range(PAIRS):
            lanes = slice(pair * 128, (pair + 1) * 128)
            lanes_k = slice(D + pair * 128, D + (pair + 1) * 128)
            lanes_v = slice(2 * D + pair * 128, 2 * D + (pair + 1) * 128)
            q, k, v = proj_ref[rows, lanes], proj_ref[rows, lanes_k], proj_ref[rows, lanes_v]
            a = ga_ref[rows, lanes]
            a2 = jnp.concatenate([a * low, a * high], 0)
            q2 = jnp.concatenate([q * low, q * high], 0)
            k2 = jnp.concatenate([k * low, k * high], 0)
            p = probs_ref[blk, pair]
            dp = dot_t(a2, v)
            pf = p.astype(F32)
            ds = (pf * (dp - jnp.sum(pf * dp, -1, keepdims=True)) * HEAD**-0.5).astype(BF)
            wide = jnp.concatenate([ds[:BLOCK], ds[BLOCK:]], 1)
            gp_ref[rows, lanes] = dot(wide, k2).astype(BF)
            gp_ref[rows, lanes_k] = t_dot(ds, q2).astype(BF)
            gp_ref[rows, lanes_v] = t_dot(p, a2).astype(BF)
    gp = gp_ref[...]
    sums_ref[0:1, :] += col_sum(gp[:, :D].astype(F32))
    sums_ref[1:2, :] += col_sum(gp[:, 2 * D :].astype(F32))
    gx = dot_t(gp, w_ref[:, :AT_OUT]) + hidden
    half = pl.num_programs(0) // 2

    @pl.when(i < half)
    def near():
        own_ref[...] = gx

    @pl.when(i >= half)
    def away():
        far_ref[...] = gx.astype(BF)


def attend_back(gu, w_up, second, hat, rstd, w_one, vec, proj, probs):
    rows = gu.shape[0]
    shape = jax.ShapeDtypeStruct
    per = TILE // BLOCK
    steps = rows // TILE
    half = steps // 2
    return pl.pallas_call(
        attend_back_kernel,
        grid=(steps,),
        out_shape=(
            shape((rows, D), BF),
            shape((rows, 3 * D), BF),
            shape((rows // 2, D), F32),
            shape((rows // 2, D), BF),
            shape((8, D), F32),
        ),
        in_specs=[
            row_block(FF),
            whole_block(w_up.shape),
            row_block(D),
            row_block(D),
            row_block(1),
            whole_block(w_one.shape),
            whole_block(vec.shape),
            row_block(3 * D),
            pl.BlockSpec((per, PAIRS, 2 * BLOCK, BLOCK), lambda i: (i, 0, 0, 0)),
        ],
        out_specs=[
            row_block(D),
            row_block(3 * D),
            pl.BlockSpec((TILE, D), lambda i: (jnp.minimum(i, half - 1), 0)),
            pl.BlockSpec((TILE, D), lambda i: (jnp.maximum(i - half, 0), 0)),
            whole_block((8, D)),
        ],
        scratch_shapes=[pltpu.VMEM((TILE, D), BF)],
        compiler_params=params(56),
        name="attend_back",
    )(gu, w_up, second, hat, rstd, w_one, vec, proj, probs)


def on_device(
    plan, query_tokens, passage_tokens, query_cot, passage_cot, positives, w_qkv, w_out, w_up, w_down, biases, gains
):
    me = lax.axis_index("dp")
    core = lax.axis_index("rep")
    tower = (me >> 2) & 1
    span = jnp.where(tower == 0, query_tokens.shape[1], passage_tokens.shape[1])
    where = jnp.stack([me, core, tower, span]).astype(jnp.int32)
    swap = plan.along(1)

    def exchange(a, b):
        a, b = a.reshape(-1, D), b.reshape(-1, D)
        return jnp.concatenate([jnp.where(tower == 0, a, b), send(jnp.where(tower == 0, b, a), swap)], 0)

    vecs = jnp.swapaxes(jnp.concatenate([biases, gains], 1), 1, 2)
    one = jnp.concatenate([w_qkv, w_out, jnp.pad(vecs, ((0, 0), (0, 0), (0, W_ONE - AT_VEC - vecs.shape[2])))], 2)
    x = exchange(query_tokens, passage_tokens)
    w_one = gather_chunk(plan, where, one)
    w_two = gather_chunk(plan, where, w_up)
    w_three = gather_chunk(plan, where, w_down)
    cot = exchange(query_cot, passage_cot)

    proj, probs, attn, hat1, rstd1, norm, vec = attend(where, x, w_one)
    act, slope = up(norm, w_two, vec)
    out, hat2, rstd2, cls = down(act, w_three, hat1, vec)
    half = out.shape[0] // 2
    out_back = send(out[half:], swap)
    query_out = jnp.where(tower == 0, out[:half], out_back).reshape(query_tokens.shape)
    passage_out = jnp.where(tower == 0, out_back, out[:half]).reshape(passage_tokens.shape)
    query_loss, cls_grad = contrast(plan, where, cls, positives)

    second, gs, sums_top = top(cot, cls_grad, hat2, rstd2, vec)
    g_three = t_dot(act, gs).astype(BF)
    grad_down = scatter_chunk(plan, where, g_three, w_down.shape[1])
    gu, sums_up = gelu_back(gs, w_three, slope)
    g_two = t_dot(norm, gu).astype(BF)
    grad_up = scatter_chunk(plan, where, g_two, w_up.shape[1])
    go, gp, gx_own, gx_far, sums = attend_back(gu, w_two, second, hat1, rstd1, w_one, vec, proj, probs)
    gx_back = send(gx_far, swap).astype(F32)
    query_grad = jnp.where(tower == 0, gx_own, gx_back).reshape(query_tokens.shape)
    passage_grad = jnp.where(tower == 0, gx_back, gx_own).reshape(passage_tokens.shape)
    lines = jnp.concatenate(
        [sums[0:4], sums_up[0:4], sums_top[0:2], sums[4:5], sums_top[2:3], jnp.zeros((W_ONE - AT_VEC - 12, D), F32)], 0
    )
    g_one = jnp.concatenate([t_dot(x, gp).astype(BF), t_dot(attn, go).astype(BF), lines.T.astype(BF)], 1)
    grad_one = scatter_chunk(plan, where, g_one, w_qkv.shape[1])
    grad_vecs = jnp.swapaxes(grad_one[:, :, AT_VEC : AT_VEC + 12], 1, 2)
    return (
        query_out,
        passage_out,
        query_grad,
        passage_grad,
        query_loss,
        grad_one[:, :, :AT_OUT],
        grad_one[:, :, AT_OUT:AT_VEC],
        grad_up,
        grad_down,
        grad_vecs[:, :10],
        grad_vecs[:, 10:],
    )


def solution(mesh):
    plan = Plan(mesh.shape["dp"], mesh.shape["rep"])
    rows = P(("dp", "rep"), None, None)
    shards = P(None, "dp", None)
    lanes = P(None, None, "dp")
    return jax.shard_map(
        partial(on_device, plan),
        mesh=mesh,
        in_specs=(rows,) * 4 + (P(("dp", "rep"), None),) + (shards,) * 4 + (lanes,) * 2,
        out_specs=(rows,) * 4 + (P(("dp", "rep")),) + (shards,) * 4 + (lanes,) * 2,
        check_vma=False,
    )
```

```python
from functools import partial

import jax
import jax.numpy as jnp
from jax import lax
from jax.experimental import pallas as pl
from jax.experimental.pallas import tpu as pltpu
from jax.sharding import PartitionSpec as P

AXES = ("dp", "rep")
BF = jnp.bfloat16
F32 = jnp.float32
D = 768
FF = 3072
HEADS = 12
HEAD = 64
PAIRS = HEADS // 2
BLOCK = 128
TILE = 256
EPS = 1e-05
LOSS_WEIGHT = 32.0
MIB = 2**20
AT_OUT = 3 * D
AT_VEC = 4 * D
W_ONE = 4 * D + 256


def smem():
    return pl.BlockSpec(memory_space=pltpu.SMEM)


def vmem():
    return pl.BlockSpec(memory_space=pltpu.VMEM)


def cost(us):
    return pl.CostEstimate(flops=int(us * 1.0e9), transcendentals=0, bytes_accessed=int(us * 3.0e6))


def params(mib):
    return pltpu.CompilerParams(vmem_limit_bytes=mib * MIB)


def still(shape, at=None):
    index = at if at is not None else (0,) * len(shape)
    return pl.BlockSpec(shape, lambda i, *_: index, pipeline_mode=pl.Buffered(1))


def rows_at(width, rows=TILE):
    return pl.BlockSpec((rows, width), lambda i, *_: (i, 0))


def shape(dims, dtype):
    return jax.ShapeDtypeStruct(dims, dtype)


def far(dims, dtype):
    return pltpu.HBM(dims, dtype)


def stay(v):
    return pltpu.with_memory_space_constraint(v, pltpu.HBM)


def after(v, *others):
    return lax.optimization_barrier((v,) + others)[0]


class Order:
    def __init__(self, where):
        self.where = where

    def done(self, out):
        self.where = after(self.where, out)
        return out


def halves(ref_pairs, core, width, source):
    for q, ref in enumerate(ref_pairs):
        at = pl.multiple_of((core ^ q) * width, 128)
        ref[...] = source[:, pl.ds(at, width)]


def send(v, pairs):
    return lax.ppermute(v, AXES, pairs)


class Plan:
    def __init__(self, n, reps):
        self.n, self.reps, self.depth = n, reps, n // 4

    def pairs(self, move):
        return [
            (d * self.reps + r, (d ^ move(r)[0]) * self.reps + (r ^ move(r)[1]))
            for d in range(self.n)
            for r in range(self.reps)
        ]

    def along(self, k):
        return self.pairs(lambda r: (4 * k, 0))

    def first(self):
        return self.pairs(lambda r: (1 + r % 2, 0))

    def second(self):
        return self.pairs(lambda r: (2 - r % 2, 0))

    def sibling(self, q):
        return self.pairs(lambda r: (0, q))


def assemble_kernel(depth, reps, width, where_ref, *refs):
    bufs, out = refs[: 2 * reps], refs[2 * reps]
    me, core = where_ref[0], where_ref[1]
    for q in range(reps):
        owner = core ^ q
        p1 = 1 + owner % 2
        p2 = 2 - owner % 2
        lanes = pl.ds(pl.multiple_of(owner * width, 128), width)
        for b in range(2):
            for f in range(2):
                for k in range(depth):
                    dst = (me ^ (b * p2) ^ (f * p1)) ^ (4 * k)
                    out[pl.ds(dst, 1), :, lanes] = bufs[q * 2 + b][pl.ds(f * depth + k, 1)]


def shards_of(plan, where, shard):
    core, tower = where[1], where[2]
    rows, whole = shard.shape[1:]
    width = whole // plan.reps
    mine = lax.dynamic_slice(shard, (tower, 0, core * width), (1, rows, width))
    other = lax.dynamic_slice(shard, (1 - tower, 0, core * width), (1, rows, width))
    return mine, other


def gather_line(plan, mine, other):
    got = [send(other if k % 2 else mine, plan.along(k)) for k in range(1, plan.depth)]
    return jnp.concatenate([mine] + got, 0)


def gather_steps(plan, both, *others):
    z = both
    k = 2
    while k < plan.depth:
        if others:
            z, others = after(z, *others), ()
        z = jnp.concatenate([z, send(z, plan.along(k))], 0)
        k *= 2
    return z


def gather_plane(plan, z, *others):
    near = jnp.concatenate([z, send(z, plan.first())], 0)
    if others:
        near = after(near, *others)
    return near, send(near, plan.second())


def gather_cores(plan, order, bufs):
    rows, width = bufs[0].shape[1:]
    bufs = list(bufs)
    for q in range(1, plan.reps):
        bufs += [send(b, plan.sibling(q)) for b in bufs[:2]]
    full = pl.pallas_call(
        partial(assemble_kernel, plan.depth, plan.reps, width),
        out_shape=jax.ShapeDtypeStruct((plan.n, rows, width * plan.reps), BF),
        in_specs=[smem()] + [vmem()] * len(bufs),
        out_specs=vmem(),
        compiler_params=params(24),
        name="assemble",
        cost_estimate=cost(2),
    )(order.where, *bufs)
    order.done(full)
    return full.reshape(plan.n * rows, width * plan.reps)


def add_kernel(depth, where_ref, a_hbm, b_ref, s_ref, k_ref, a_ref, sem):
    me, core = where_ref[0], where_ref[1]
    p1 = 1 + core % 2
    p2 = 2 - core % 2
    copies = []
    for j in range(4 * depth):
        at = me ^ ((1 - j // (2 * depth)) * p1) ^ ((1 - j // depth % 2) * p2) ^ (4 * (j % depth))
        copy = pltpu.make_async_copy(a_hbm.at[at], a_ref.at[j], sem.at[j])
        copy.start()
        copies.append((at, copy))
    for j, (at, copy) in enumerate(copies):
        copy.wait()
        o_ref, to = (s_ref, j) if j < 2 * depth else (k_ref, j - 2 * depth)
        o_ref[to] = (a_ref[j].astype(F32) + b_ref[at].astype(F32)).astype(BF)


def two_kernel(where_ref, k_ref, r_ref, s_ref, o_ref):
    q = s_ref.shape[0]
    for j in range(2 * q):
        total = (k_ref[j].astype(F32) + r_ref[j].astype(F32)).astype(BF)
        if j < q:
            s_ref[j] = total
        else:
            o_ref[j - q] = total


def line_kernel(where_ref, k_ref, r_ref, s_ref, o_ref):
    half = o_ref.shape[0]
    for j in range(2 * half):
        total = (k_ref[j].astype(F32) + r_ref[j].astype(F32)).astype(BF)
        if j < half:
            o_ref[j] = total
        else:
            s_ref[j - half] = total


def last_kernel(where_ref, own_ref, got_ref, out):
    tower = where_ref[2]
    out[pl.ds(tower, 1)] = own_ref[...]
    out[pl.ds(1 - tower, 1)] = got_ref[...]


def plus(a, b):
    return (a.astype(F32) + b.astype(F32)).astype(BF)


def in_vmem(kernel, name, us, outs, *args, mib=24):
    return pl.pallas_call(
        kernel,
        out_shape=tuple(shape(*o) for o in outs),
        in_specs=[smem() if a.ndim == 1 else vmem() for a in args],
        out_specs=tuple(vmem() for _ in outs),
        compiler_params=params(mib),
        name=name,
        cost_estimate=cost(us),
    )(*args)


class Scatter:
    def __init__(self, plan, order, parts, rows):
        self.plan, self.order, self.rows = plan, order, rows
        self.width = parts[0].shape[1]
        parts = [p.reshape(plan.n, rows, self.width) for p in parts]
        self.own = parts[0]
        got = [send(parts[q], plan.sibling(q)) for q in range(1, plan.reps)]
        self.rest = got[0]
        for o in got[1:]:
            self.rest = plus(self.rest, o)

    def run(self, kernel, name, us, outs, *args):
        return self.order.done(in_vmem(kernel, name, us, outs, self.order.where, *args))

    def one(self):
        plan = self.plan
        n = plan.n
        whole = (n, self.rows, self.width)
        half = shape((n // 2, self.rows, self.width), BF)
        hs, self.hk = self.order.done(
            pl.pallas_call(
                partial(add_kernel, plan.depth),
                out_shape=(half, half),
                in_specs=[smem(), pl.BlockSpec(memory_space=pl.ANY), vmem()],
                out_specs=(vmem(), vmem()),
                scratch_shapes=[pltpu.VMEM(whole, BF), pltpu.SemaphoreType.DMA((n,))],
                compiler_params=params(24),
                name="pick_add",
                cost_estimate=cost(3),
            )(self.order.where, stay(self.own), self.rest)
        )
        self.r1 = send(hs, plan.first())

    def two(self):
        quarter = ((self.plan.n // 4, self.rows, self.width), BF)
        ks, self.kk = self.run(two_kernel, "add_two", 1, (quarter, quarter), self.hk, self.r1)
        self.r2 = send(ks, self.plan.second())

    def line(self):
        n = self.kk.shape[0] // 2
        half = ((n, self.rows, self.width), BF)
        out, self.kk = self.run(line_kernel, "add_line", 1, (half, half), self.kk, self.r2)
        self.r2 = send(out, self.plan.along(n))
        return out

    def three(self):
        self.line()

    def four(self):
        while self.kk.shape[0] > 1:
            self.out = self.line()

    def last(self):
        plan = self.plan
        outs = (((2, self.rows, self.width), BF),)
        (pair,) = self.run(last_kernel, "add_last", 1, outs, self.kk, self.r2)
        self.ends = [pair] + [send(pair, plan.sibling(q)) for q in range(1, plan.reps)]


def finish_kernel(reps, spans, where_ref, *refs):
    chunks = len(spans)
    ins, outs = refs[: chunks * reps], refs[chunks * reps :]
    core = where_ref[1]
    for c in range(chunks):
        parts = ins[c * reps : (c + 1) * reps]
        width = parts[0].shape[2]
        for q in range(reps):
            for mine in range(reps):

                @pl.when((core ^ q) == mine)
                def copy(q=q, mine=mine):
                    for at, size, out, to in spans[c]:
                        low, high = max(at, mine * width), min(at + size, (mine + 1) * width)
                        if low < high:
                            outs[out][:, :, to + low - at : to + high - at] = parts[q][
                                :, :, low - mine * width : high - mine * width
                            ].astype(F32)


def finish(plan, order, chunks, spans, widths):
    rows = chunks[0].rows
    outs = tuple(((2, rows, w), F32) for w in widths)
    args = [p for c in chunks for p in c.ends]
    return order.done(in_vmem(partial(finish_kernel, plan.reps, spans), "finish", 2, outs, order.where, *args))


def dot(a, b):
    return jnp.dot(a, b, preferred_element_type=F32)


def dot_t(a, b):
    return lax.dot_general(a, b, (((1,), (1,)), ((), ())), preferred_element_type=F32)


def t_dot(a, b):
    return lax.dot_general(a, b, (((0,), (0,)), ((), ())), preferred_element_type=F32)


def normalize(h):
    center = h - jnp.mean(h, -1, keepdims=True)
    rstd = lax.rsqrt(jnp.mean(center * center, -1, keepdims=True) + EPS)
    return center * rstd, rstd


def lane_masks():
    lane = lax.broadcasted_iota(jnp.int32, (1, 2 * HEAD), 1)
    low = (lane < HEAD).astype(F32).astype(BF)
    return low, (1.0 - low.astype(F32)).astype(BF)


def attend_kernel(part, where_ref, x_ref, w_ref, *rest):
    proj_ref, probs_ref, attn_ref, hat_ref, rstd_ref, norm_ref, vec_ref, bias_ref = rest[-8:]

    @pl.when(pl.program_id(0) == 0)
    def prepare():
        vec_ref[...] = jnp.transpose(w_ref[:, AT_VEC : AT_VEC + 128].astype(F32))
        span = where_ref[3]
        row = lax.broadcasted_iota(jnp.int32, (2 * BLOCK, BLOCK), 0) % BLOCK
        col = lax.broadcasted_iota(jnp.int32, (2 * BLOCK, BLOCK), 1)
        bias_ref[...] = jnp.where((row ^ col) < span, 0.0, -1e30)

    x = x_ref[...]
    for j in range(3):
        part = dot(x, w_ref[:, j * D : (j + 1) * D])
        if j != 1:
            part = part + vec_ref[j // 2 : j // 2 + 1, :]
        proj_ref[:, j * D : (j + 1) * D] = part.astype(BF)
    low, high = lane_masks()
    bias = bias_ref[...]
    for blk in range(TILE // BLOCK):
        rows = slice(blk * BLOCK, (blk + 1) * BLOCK)
        for pair in range(PAIRS):
            lanes = slice(pair * 128, (pair + 1) * 128)
            q = proj_ref[rows, lanes]
            k = proj_ref[rows, D + pair * 128 : D + (pair + 1) * 128]
            v = proj_ref[rows, 2 * D + pair * 128 : 2 * D + (pair + 1) * 128]
            s = dot_t(jnp.concatenate([q * low, q * high], 0), k) * HEAD**-0.5 + bias
            e = jnp.exp(s - jnp.max(s, -1, keepdims=True))
            p = (e * (1.0 / jnp.sum(e, -1, keepdims=True))).astype(BF)
            probs_ref[blk, pair] = p
            wide = jnp.concatenate([p[:BLOCK], p[BLOCK:]], 1)
            attn_ref[rows, lanes] = dot(wide, jnp.concatenate([v * low, v * high], 0)).astype(BF)
    hidden = x.astype(F32) + (dot(attn_ref[...], w_ref[:, AT_OUT:AT_VEC]) + vec_ref[2:3, :])
    hat, rstd = normalize(hidden)
    hat_ref[...] = hat
    rstd_ref[...] = rstd
    norm_ref[...] = (hat * vec_ref[10:11, :] + vec_ref[3:4, :]).astype(BF)


def attend(order, x, w_one, part, before=()):
    rows = x.shape[0]
    per = TILE // BLOCK
    steps = rows // TILE // 2
    first = part * steps

    def here(width):
        return pl.BlockSpec((TILE, width), lambda i: (i + first, 0))

    return pl.pallas_call(
        partial(attend_kernel, part),
        grid=(steps,),
        out_shape=(
            far((rows, 3 * D), BF),
            far((rows // BLOCK, PAIRS, 2 * BLOCK, BLOCK), BF),
            far((rows, D), BF),
            far((rows, D), F32),
            far((rows, 1), F32),
            far((rows, D), BF),
            shape((128, D), F32),
        ),
        in_specs=[smem(), here(D), still(w_one.shape)] + [pl.BlockSpec(memory_space=pl.ANY)] * len(before),
        out_specs=[
            here(3 * D),
            pl.BlockSpec((per, PAIRS, 2 * BLOCK, BLOCK), lambda i: (i + first, 0, 0, 0)),
            here(D),
            here(D),
            here(1),
            here(D),
            still((128, D)),
        ],
        scratch_shapes=[pltpu.VMEM((2 * BLOCK, BLOCK), F32)],
        input_output_aliases={3 + j: j for j in range(len(before))},
        compiler_params=params(24),
        name="attend",
        cost_estimate=cost(7),
    )(order.where, x, w_one, *[stay(b) for b in before])


def gelu_pair(u):
    t = 1.0 / (1.0 + (0.3275911 * 2**-0.5) * jnp.abs(u))
    e = jnp.exp(-0.5 * u * u)
    poly = t * (
        0.5 * 0.254829592
        + t * (0.5 * -0.284496736 + t * (0.5 * 1.421413741 + t * (0.5 * -1.453152027 + t * (0.5 * 1.061405429))))
    )
    tail = poly * e
    phi = jnp.where(u < 0, tail, 1.0 - tail)
    return u * phi, phi + u * (e * 0.3989422804014327)


def up_kernel(first, where_ref, norm_ref, w_ref, vec_ref, *rest):
    act_ref, slope_ref = rest[-2:]
    bias = vec_ref[pl.ds(4 + first + pl.program_id(0), 1), :]
    for m in range(0, norm_ref.shape[0], TILE):
        rows = slice(m, m + TILE)
        act, slope = gelu_pair(dot(norm_ref[rows, :], w_ref[...]) + bias)
        act_ref[rows, :] = act.astype(BF)
        slope_ref[rows, :] = slope.astype(BF)


def up(order, norm, w_up, vec, part, before=()):
    rows = norm.shape[0]
    steps = FF // D // 2
    first = part * steps
    col = pl.BlockSpec((rows, D), lambda i: (0, i + first))
    return pl.pallas_call(
        partial(up_kernel, first),
        grid=(steps,),
        out_shape=(far((rows, FF), BF), far((rows, FF), BF)),
        in_specs=[
            smem(),
            still(norm.shape),
            pl.BlockSpec((D, D), lambda i: (0, i + first)),
            still(vec.shape),
        ]
        + [pl.BlockSpec(memory_space=pl.ANY)] * len(before),
        out_specs=[col, col],
        input_output_aliases={4 + j: j for j in range(len(before))},
        compiler_params=params(24),
        name="up",
        cost_estimate=cost(8),
    )(order.where, norm, w_up, vec, *[stay(b) for b in before])


def down_kernel(where_ref, act_ref, w_ref, hat_ref, vec_ref, out_ref, hat2_ref, rstd2_ref, cls_ref):
    normed = hat_ref[...] * vec_ref[10:11, :] + vec_ref[3:4, :]
    second = normed + (dot(act_ref[...], w_ref[...]) + vec_ref[8:9, :])
    hat, rstd = normalize(second)
    hat2_ref[...] = hat
    rstd2_ref[...] = rstd
    out = hat * vec_ref[11:12, :] + vec_ref[9:10, :]
    out_ref[...] = out.astype(BF)
    for j in range(TILE // 32):
        cls_ref[j : j + 1, :] = out[32 * j : 32 * j + 1, :]


def down(order, act, w_down, hat, vec):
    rows = act.shape[0]
    return pl.pallas_call(
        down_kernel,
        grid=(rows // TILE,),
        out_shape=(far((rows, D), BF), far((rows, D), F32), far((rows, 1), F32), shape((rows // 32, D), F32)),
        in_specs=[smem(), rows_at(FF), still(w_down.shape), rows_at(D), still(vec.shape)],
        out_specs=[rows_at(D), rows_at(D), rows_at(1), rows_at(D, TILE // 32)],
        compiler_params=params(24),
        name="down",
        cost_estimate=cost(8),
    )(order.where, stay(act), w_down, hat, vec)


def contrast_kernel(reps, depth, per, where_ref, q_ref, p_ref, loss_ref, grad_ref, acc_ref):
    i = pl.program_id(0)
    me, core, tower = where_ref[0], where_ref[1], where_ref[2]
    pieces = p_ref.shape[0]
    total_p = pieces * per * 2
    cls_q = q_ref[:, :32, :D].reshape(-1, D)
    marks = q_ref[:, :32, D:].reshape(-1, q_ref.shape[2] - D)
    cls_p = p_ref[:, 32:, :D].reshape(-1, D)
    cols = cls_p.shape[0]
    col = lax.broadcasted_iota(jnp.int32, (marks.shape[1], cols), 1)
    row = lax.broadcasted_iota(jnp.int32, (marks.shape[1], cols), 0)
    j, slot = col // 16, col % 16
    line = j % (depth // 2)
    flip = (j // (depth // 2)) % 4
    from_core = core ^ (j // (2 * depth))
    base = (me | 4) ^ (8 * line) ^ flip
    owner = jnp.where(slot < per, base, base ^ 4)
    passage = (owner * reps + from_core) * per + slot % per
    good = slot < 2 * per
    pick = jnp.where((row == passage) & good, 1.0, 0.0).astype(BF)
    marked_cols = dot(marks, pick)
    valid = lax.broadcasted_iota(jnp.int32, (1, cols), 1) % 16 < 2 * per
    raw = jnp.where(valid, dot_t(cls_q, cls_p) * D**-0.5, -1e30)
    e = jnp.exp(raw - jnp.max(raw, -1, keepdims=True))
    total = jnp.sum(e, -1, keepdims=True)
    me_ = marked_cols * e
    marked = jnp.sum(me_, -1, keepdims=True)
    grad = (LOSS_WEIGHT * (e / total - me_ / marked)).astype(BF)
    part = t_dot(grad[:, :128], cls_q) * D**-0.5

    @pl.when(i == 0)
    def first():
        loss_ref[...] = (jnp.log(total) - jnp.log(marked))[:32]
        acc_ref[...] = jnp.zeros_like(acc_ref)
        grad_ref[...] = dot(grad[:32], cls_p) * D**-0.5

    acc_ref[...] += part

    @pl.when((i == pl.num_programs(0) - 1) & (tower == 1))
    def last():
        grad_ref[...] = jnp.zeros_like(grad_ref)
        for s in range(2 * per):
            at = s * (32 // (2 * per))
            grad_ref[at : at + 1, :] = acc_ref[s : s + 1, :]


def contrast(plan, order, cls, positives):
    where = order.where
    tower = where[2]
    queries, passages = positives.shape
    per = queries // 4
    marks = jnp.pad(positives.astype(BF), ((0, 32 - queries), (0, 0)))
    msg = jnp.concatenate([cls.astype(BF), marks], 1)
    got = [msg] + [send(msg, plan.along(k)) for k in range(1, plan.depth)]
    same, other = jnp.stack(got[0::2]), jnp.stack(got[1::2])
    zero = jnp.where(tower == 0, same, other)
    one = jnp.where(tower == 0, other, same)
    marks = jnp.concatenate([zero[:, :queries, D:], one[:, :queries, D:]], 1)
    top = jnp.concatenate([zero[:, :, :D], marks], 2)
    low = jnp.pad(one[:, :: 32 // (2 * per)], ((0, 0), (0, 16 - 2 * per), (0, 0)))
    buf = jnp.concatenate([top, low], 1)
    buf = jnp.concatenate([buf] + [send(buf, plan.pairs(lambda r, m=m: (m, 0))) for m in range(1, 4)], 0)
    buf = jnp.concatenate([buf] + [send(buf, plan.sibling(s)) for s in range(1, plan.reps)], 0)
    pieces = buf.shape[0]
    group = min(16, pieces)
    width = buf.shape[2]
    loss, grad = pl.pallas_call(
        partial(contrast_kernel, plan.reps, plan.depth, per),
        grid=(pieces // group,),
        out_shape=(jax.ShapeDtypeStruct((32, 1), F32), jax.ShapeDtypeStruct((32, D), F32)),
        in_specs=[
            smem(),
            pl.BlockSpec((group, 48, width), lambda i: (i, 0, 0)),
            still(buf.shape),
        ],
        out_specs=[still((32, 1)), still((32, D))],
        scratch_shapes=[pltpu.VMEM((128, D), F32)],
        compiler_params=params(32),
        name="contrast",
        cost_estimate=cost(2),
    )(where, buf, buf)
    loss = lax.dynamic_slice(loss, (tower * queries, 0), (queries, 1))[:, 0]
    return loss, grad


def norm_back(grad, hat, rstd, gain):
    scaled = grad * gain
    a = jnp.mean(scaled, -1, keepdims=True)
    b = jnp.mean(scaled * hat, -1, keepdims=True)
    return rstd * (scaled - a - hat * b)


def col_sum(v):
    return jnp.sum(v, 0, keepdims=True)


def top_kernel(
    reps, where_ref, cot_ref, cls_ref, hat_ref, rstd_ref, vec_ref, act_ref, second_ref, gs_ref, sums_ref, *rest
):
    parts, full_ref = rest[:-1], rest[-1]

    @pl.when(pl.program_id(0) == 0)
    def norm():
        groups = TILE // 32
        at_first = lax.broadcasted_iota(jnp.int32, (groups, 32, D), 1) == 0
        sums_ref[...] = jnp.zeros_like(sums_ref)
        for m in range(0, cot_ref.shape[0], TILE):
            rows = slice(m, m + TILE)
            cls = cls_ref[m // 32 : (m + TILE) // 32, :].reshape(groups, 1, D)
            dout = cot_ref[rows, :].astype(F32) + jnp.where(at_first, cls, 0.0).reshape(TILE, D)
            hat = hat_ref[rows, :]
            grad = norm_back(dout, hat, rstd_ref[rows, :], vec_ref[11:12, :])
            second_ref[rows, :] = grad
            gs = grad.astype(BF)
            gs_ref[rows, :] = gs
            sums_ref[0:1, :] += col_sum(gs.astype(F32))
            sums_ref[1:2, :] += col_sum(dout)
            sums_ref[2:3, :] += col_sum(dout * hat)

    full_ref[...] = t_dot(act_ref[...], gs_ref[...]).astype(BF)
    halves(parts, where_ref[1], D // reps, full_ref)


def top(plan, order, cot, cls_grad, hat2, rstd2, vec, act):
    rows = cot.shape[0]
    part = D // plan.reps
    second, gs, sums, *parts = pl.pallas_call(
        partial(top_kernel, plan.reps),
        grid=(FF // D,),
        out_shape=(far((rows, D), F32), shape((rows, D), BF), shape((8, D), F32))
        + (far((FF, part), BF),) * plan.reps,
        in_specs=[
            smem(),
            still(cot.shape),
            still(cls_grad.shape),
            still(hat2.shape),
            still(rstd2.shape),
            still(vec.shape),
            pl.BlockSpec((rows, D), lambda i: (0, i)),
        ],
        out_specs=[still((rows, D)), still((rows, D)), still((8, D))] + [rows_at(part, D)] * plan.reps,
        scratch_shapes=[pltpu.VMEM((D, D), BF)],
        compiler_params=params(28),
        name="top",
        cost_estimate=cost(11),
    )(order.where, cot, cls_grad, hat2, rstd2, vec, stay(act))
    return second, gs, sums, parts


def gelu_back_kernel(reps, column, where_ref, gs_ref, w_ref, slope_ref, norm_ref, up_ref, acc_ref, sums_ref, *rest):
    parts, gu_ref = rest[:-1], rest[-1]
    i = pl.program_id(0)
    total = jnp.zeros((1, D), F32)
    for m in range(0, gs_ref.shape[0], TILE):
        rows = slice(m, m + TILE)
        gu = (dot_t(gs_ref[rows, :], w_ref[...]) * slope_ref[rows, :].astype(F32)).astype(BF)
        gu_ref[rows, :] = gu
        total = total + col_sum(gu.astype(F32))
    sums_ref[pl.ds(column(i, where_ref), 1), :] = total
    grad = t_dot(norm_ref[...], gu_ref[...]).astype(BF)
    per = (FF // D) // reps
    for q in range(reps):

        @pl.when(i // per == reps - 1 - q)
        def put(q=q):
            parts[q][...] = grad

    @pl.when(i == 0)
    def start():
        acc_ref[...] = dot_t(gu_ref[...], up_ref[...])

    @pl.when(i > 0)
    def add():
        acc_ref[...] += dot_t(gu_ref[...], up_ref[...])


def gelu_back(plan, order, gs, w_down, slope, norm, w_up):
    rows = gs.shape[0]
    reps = plan.reps
    per = (FF // D) // reps

    def column(i, table):
        return (table[1] ^ (reps - 1 - i // per)) * per + i % per

    def held(q):
        return pl.BlockSpec((D, D), lambda i, table: (0, jnp.clip(i - (reps - 1 - q) * per, 0, per - 1)))

    acc, sums, *parts = pl.pallas_call(
        partial(gelu_back_kernel, reps, column),
        out_shape=(shape((rows, D), F32), shape((8, D), F32)) + (far((D, FF // reps), BF),) * reps,
        grid_spec=pltpu.PrefetchScalarGridSpec(
            num_scalar_prefetch=1,
            grid=(FF // D,),
            in_specs=[
                still(gs.shape),
                pl.BlockSpec((D, D), lambda i, table: (column(i, table), 0)),
                pl.BlockSpec((rows, D), lambda i, table: (0, column(i, table))),
                still(norm.shape),
                pl.BlockSpec((D, D), lambda i, table: (0, column(i, table))),
            ],
            out_specs=[still((rows, D)), still((8, D))] + [held(q) for q in range(reps)],
            scratch_shapes=[pltpu.VMEM((rows, D), BF)],
        ),
        compiler_params=params(28),
        name="gelu_back",
        cost_estimate=cost(20),
    )(order.where, gs, stay(w_down), stay(slope), norm, stay(w_up))
    return acc, sums, parts


def hidden_back_kernel(
    where_ref, acc_ref, second_ref, hat_ref, rstd_ref, w_ref, vec_ref, hidden_ref, go_ref, ga_ref, sums_ref
):
    @pl.when(pl.program_id(0) == 0)
    def clear():
        sums_ref[...] = jnp.zeros_like(sums_ref)

    grad = acc_ref[...] + second_ref[...]
    hat = hat_ref[...]
    hidden = norm_back(grad, hat, rstd_ref[...], vec_ref[10:11, :])
    hidden_ref[...] = hidden
    go = hidden.astype(BF)
    go_ref[...] = go
    sums_ref[0:1, :] += col_sum(go.astype(F32))
    sums_ref[1:2, :] += col_sum(grad)
    sums_ref[2:3, :] += col_sum(grad * hat)
    ga_ref[...] = dot_t(go, w_ref[...]).astype(BF)


def hidden_back(order, acc, second, hat, rstd, w_one, vec):
    rows = acc.shape[0]
    return pl.pallas_call(
        hidden_back_kernel,
        grid=(rows // TILE,),
        out_shape=(far((rows, D), F32), shape((rows, D), BF), shape((rows, D), BF), shape((8, D), F32)),
        in_specs=[smem()]
        + [rows_at(D)] * 3
        + [rows_at(1), still((D, D), (0, AT_OUT // D)), still(vec.shape)],
        out_specs=[rows_at(D), rows_at(D), rows_at(D), still((8, D))],
        compiler_params=params(20),
        name="hidden_back",
        cost_estimate=cost(5),
    )(order.where, acc, stay(second), stay(hat), stay(rstd), stay(w_one), vec)


def pair_back(pair, block, rows, ga_ref, proj_ref, probs_ref, low, high):
    q = proj_ref[rows, pair * 128 : (pair + 1) * 128]
    k = proj_ref[rows, D + pair * 128 : D + (pair + 1) * 128]
    v = proj_ref[rows, 2 * D + pair * 128 : 2 * D + (pair + 1) * 128]
    a = ga_ref[rows, pair * 128 : (pair + 1) * 128]
    a2 = jnp.concatenate([a * low, a * high], 0)
    q2 = jnp.concatenate([q * low, q * high], 0)
    k2 = jnp.concatenate([k * low, k * high], 0)
    p = probs_ref[block, pair]
    dp = dot_t(a2, v)
    pf = p.astype(F32)
    ds = (pf * (dp - jnp.sum(pf * dp, -1, keepdims=True)) * HEAD**-0.5).astype(BF)
    wide = jnp.concatenate([ds[:BLOCK], ds[BLOCK:]], 1)
    return dot(wide, k2).astype(BF), t_dot(ds, q2).astype(BF), t_dot(p, a2).astype(BF)


def heads_back(first, count, at, ga_ref, proj_ref, probs_ref, gp_ref):
    low, high = lane_masks()
    for block in range(TILE // BLOCK):
        rows = slice(block * BLOCK, (block + 1) * BLOCK)
        to = pl.ds(pl.multiple_of(at + block * BLOCK, BLOCK), BLOCK)
        for j in range(count):
            three = pair_back(first + j, block, rows, ga_ref, proj_ref, probs_ref, low, high)
            for n, grad in enumerate(three):
                lane = (n * count + j) * 128
                gp_ref[to, lane : lane + 128] = grad


def attend_back_kernel(
    reps, count, where_ref, ga_ref, proj_ref, probs_ref, x_ref, attn_ref, go_ref, gp_ref, sums_ref, *rest
):
    parts, full_ref = rest[:-1], rest[-1]
    i = pl.program_id(0)
    part = count * 128
    heads_back(0, count, i * TILE, ga_ref, proj_ref, probs_ref, gp_ref)

    @pl.when(i == pl.num_programs(0) - 1)
    def weights():
        sums_ref[...] = jnp.zeros_like(sums_ref)
        sums_ref[0:1, :] = col_sum(gp_ref[:, :part].astype(F32))
        sums_ref[1:2, :] = col_sum(gp_ref[:, 2 * part :].astype(F32))
        full_ref[:, :D] = t_dot(attn_ref[...], go_ref[...]).astype(BF)
        full_ref[:, D:] = t_dot(x_ref[...], gp_ref[...]).astype(BF)
        halves(parts, where_ref[1], full_ref.shape[1] // reps, full_ref)


def tile_specs(first):
    per = TILE // BLOCK
    return [
        pl.BlockSpec((TILE, D), lambda i: (i + first, 0)),
        pl.BlockSpec((TILE, 3 * D), lambda i: (i + first, 0)),
        pl.BlockSpec((per, PAIRS, 2 * BLOCK, BLOCK), lambda i: (i + first, 0, 0, 0)),
    ]


def attend_back(plan, order, count, ga, proj, probs, x, attn, go):
    rows = ga.shape[0]
    wide = count * 128
    total = 3 * wide + D
    part = total // plan.reps
    gp, sums, *parts = pl.pallas_call(
        partial(attend_back_kernel, plan.reps, count),
        grid=(rows // TILE,),
        out_shape=(shape((rows, 3 * wide), BF), shape((8, wide), F32)) + (far((D, part), BF),) * plan.reps,
        in_specs=[smem()] + tile_specs(0) + [still(x.shape)] * 3,
        out_specs=[still((rows, 3 * wide)), still((8, wide))] + [still((D, part))] * plan.reps,
        scratch_shapes=[pltpu.VMEM((D, total), BF)],
        compiler_params=params(28),
        name="attend_back",
        cost_estimate=cost(18),
    )(order.where, ga, stay(proj), stay(probs), x, stay(attn), go)
    return gp, sums, parts


def gx_of(count, a_ref, b_ref, w_ref, hidden):
    ca, cb = count * 128, D - count * 128
    for j in range(3):
        hidden = hidden + dot_t(a_ref[:, j * ca : (j + 1) * ca], w_ref[:, j * D : j * D + ca])
        hidden = hidden + dot_t(b_ref[:, j * cb : (j + 1) * cb], w_ref[:, j * D + ca : (j + 1) * D])
    return hidden


def far_back_kernel(count, where_ref, ga_ref, proj_ref, probs_ref, a_ref, w_ref, hidden_ref, gp_ref, far_ref):
    heads_back(count, PAIRS - count, 0, ga_ref, proj_ref, probs_ref, gp_ref)
    far_ref[...] = gx_of(count, a_ref, gp_ref, w_ref, hidden_ref[...]).astype(BF)


def far_back(order, count, ga, proj, probs, gp, w_one, hidden):
    rows = ga.shape[0] // 2
    steps = rows // TILE
    wide = 3 * (D - count * 128)
    return pl.pallas_call(
        partial(far_back_kernel, count),
        grid=(steps,),
        out_shape=(shape((rows, wide), BF), shape((rows, D), BF)),
        in_specs=[smem()]
        + tile_specs(steps)
        + [
            pl.BlockSpec((TILE, gp.shape[1]), lambda i: (i + steps, 0)),
            still((D, 3 * D)),
            pl.BlockSpec((TILE, D), lambda i: (i + steps, 0)),
        ],
        out_specs=[rows_at(wide), rows_at(D)],
        compiler_params=params(24),
        name="far_back",
        cost_estimate=cost(9),
    )(order.where, ga, stay(proj), stay(probs), gp, stay(w_one), stay(hidden))


def near_back_kernel(
    reps, count, where_ref, ga_ref, proj_ref, probs_ref, x_ref, far_ref, lines_ref, sums_ref, gp_ref, *rest
):
    parts, full_ref = rest[:-1], rest[-1]
    i = pl.program_id(0)
    heads_back(count, PAIRS - count, i * TILE, ga_ref, proj_ref, probs_ref, gp_ref)

    @pl.when(i == pl.num_programs(0) - 1)
    def weights():
        part = D - count * 128
        split = count * 128
        half = gp_ref.shape[0]
        full_ref[:, : 3 * part] = (t_dot(x_ref[:half, :], gp_ref[...]) + t_dot(x_ref[half:, :], far_ref[...])).astype(BF)
        lines = lines_ref[...]
        row = lax.broadcasted_iota(jnp.int32, lines.shape, 0)
        for n, at in ((0, 0), (1, 2 * part)):
            rest_of = col_sum(gp_ref[:, at : at + part].astype(F32)) + col_sum(far_ref[:, at : at + part].astype(F32))
            line = jnp.concatenate([sums_ref[n : n + 1, :], rest_of], 1)
            lines = jnp.where(row == n, line, lines)
        full_ref[:, 3 * part : 3 * part + 128] = jnp.transpose(lines).astype(BF)
        full_ref[:, 3 * part + 128 :] = jnp.zeros((D, full_ref.shape[1] - 3 * part - 128), BF)
        halves(parts, where_ref[1], full_ref.shape[1] // reps, full_ref)


def near_back(plan, order, count, ga, proj, probs, x, gp_far, lines, sums):
    rows = ga.shape[0] // 2
    wide = 3 * (D - count * 128)
    total = wide + W_ONE - AT_VEC
    part = total // plan.reps
    gp, *parts = pl.pallas_call(
        partial(near_back_kernel, plan.reps, count),
        grid=(rows // TILE,),
        out_shape=(shape((rows, wide), BF),) + (far((D, part), BF),) * plan.reps,
        in_specs=[smem()] + tile_specs(0) + [still(x.shape), still(gp_far.shape), still(lines.shape), still(sums.shape)],
        out_specs=[still((rows, wide))] + [still((D, part))] * plan.reps,
        scratch_shapes=[pltpu.VMEM((D, total), BF)],
        compiler_params=params(24),
        name="near_back",
        cost_estimate=cost(7),
    )(order.where, ga, stay(proj), stay(probs), x, gp_far, lines, sums)
    return gp, parts


def token_back_kernel(count, where_ref, a_ref, b_ref, w_ref, hidden_ref, own_ref):
    own_ref[...] = gx_of(count, a_ref, b_ref, w_ref, hidden_ref[...])


def token_back(order, count, ga, gb, w_one, hidden):
    rows = gb.shape[0]
    return pl.pallas_call(
        partial(token_back_kernel, count),
        grid=(rows // TILE,),
        out_shape=shape((rows, D), F32),
        in_specs=[smem(), rows_at(ga.shape[1]), rows_at(gb.shape[1]), still((D, 3 * D)), rows_at(D)],
        out_specs=rows_at(D),
        compiler_params=params(24),
        name="token_back",
        cost_estimate=cost(4),
    )(order.where, ga, gb, stay(w_one), stay(hidden))


def on_device(
    plan, query_tokens, passage_tokens, query_cot, passage_cot, positives, w_qkv, w_out, w_up, w_down, biases, gains
):
    me = lax.axis_index("dp")
    core = lax.axis_index("rep")
    tower = (me >> 2) & 1
    span = jnp.where(tower == 0, query_tokens.shape[1], passage_tokens.shape[1])
    where = jnp.stack([me, core, tower, span]).astype(jnp.int32)
    swap = plan.along(1)

    def exchange(a, b):
        a, b = a.reshape(-1, D), b.reshape(-1, D)
        return jnp.concatenate([jnp.where(tower == 0, a, b), send(jnp.where(tower == 0, b, a), swap)], 0)

    def merged(own, back):
        a = jnp.where(tower == 0, own, back)
        b = jnp.where(tower == 0, back, own)
        return a.reshape(query_tokens.shape), b.reshape(passage_tokens.shape)

    vecs = jnp.swapaxes(jnp.concatenate([biases, gains], 1), 1, 2)
    one = jnp.concatenate([w_qkv, w_out, jnp.pad(vecs, ((0, 0), (0, 0), (0, W_ONE - AT_VEC - vecs.shape[2])))], 2)
    mine, other = shards_of(plan, where, one)
    mine2, other2 = shards_of(plan, where, w_up)
    mine3, other3 = shards_of(plan, where, w_down)
    z1 = gather_line(plan, mine, other)
    x = exchange(query_tokens, passage_tokens)
    both2 = jnp.concatenate([mine2, send(other2, swap)], 0)
    z2 = gather_steps(plan, both2, z1)
    p1 = gather_plane(plan, z1, x, both2)
    both3 = jnp.concatenate([mine3, send(after(other3, x), swap)], 0)
    p1 = tuple(after(b, z2, both3) for b in p1)
    order = Order(where)
    w_one = gather_cores(plan, order, p1)
    p2 = gather_plane(plan, z2)
    z3 = gather_steps(plan, both3, z2)
    p3 = gather_plane(plan, after(z3, p2[0]))

    order.done(p2[0])
    first = order.done(attend(order, x, w_one, 0))
    proj, probs, attn, hat1, rstd1, norm, vec = order.done(attend(order, x, w_one, 1, first[:6]))
    w_two = gather_cores(plan, order, tuple(after(b, first[6]) for b in p2))
    half_up = order.done(up(order, norm, w_two, vec, 0))
    act, slope = order.done(up(order, norm, w_two, vec, 1, half_up))
    w_three = gather_cores(plan, order, tuple(after(b, half_up[0]) for b in p3))
    cot = exchange(after(query_cot, p3[0]), after(passage_cot, p3[0]))
    out, hat2, rstd2, cls = order.done(down(order, act, w_three, hat1, vec))
    query_loss, cls_grad = order.done(contrast(plan, order, cls, positives))

    second, gs, sums_top, g_down = order.done(top(plan, order, cot, cls_grad, hat2, rstd2, vec, act))
    half = out.shape[0] // 2
    out_back = send(after(out[half:], gs), swap)
    down_part = Scatter(plan, order, g_down, w_down.shape[1])
    acc, sums_up, g_up = order.done(gelu_back(plan, order, gs, w_three, slope, norm, w_two))
    up_part = Scatter(plan, order, g_up, w_up.shape[1])
    down_part.one()
    hidden, go, ga, sums = order.done(hidden_back(order, acc, second, hat1, rstd1, w_one, vec))
    up_part.one()
    down_part.two()
    order.done(out_back)
    split = 4
    gp_a, sums_a, g_a = order.done(attend_back(plan, order, split, ga, proj, probs, x, attn, go))
    a_part = Scatter(plan, order, g_a, w_qkv.shape[1])
    down_part.three()
    up_part.two()
    lines = jnp.concatenate(
        [jnp.zeros((2, D), F32), sums[0:2], sums_up[0:4], sums_top[0:2], sums[2:3], sums_top[2:3], jnp.zeros((116, D), F32)],
        0,
    )
    gp_far, gx_far = order.done(far_back(order, split, ga, proj, probs, gp_a, w_one, hidden))
    gx_back = send(gx_far, swap)
    a_part.one()
    down_part.four()
    up_part.three()
    gp_near, g_b = order.done(near_back(plan, order, split, ga, proj, probs, x, gp_far, lines, sums_a))
    b_part = Scatter(plan, order, g_b, w_qkv.shape[1])
    a_part.two()
    down_part.last()
    b_part.one()
    up_part.four()
    gx_own = order.done(token_back(order, split, gp_a, gp_near, w_one, hidden))
    a_part.three()
    b_part.two()
    up_part.last()
    a_part.four()
    b_part.three()
    (grad_down,) = finish(plan, order, [down_part], [[(0, D, 0, 0)]], [D])
    (grad_up,) = finish(plan, order, [up_part], [[(0, FF, 0, 0)]], [FF])
    b_part.four()
    query_out, passage_out = merged(out[:half], after(out_back, b_part.out))
    query_grad, passage_grad = merged(gx_own, after(gx_back, b_part.out).astype(F32))
    a_part.last()
    b_part.last()
    qa, qb = split * 128, D - split * 128
    spans_a = [(0, D, 1, 0)] + [(D + j * qa, qa, 0, j * D) for j in range(3)]
    spans_b = [(j * qb, qb, 0, j * D + qa) for j in range(3)] + [(3 * qb, 128, 2, 0)]
    grad_qkv, grad_out, grad_vecs = finish(plan, order, [a_part, b_part], [spans_a, spans_b], [3 * D, D, 128])
    grad_vecs = jnp.swapaxes(grad_vecs[:, :, :12], 1, 2)
    return (
        query_out,
        passage_out,
        query_grad,
        passage_grad,
        query_loss,
        grad_qkv,
        grad_out,
        grad_up,
        grad_down,
        grad_vecs[:, :10],
        grad_vecs[:, 10:],
    )


def solution(mesh):
    plan = Plan(mesh.shape["dp"], mesh.shape["rep"])
    rows = P(("dp", "rep"), None, None)
    shards = P(None, "dp", None)
    lanes = P(None, None, "dp")
    return jax.shard_map(
        partial(on_device, plan),
        mesh=mesh,
        in_specs=(rows,) * 4 + (P(("dp", "rep"), None),) + (shards,) * 4 + (lanes,) * 2,
        out_specs=(rows,) * 4 + (P(("dp", "rep")),) + (shards,) * 4 + (lanes,) * 2,
        check_vma=False,
    )
```

```python
from functools import partial

import jax
import jax.numpy as jnp
from jax import lax
from jax.experimental import pallas as pl
from jax.experimental.pallas import tpu as pltpu
from jax.sharding import PartitionSpec as P

AXES = ("dp", "rep")
BF = jnp.bfloat16
F32 = jnp.float32
D = 768
FF = 3072
HEADS = 12
HEAD = 64
PAIRS = HEADS // 2
BLOCK = 128
TILE = 256
EPS = 1e-05
LOSS_WEIGHT = 32.0
MIB = 2**20
AT_OUT = 3 * D
AT_VEC = 4 * D


def smem():
    return pl.BlockSpec(memory_space=pltpu.SMEM)


def vmem():
    return pl.BlockSpec(memory_space=pltpu.VMEM)


def cost(us):
    return pl.CostEstimate(flops=int(us * 1.0e9), transcendentals=0, bytes_accessed=int(us * 3.0e6))


def behind(us):
    return cost(4 * us)


def params(mib):
    return pltpu.CompilerParams(vmem_limit_bytes=mib * MIB)


def still(shape, at=None):
    index = at if at is not None else (0,) * len(shape)
    return pl.BlockSpec(shape, lambda i, *_: index, pipeline_mode=pl.Buffered(1))


def rows_at(width, rows=TILE):
    return pl.BlockSpec((rows, width), lambda i, *_: (i, 0))


def shape(dims, dtype):
    return jax.ShapeDtypeStruct(dims, dtype)


def far(dims, dtype):
    return pltpu.HBM(dims, dtype)


def stay(v):
    return pltpu.with_memory_space_constraint(v, pltpu.HBM)


def after(v, *others):
    return lax.optimization_barrier((v,) + others)[0]


class Order:
    def __init__(self, where):
        self.where = where

    def done(self, out):
        self.where = after(self.where, out)
        return out


def in_vmem(kernel, name, us, outs, *args, mib=24):
    return pl.pallas_call(
        kernel,
        out_shape=tuple(shape(*o) for o in outs),
        in_specs=[smem() if a.ndim == 1 else vmem() for a in args],
        out_specs=tuple(vmem() for _ in outs),
        compiler_params=params(mib),
        name=name,
        cost_estimate=cost(us),
    )(*args)


def wide(width, reps):
    unit = 128 * reps
    return -(-width // unit) * unit


def by_core(core, reps, width, move):
    if width % 128 == 0:
        move(pl.ds(pl.multiple_of(core * width, 128), width))
        return
    for c in range(reps):

        @pl.when(core == c)
        def one(c=c):
            move(slice(c * width, (c + 1) * width))


def halves(refs, core, source):
    width = refs[0].shape[1]
    for q, ref in enumerate(refs):

        def move(lanes, ref=ref):
            ref[...] = source[:, lanes]

        by_core(core ^ q, len(refs), width, move)


def send(v, pairs):
    return lax.ppermute(v, AXES, pairs)


class Plan:
    def __init__(self, n, reps):
        self.n, self.reps, self.depth = n, reps, n // 4

    def pairs(self, move):
        return [
            (d * self.reps + r, (d ^ move(r)[0]) * self.reps + (r ^ move(r)[1]))
            for d in range(self.n)
            for r in range(self.reps)
        ]

    def along(self, k):
        return self.pairs(lambda r: (4 * k, 0))

    def first(self):
        return self.pairs(lambda r: (1 + r % 2, 0))

    def second(self):
        return self.pairs(lambda r: (2 - r % 2, 0))

    def sibling(self, q):
        return self.pairs(lambda r: (0, q))


def assemble_kernel(depth, reps, width, where_ref, *refs):
    bufs, out = refs[: 2 * reps], refs[2 * reps]
    me, core = where_ref[0], where_ref[1]
    for q in range(reps):
        owner = core ^ q
        p1 = 1 + owner % 2
        p2 = 2 - owner % 2

        def move(lanes, q=q, p1=p1, p2=p2):
            for b in range(2):
                for f in range(2):
                    for k in range(depth):
                        dst = (me ^ (b * p2) ^ (f * p1)) ^ (4 * k)
                        out[pl.ds(dst, 1), :, lanes] = bufs[q * 2 + b][pl.ds(f * depth + k, 1)]

        by_core(owner, reps, width, move)


def shards_kernel(reps, where_ref, qkv_ref, out_ref, bias_ref, gain_ref, up_ref, down_ref, *rest):
    outs, full_ref = rest[:-1], rest[-1]
    core, tower = where_ref[1], where_ref[2]
    spare = full_ref.shape[2] - AT_VEC

    def turned(ref, t, at):
        rows = ref[t][0].astype(F32)
        i = lax.broadcasted_iota(jnp.int32, (rows.shape[0], spare), 0)
        j = lax.broadcasted_iota(jnp.int32, (rows.shape[0], spare), 1)
        return t_dot(rows.astype(BF), jnp.where(i + at == j, 1.0, 0.0).astype(BF))

    for n in range(2):
        t = pl.ds(tower if n == 0 else 1 - tower, 1)
        full_ref[:, :, :AT_OUT] = qkv_ref[t]
        full_ref[:, :, AT_OUT:AT_VEC] = out_ref[t]
        full_ref[0, :, AT_VEC:] = (turned(bias_ref, t, 0) + turned(gain_ref, t, bias_ref.shape[1])).astype(BF)
        for c, ref in enumerate((full_ref, up_ref, down_ref)):
            put = outs[2 * c + n]

            def move(lanes, ref=ref, put=put, t=t):
                put[...] = ref[:, :, lanes] if ref is full_ref else ref[t, :, lanes]

            by_core(core, reps, put.shape[2], move)


def shards_of(plan, order, w_qkv, w_out, biases, gains, w_up, w_down):
    reps = plan.reps
    one = wide(AT_VEC + 128, reps)
    outs = []
    for rows, width in ((w_qkv.shape[1], one), (w_up.shape[1], FF), (w_down.shape[1], D)):
        outs += [shape((1, rows, width // reps), BF)] * 2
    args = (w_qkv, w_out, biases, gains, w_up, w_down)
    got = pl.pallas_call(
        partial(shards_kernel, reps),
        grid=(1,),
        out_shape=tuple(outs),
        in_specs=[smem()] + [still(a.shape) for a in args],
        out_specs=[still(o.shape) for o in outs],
        scratch_shapes=[pltpu.VMEM((1, w_qkv.shape[1], one), BF)],
        compiler_params=params(24),
        name="shards",
        cost_estimate=cost(2),
    )(order.where, *[stay(a) for a in args])
    return order.done(got)


def join_kernel(where_ref, *refs):
    ins, out_ref = refs[:-1], refs[-1]
    at = 0
    for ref in ins:
        out_ref[at : at + ref.shape[0]] = ref[...]
        at += ref.shape[0]


def join(order, *bufs):
    total = sum(b.shape[0] for b in bufs)
    outs = (((total,) + bufs[0].shape[1:], bufs[0].dtype),)
    return order.done(in_vmem(join_kernel, "join", 0.5, outs, order.where, *bufs))[0]


def gather_line(plan, mine, other):
    got = [send(other if k % 2 else mine, plan.along(k)) for k in range(1, plan.depth)]
    return jnp.concatenate([mine] + got, 0)


def gather_steps(plan, both, *others):
    z = both
    k = 2
    while k < plan.depth:
        if others:
            z, others = after(z, *others), ()
        z = jnp.concatenate([z, send(z, plan.along(k))], 0)
        k *= 2
    return z


def gather_plane(plan, z, *others):
    near = jnp.concatenate([z, send(z, plan.first())], 0)
    if others:
        near = after(near, *others)
    return near, send(near, plan.second())


def gather_cores(plan, order, bufs):
    rows, width = bufs[0].shape[1:]
    bufs = list(bufs)
    for q in range(1, plan.reps):
        bufs += [send(b, plan.sibling(q)) for b in bufs[:2]]
    full = pl.pallas_call(
        partial(assemble_kernel, plan.depth, plan.reps, width),
        out_shape=jax.ShapeDtypeStruct((plan.n, rows, width * plan.reps), BF),
        in_specs=[smem()] + [vmem()] * len(bufs),
        out_specs=vmem(),
        compiler_params=params(24),
        name="assemble",
        cost_estimate=cost(2),
    )(order.where, *bufs)
    order.done(full)
    return full.reshape(plan.n * rows, width * plan.reps)


def add_kernel(depth, where_ref, a_hbm, b_ref, s_ref, k_ref, a_ref, sem):
    me, core = where_ref[0], where_ref[1]
    p1 = 1 + core % 2
    p2 = 2 - core % 2
    copies = []
    for j in range(4 * depth):
        at = me ^ ((1 - j // (2 * depth)) * p1) ^ ((1 - j // depth % 2) * p2) ^ (4 * (j % depth))
        copy = pltpu.make_async_copy(a_hbm.at[at], a_ref.at[j], sem.at[j])
        copy.start()
        copies.append((at, copy))
    for j, (at, copy) in enumerate(copies):
        copy.wait()
        o_ref, to = (s_ref, j) if j < 2 * depth else (k_ref, j - 2 * depth)
        o_ref[to] = (a_ref[j].astype(F32) + b_ref[at].astype(F32)).astype(BF)


def two_kernel(where_ref, k_ref, r_ref, s_ref, o_ref):
    q = s_ref.shape[0]
    for j in range(2 * q):
        total = (k_ref[j].astype(F32) + r_ref[j].astype(F32)).astype(BF)
        if j < q:
            s_ref[j] = total
        else:
            o_ref[j - q] = total


def line_kernel(where_ref, k_ref, r_ref, s_ref, o_ref):
    half = o_ref.shape[0]
    for j in range(2 * half):
        total = (k_ref[j].astype(F32) + r_ref[j].astype(F32)).astype(BF)
        if j < half:
            o_ref[j] = total
        else:
            s_ref[j - half] = total


def last_kernel(where_ref, own_ref, got_ref, out):
    tower = where_ref[2]
    out[pl.ds(tower, 1)] = own_ref[...]
    out[pl.ds(1 - tower, 1)] = got_ref[...]


def plus(a, b):
    return (a.astype(F32) + b.astype(F32)).astype(BF)


class Scatter:
    def __init__(self, plan, order, parts, rows):
        self.plan, self.order, self.rows = plan, order, rows
        self.width = parts[0].shape[1]
        parts = [p.reshape(plan.n, rows, self.width) for p in parts]
        self.own = parts[0]
        got = [send(parts[q], plan.sibling(q)) for q in range(1, plan.reps)]
        self.rest = got[0]
        for o in got[1:]:
            self.rest = plus(self.rest, o)

    def run(self, kernel, name, us, outs, *args):
        return self.order.done(in_vmem(kernel, name, us, outs, self.order.where, *args))

    def one(self):
        plan = self.plan
        n = plan.n
        whole = (n, self.rows, self.width)
        half = shape((n // 2, self.rows, self.width), BF)
        hs, self.hk = self.order.done(
            pl.pallas_call(
                partial(add_kernel, plan.depth),
                out_shape=(half, half),
                in_specs=[smem(), pl.BlockSpec(memory_space=pl.ANY), vmem()],
                out_specs=(vmem(), vmem()),
                scratch_shapes=[pltpu.VMEM(whole, BF), pltpu.SemaphoreType.DMA((n,))],
                compiler_params=params(24),
                name="pick_add",
                cost_estimate=behind(3),
            )(self.order.where, stay(self.own), self.rest)
        )
        self.r1 = send(hs, plan.first())

    def two(self):
        quarter = ((self.plan.n // 4, self.rows, self.width), BF)
        ks, self.kk = self.run(two_kernel, "add_two", 1, (quarter, quarter), self.hk, self.r1)
        self.r2 = send(ks, self.plan.second())

    def line(self):
        n = self.kk.shape[0] // 2
        half = ((n, self.rows, self.width), BF)
        out, self.kk = self.run(line_kernel, "add_line", 1, (half, half), self.kk, self.r2)
        self.r2 = send(out, self.plan.along(n))
        return out

    def three(self):
        self.line()

    def four(self):
        while self.kk.shape[0] > 1:
            self.out = self.line()

    def last(self):
        plan = self.plan
        outs = (((2, self.rows, self.width), BF),)
        (pair,) = self.run(last_kernel, "add_last", 1, outs, self.kk, self.r2)
        self.ends = [pair] + [send(pair, plan.sibling(q)) for q in range(1, plan.reps)]


def finish_kernel(reps, spans, where_ref, *refs):
    chunks = len(spans)
    ins, outs = refs[: chunks * reps], refs[chunks * reps :]
    core = where_ref[1]
    for c in range(chunks):
        parts = ins[c * reps : (c + 1) * reps]
        width = parts[0].shape[2]
        for q in range(reps):
            for mine in range(reps):

                @pl.when((core ^ q) == mine)
                def copy(q=q, mine=mine):
                    for at, size, out, to in spans[c]:
                        low, high = max(at, mine * width), min(at + size, (mine + 1) * width)
                        if low < high:
                            outs[out][:, :, to + low - at : to + high - at] = parts[q][
                                :, :, low - mine * width : high - mine * width
                            ].astype(F32)


def finish(plan, order, chunks, spans, widths):
    rows = chunks[0].rows
    outs = tuple(((2, rows, w), F32) for w in widths)
    args = [p for c in chunks for p in c.ends]
    return order.done(in_vmem(partial(finish_kernel, plan.reps, spans), "finish", 2, outs, order.where, *args))


def dot(a, b):
    return jnp.dot(a, b, preferred_element_type=F32)


def dot_t(a, b):
    return lax.dot_general(a, b, (((1,), (1,)), ((), ())), preferred_element_type=F32)


def t_dot(a, b):
    return lax.dot_general(a, b, (((0,), (0,)), ((), ())), preferred_element_type=F32)


def normalize(h):
    center = h - jnp.mean(h, -1, keepdims=True)
    rstd = lax.rsqrt(jnp.mean(center * center, -1, keepdims=True) + EPS)
    return center * rstd, rstd


def lane_masks():
    lane = lax.broadcasted_iota(jnp.int32, (1, 2 * HEAD), 1)
    low = (lane < HEAD).astype(F32).astype(BF)
    return low, (1.0 - low.astype(F32)).astype(BF)


def attend_kernel(part, where_ref, x_ref, w_ref, *rest):
    proj_ref, probs_ref, attn_ref, hat_ref, rstd_ref, norm_ref, vec_ref, cls_ref, bias_ref = rest[-9:]

    @pl.when(pl.program_id(0) == 0)
    def prepare():
        vec_ref[...] = jnp.transpose(w_ref[:, AT_VEC : AT_VEC + 128].astype(F32))
        span = where_ref[3]
        row = lax.broadcasted_iota(jnp.int32, (BLOCK, 2 * BLOCK), 0)
        col = lax.broadcasted_iota(jnp.int32, (BLOCK, 2 * BLOCK), 1) % BLOCK
        bias_ref[...] = jnp.where((row ^ col) < span, 0.0, -1e30)

    x = x_ref[...]
    for j in range(3):
        part = dot(x, w_ref[:, j * D : (j + 1) * D])
        if j != 1:
            part = part + vec_ref[j // 2 : j // 2 + 1, :]
        proj_ref[:, j * D : (j + 1) * D] = part.astype(BF)
    low, high = lane_masks()
    bias = bias_ref[...]
    for blk in range(TILE // BLOCK):
        rows = slice(blk * BLOCK, (blk + 1) * BLOCK)
        for pair in range(PAIRS):
            lanes = slice(pair * 128, (pair + 1) * 128)
            q = proj_ref[rows, lanes]
            k = proj_ref[rows, D + pair * 128 : D + (pair + 1) * 128]
            v = proj_ref[rows, 2 * D + pair * 128 : 2 * D + (pair + 1) * 128]
            s = dot_t(k, jnp.concatenate([q * low, q * high], 0)) * HEAD**-0.5 + bias
            e = jnp.exp(s - jnp.max(s, 0, keepdims=True))
            p = (e * (1.0 / jnp.sum(e, 0, keepdims=True))).astype(BF)
            probs_ref[blk, pair] = p
            tall = jnp.concatenate([p[:, :BLOCK], p[:, BLOCK:]], 0)
            attn_ref[rows, lanes] = t_dot(tall, jnp.concatenate([v * low, v * high], 0)).astype(BF)
    hidden = x.astype(F32) + (dot(attn_ref[...], w_ref[:, AT_OUT:AT_VEC]) + vec_ref[2:3, :])
    hat, rstd = normalize(hidden)
    hat_ref[...] = hat
    rstd_ref[...] = rstd
    norm = hat * vec_ref[10:11, :] + vec_ref[3:4, :]
    norm_ref[...] = norm.astype(BF)
    for j in range(TILE // 32):
        cls_ref[j : j + 1, :] = norm[32 * j : 32 * j + 1, :]


def attend(order, x, w_one, part, before=()):
    rows = x.shape[0]
    per = TILE // BLOCK
    steps = rows // TILE // 2
    first = part * steps

    def here(width):
        return pl.BlockSpec((TILE, width), lambda i: (i + first, 0))

    return pl.pallas_call(
        partial(attend_kernel, part),
        grid=(steps,),
        out_shape=(
            far((rows, 3 * D), BF),
            far((rows // BLOCK, PAIRS, BLOCK, 2 * BLOCK), BF),
            far((rows, D), BF),
            far((rows, D), F32),
            far((rows, 1), F32),
            far((rows, D), BF),
            shape((128, D), F32),
            shape((rows // 64, D), F32),
        ),
        in_specs=[smem(), here(D), vmem()] + [pl.BlockSpec(memory_space=pl.ANY)] * len(before),
        out_specs=[
            here(3 * D),
            pl.BlockSpec((per, PAIRS, BLOCK, 2 * BLOCK), lambda i: (i + first, 0, 0, 0)),
            here(D),
            here(D),
            here(1),
            here(D),
            still((128, D)),
            rows_at(D, TILE // 32),
        ],
        scratch_shapes=[pltpu.VMEM((BLOCK, 2 * BLOCK), F32)],
        input_output_aliases={3 + j: j for j in range(len(before))},
        compiler_params=params(24),
        name="attend",
        cost_estimate=cost(7),
    )(order.where, x, w_one, *[stay(b) for b in before])


def gelu_pair(u):
    phi = 0.5 + 0.5 * lax.erf(u * 2**-0.5)
    return u * phi, phi + u * (jnp.exp(-0.5 * u * u) * (2 * jnp.pi) ** -0.5)


def up_kernel(first, where_ref, norm_ref, w_ref, vec_ref, *rest):
    act_ref, slope_ref = rest[-2:]
    bias = vec_ref[pl.ds(4 + first + pl.program_id(0), 1), :]
    for m in range(0, norm_ref.shape[0], TILE):
        rows = slice(m, m + TILE)
        act, slope = gelu_pair(dot(norm_ref[rows, :], w_ref[...]) + bias)
        act_ref[rows, :] = act.astype(BF)
        slope_ref[rows, :] = slope.astype(BF)


def up(order, norm, w_up, vec, part, before=()):
    rows = norm.shape[0]
    steps = FF // D // 2
    first = part * steps
    col = pl.BlockSpec((rows, D), lambda i: (0, i + first))
    return pl.pallas_call(
        partial(up_kernel, first),
        grid=(steps,),
        out_shape=(far((rows, FF), BF), far((rows, FF), BF)),
        in_specs=[
            smem(),
            still(norm.shape),
            pl.BlockSpec((D, D), lambda i: (0, i + first)),
            still(vec.shape),
        ]
        + [pl.BlockSpec(memory_space=pl.ANY)] * len(before),
        out_specs=[col, col],
        input_output_aliases={4 + j: j for j in range(len(before))},
        compiler_params=params(24),
        name="up",
        cost_estimate=cost(8),
    )(order.where, norm, w_up, vec, *[stay(b) for b in before])


def down_kernel(where_ref, act_ref, w_ref, hat_ref, vec_ref, own_ref, far_ref, hat2_ref, rstd2_ref):
    normed = hat_ref[...] * vec_ref[10:11, :] + vec_ref[3:4, :]
    second = normed + (dot(act_ref[...], w_ref[...]) + vec_ref[8:9, :])
    hat, rstd = normalize(second)
    hat2_ref[...] = hat
    rstd2_ref[...] = rstd
    out = (hat * vec_ref[11:12, :] + vec_ref[9:10, :]).astype(BF)
    half = pl.num_programs(0) // 2

    @pl.when(pl.program_id(0) < half)
    def near():
        own_ref[...] = out

    @pl.when(pl.program_id(0) >= half)
    def away():
        far_ref[...] = out


def down(order, act, w_down, hat, vec):
    rows = act.shape[0]
    half = rows // TILE // 2
    near = pl.BlockSpec((TILE, D), lambda i: (jnp.minimum(i, half - 1), 0))
    away = pl.BlockSpec((TILE, D), lambda i: (jnp.maximum(i - half, 0), 0))
    return pl.pallas_call(
        down_kernel,
        grid=(rows // TILE,),
        out_shape=(far((rows // 2, D), BF), shape((rows // 2, D), BF), far((rows, D), F32), far((rows, 1), F32)),
        in_specs=[smem(), rows_at(FF), vmem(), rows_at(D), still(vec.shape)],
        out_specs=[near, away, rows_at(D), rows_at(1)],
        compiler_params=params(24),
        name="down",
        cost_estimate=cost(8),
    )(order.where, stay(act), w_down, stay(hat), vec)


def first_kernel(where_ref, a_ref, b_ref, up_ref, down_ref, vec_ref, marks_ref, msg_ref):
    norm = jnp.concatenate([a_ref[...], b_ref[...]], 0)
    second = norm + vec_ref[8:9, :]
    wide = norm.astype(BF)
    for j in range(FF // D):
        u = dot(wide, up_ref[:, j * D : (j + 1) * D]) + vec_ref[4 + j : 5 + j, :]
        second = second + dot(gelu_pair(u)[0].astype(BF), down_ref[j * D : (j + 1) * D, :])
    hat, _ = normalize(second)
    msg_ref[:, :D] = (hat * vec_ref[11:12, :] + vec_ref[9:10, :]).astype(BF)
    marks = marks_ref[...].astype(F32)
    pad = jnp.zeros((32 - marks.shape[0], marks.shape[1]), F32)
    msg_ref[:, D:] = jnp.concatenate([marks, pad], 0).astype(BF)


def first_rows(order, a, b, w_up, w_down, vec, positives):
    outs = (((32, D + positives.shape[1]), BF),)
    return order.done(in_vmem(first_kernel, "first_rows", 4, outs, order.where, a, b, w_up, w_down, vec, positives))[0]


def pack_kernel(per, where_ref, *refs):
    msgs, out_ref = refs[:-1], refs[-1]
    queries = per * 4
    pick_row = lax.broadcasted_iota(jnp.int32, (16, 32), 0)
    pick_col = lax.broadcasted_iota(jnp.int32, (16, 32), 1)
    pick = jnp.where((pick_col == pick_row * (32 // (2 * per))) & (pick_row < 2 * per), 1.0, 0.0).astype(BF)
    for n in range(len(msgs) // 2):
        for tower in range(2):

            @pl.when(where_ref[2] == tower)
            def put(n=n, tower=tower):
                zero, one = msgs[2 * n + tower], msgs[2 * n + 1 - tower]
                out_ref[n, :32, :D] = zero[:, :D]
                out_ref[n, :queries, D:] = zero[:queries, D:]
                out_ref[n, queries:32, D:] = one[:queries, D:]
                out_ref[n, 32:, :D] = dot(pick, one[:, :D]).astype(BF)
                out_ref[n, 32:, D:] = jnp.zeros((16, out_ref.shape[2] - D), BF)


def contrast_kernel(reps, depth, per, where_ref, *refs):
    parts, loss_ref, grad_ref, acc_ref = refs[:reps], refs[reps], refs[reps + 1], refs[reps + 2]
    me, core, tower = where_ref[0], where_ref[1], where_ref[2]
    pieces = parts[0].shape[0]
    passages = parts[0].shape[2] - D
    cls_p = jnp.concatenate([part[:, 32:, :D].reshape(pieces * 16, D) for part in parts], 0)
    cols = cls_p.shape[0]
    col = lax.broadcasted_iota(jnp.int32, (passages, cols), 1)
    row = lax.broadcasted_iota(jnp.int32, (passages, cols), 0)
    j, slot = col // 16, col % 16
    base = (me | 4) ^ (8 * (j % (depth // 2))) ^ ((j // (depth // 2)) % 4)
    owner = jnp.where(slot < per, base, base ^ 4)
    passage = (owner * reps + (core ^ (j // (2 * depth)))) * per + slot % per
    pick = jnp.where((row == passage) & (slot < 2 * per), 1.0, 0.0).astype(BF)
    valid = lax.broadcasted_iota(jnp.int32, (1, cols), 1) % 16 < 2 * per
    acc_ref[...] = jnp.zeros_like(acc_ref)
    group = min(8, pieces)
    for q, part in enumerate(parts):
        for at in range(0, pieces, group):
            cls_q = part[at : at + group, :32, :D].reshape(group * 32, D)
            marks = dot(part[at : at + group, :32, D:].reshape(group * 32, passages), pick)
            raw = jnp.where(valid, dot_t(cls_q, cls_p) * D**-0.5, -1e30)
            e = jnp.exp(raw - jnp.max(raw, -1, keepdims=True))
            total = jnp.sum(e, -1, keepdims=True)
            me_ = marks * e
            marked = jnp.sum(me_, -1, keepdims=True)
            grad = (LOSS_WEIGHT * (e / total - me_ / marked)).astype(BF)
            acc_ref[...] += t_dot(grad[:, :128], cls_q)[:16] * D**-0.5
            if q == 0 and at == 0:
                loss_ref[...] = (jnp.log(total) - jnp.log(marked))[:32]
                grad_ref[...] = dot(grad[:32], cls_p) * D**-0.5

    @pl.when(tower == 1)
    def passages_own():
        grad_ref[...] = jnp.zeros_like(grad_ref)
        for s in range(2 * per):
            at = s * (32 // (2 * per))
            grad_ref[at : at + 1, :] = acc_ref[s : s + 1, :]


class Contrast:
    def __init__(self, plan, order, msg, queries):
        self.plan, self.order, self.queries = plan, order, queries
        self.msgs = [msg] + [send(msg, plan.along(k)) for k in range(1, plan.depth)]

    def pack(self):
        plan = self.plan
        outs = (((plan.depth // 2, 48, self.msgs[0].shape[1]), BF),)
        kernel = partial(pack_kernel, self.queries // 4)
        (buf,) = self.order.done(in_vmem(kernel, "pack", 1, outs, self.order.where, *self.msgs))
        self.bufs = [buf] + [send(buf, plan.pairs(lambda r, m=m: (m, 0))) for m in range(1, 4)]

    def join(self):
        plan = self.plan
        buf = join(self.order, *self.bufs)
        self.parts = [buf] + [send(buf, plan.sibling(s)) for s in range(1, plan.reps)]

    def loss(self):
        plan, order = self.plan, self.order
        loss, grad = order.done(
            pl.pallas_call(
                partial(contrast_kernel, plan.reps, plan.depth, self.queries // 4),
                out_shape=(shape((32, 1), F32), shape((32, D), F32)),
                in_specs=[smem()] + [vmem()] * plan.reps,
                out_specs=(vmem(), vmem()),
                scratch_shapes=[pltpu.VMEM((16, D), F32)],
                compiler_params=params(40),
                name="contrast",
                cost_estimate=cost(2),
            )(order.where, *self.parts)
        )
        at = order.where[2] * self.queries
        return lax.dynamic_slice(loss, (at, 0), (self.queries, 1))[:, 0], grad


def norm_back(grad, hat, rstd, gain):
    scaled = grad * gain
    a = jnp.mean(scaled, -1, keepdims=True)
    b = jnp.mean(scaled * hat, -1, keepdims=True)
    return rstd * (scaled - a - hat * b)


def col_sum(v):
    return jnp.sum(v, 0, keepdims=True)


def top_kernel(
    where_ref, cot_ref, cls_ref, hat_ref, rstd_ref, vec_ref, act_ref, second_ref, gs_ref, sums_ref, *rest
):
    parts, full_ref = rest[:-1], rest[-1]

    @pl.when(pl.program_id(0) == 0)
    def norm():
        groups = TILE // 32
        at_first = lax.broadcasted_iota(jnp.int32, (groups, 32, D), 1) == 0
        sums_ref[...] = jnp.zeros_like(sums_ref)
        for m in range(0, cot_ref.shape[0], TILE):
            rows = slice(m, m + TILE)
            cls = cls_ref[m // 32 : (m + TILE) // 32, :].reshape(groups, 1, D)
            dout = cot_ref[rows, :].astype(F32) + jnp.where(at_first, cls, 0.0).reshape(TILE, D)
            hat = hat_ref[rows, :]
            grad = norm_back(dout, hat, rstd_ref[rows, :], vec_ref[11:12, :])
            second_ref[rows, :] = grad
            gs = grad.astype(BF)
            gs_ref[rows, :] = gs
            sums_ref[0:1, :] += col_sum(gs.astype(F32))
            sums_ref[1:2, :] += col_sum(dout)
            sums_ref[2:3, :] += col_sum(dout * hat)

    full_ref[...] = t_dot(act_ref[...], gs_ref[...]).astype(BF)
    halves(parts, where_ref[1], full_ref)


def top(plan, order, cot, cls_grad, hat2, rstd2, vec, act):
    rows = cot.shape[0]
    part = D // plan.reps
    second, gs, sums, *parts = pl.pallas_call(
        top_kernel,
        grid=(FF // D,),
        out_shape=(far((rows, D), F32), shape((rows, D), BF), shape((8, D), F32))
        + (far((FF, part), BF),) * plan.reps,
        in_specs=[
            smem(),
            still(cot.shape),
            still(cls_grad.shape),
            still(hat2.shape),
            still(rstd2.shape),
            still(vec.shape),
            pl.BlockSpec((rows, D), lambda i: (0, i)),
        ],
        out_specs=[still((rows, D)), still((rows, D)), still((8, D))] + [rows_at(part, D)] * plan.reps,
        scratch_shapes=[pltpu.VMEM((D, D), BF)],
        compiler_params=params(28),
        name="top",
        cost_estimate=behind(11),
    )(order.where, cot, cls_grad, hat2, rstd2, vec, stay(act))
    return second, gs, sums, parts


def gelu_back_kernel(reps, column, where_ref, gs_ref, w_ref, slope_ref, norm_ref, up_ref, acc_ref, sums_ref, *rest):
    parts, gu_ref = rest[:-1], rest[-1]
    i = pl.program_id(0)
    total = jnp.zeros((1, D), F32)
    for m in range(0, gs_ref.shape[0], TILE):
        rows = slice(m, m + TILE)
        gu = (dot_t(gs_ref[rows, :], w_ref[...]) * slope_ref[rows, :].astype(F32)).astype(BF)
        gu_ref[rows, :] = gu
        total = total + col_sum(gu.astype(F32))
    sums_ref[pl.ds(column(i, where_ref), 1), :] = total
    grad = t_dot(norm_ref[...], gu_ref[...]).astype(BF)
    per = (FF // D) // reps
    for q in range(reps):

        @pl.when(i // per == reps - 1 - q)
        def put(q=q):
            parts[q][...] = grad

    @pl.when(i == 0)
    def start():
        acc_ref[...] = dot_t(gu_ref[...], up_ref[...])

    @pl.when(i > 0)
    def add():
        acc_ref[...] += dot_t(gu_ref[...], up_ref[...])


def gelu_back(plan, order, gs, w_down, slope, norm, w_up):
    rows = gs.shape[0]
    reps = plan.reps
    per = (FF // D) // reps

    def column(i, table):
        return (table[1] ^ (reps - 1 - i // per)) * per + i % per

    def held(q):
        return pl.BlockSpec((D, D), lambda i, table: (0, jnp.clip(i - (reps - 1 - q) * per, 0, per - 1)))

    acc, sums, *parts = pl.pallas_call(
        partial(gelu_back_kernel, reps, column),
        out_shape=(shape((rows, D), F32), shape((8, D), F32)) + (far((D, FF // reps), BF),) * reps,
        grid_spec=pltpu.PrefetchScalarGridSpec(
            num_scalar_prefetch=1,
            grid=(FF // D,),
            in_specs=[
                still(gs.shape),
                pl.BlockSpec((D, D), lambda i, table: (column(i, table), 0)),
                pl.BlockSpec((rows, D), lambda i, table: (0, column(i, table))),
                still(norm.shape),
                pl.BlockSpec((D, D), lambda i, table: (0, column(i, table))),
            ],
            out_specs=[still((rows, D)), still((8, D))] + [held(q) for q in range(reps)],
            scratch_shapes=[pltpu.VMEM((rows, D), BF)],
        ),
        compiler_params=params(28),
        name="gelu_back",
        cost_estimate=behind(20),
    )(order.where, gs, stay(w_down), stay(slope), norm, stay(w_up))
    return acc, sums, parts


def hidden_back_kernel(
    where_ref, acc_ref, second_ref, hat_ref, rstd_ref, w_ref, vec_ref, hidden_ref, go_ref, ga_ref, sums_ref
):
    @pl.when(pl.program_id(0) == 0)
    def clear():
        sums_ref[...] = jnp.zeros_like(sums_ref)

    grad = acc_ref[...] + second_ref[...]
    hat = hat_ref[...]
    hidden = norm_back(grad, hat, rstd_ref[...], vec_ref[10:11, :])
    hidden_ref[...] = hidden
    go = hidden.astype(BF)
    go_ref[...] = go
    sums_ref[0:1, :] += col_sum(go.astype(F32))
    sums_ref[1:2, :] += col_sum(grad)
    sums_ref[2:3, :] += col_sum(grad * hat)
    ga_ref[...] = dot_t(go, w_ref[...]).astype(BF)


def hidden_back(order, acc, second, hat, rstd, w_one, vec):
    rows = acc.shape[0]
    return pl.pallas_call(
        hidden_back_kernel,
        grid=(rows // TILE,),
        out_shape=(far((rows, D), F32), shape((rows, D), BF), shape((rows, D), BF), shape((8, D), F32)),
        in_specs=[smem()]
        + [rows_at(D)] * 3
        + [rows_at(1), still((D, D), (0, AT_OUT // D)), still(vec.shape)],
        out_specs=[rows_at(D), rows_at(D), rows_at(D), still((8, D))],
        compiler_params=params(20),
        name="hidden_back",
        cost_estimate=behind(5),
    )(order.where, acc, stay(second), stay(hat), stay(rstd), stay(w_one), vec)


def pair_back(pair, block, rows, ga_ref, proj_ref, probs_ref, low, high):
    q = proj_ref[rows, pair * 128 : (pair + 1) * 128]
    k = proj_ref[rows, D + pair * 128 : D + (pair + 1) * 128]
    v = proj_ref[rows, 2 * D + pair * 128 : 2 * D + (pair + 1) * 128]
    a = ga_ref[rows, pair * 128 : (pair + 1) * 128]
    a2 = jnp.concatenate([a * low, a * high], 0)
    q2 = jnp.concatenate([q * low, q * high], 0)
    k2 = jnp.concatenate([k * low, k * high], 0)
    p = probs_ref[block, pair]
    dp = dot_t(v, a2)
    pf = p.astype(F32)
    ds = (pf * (dp - jnp.sum(pf * dp, 0, keepdims=True)) * HEAD**-0.5).astype(BF)
    tall = jnp.concatenate([ds[:, :BLOCK], ds[:, BLOCK:]], 0)
    return t_dot(tall, k2).astype(BF), dot(ds, q2).astype(BF), dot(p, a2).astype(BF)


def heads_back(first, count, at, ga_ref, proj_ref, probs_ref, gp_ref):
    low, high = lane_masks()
    for block in range(TILE // BLOCK):
        rows = slice(block * BLOCK, (block + 1) * BLOCK)
        to = pl.ds(pl.multiple_of(at + block * BLOCK, BLOCK), BLOCK)
        for j in range(count):
            three = pair_back(first + j, block, rows, ga_ref, proj_ref, probs_ref, low, high)
            for n, grad in enumerate(three):
                lane = (n * count + j) * 128
                gp_ref[to, lane : lane + 128] = grad


def attend_back_kernel(first, count, where_ref, ga_ref, proj_ref, probs_ref, gp_ref):
    heads_back(first, count, 0, ga_ref, proj_ref, probs_ref, gp_ref)


def tile_specs(first):
    per = TILE // BLOCK
    return [
        pl.BlockSpec((TILE, D), lambda i: (i + first, 0)),
        pl.BlockSpec((TILE, 3 * D), lambda i: (i + first, 0)),
        pl.BlockSpec((per, PAIRS, BLOCK, 2 * BLOCK), lambda i: (i + first, 0, 0, 0)),
    ]


def attend_back(order, first, count, ga, proj, probs, rows):
    wide = 3 * count * 128
    return pl.pallas_call(
        partial(attend_back_kernel, first, count),
        grid=(rows // TILE,),
        out_shape=shape((rows, wide), BF),
        in_specs=[smem()] + tile_specs(0),
        out_specs=rows_at(wide),
        compiler_params=params(20),
        name="attend_back",
        cost_estimate=behind(10 * count * rows // 4096),
    )(order.where, ga, stay(proj), stay(probs))


def both_rows(x_ref, near_ref, far_ref):
    half = near_ref.shape[0]
    return (t_dot(x_ref[:half, :], near_ref[...]) + t_dot(x_ref[half:, :], far_ref[...])).astype(BF)


def first_weights_kernel(where_ref, x_ref, near_ref, far_ref, attn_ref, go_ref, *rest):
    parts, full_ref = rest[:-1], rest[-1]
    full_ref[:, :D] = t_dot(attn_ref[...], go_ref[...]).astype(BF)
    end = D + near_ref.shape[1]
    full_ref[:, D:end] = both_rows(x_ref, near_ref, far_ref)
    if end < full_ref.shape[1]:
        full_ref[:, end:] = jnp.zeros((D, full_ref.shape[1] - end), BF)
    halves(parts, where_ref[1], full_ref)


def last_weights_kernel(
    count, where_ref, x_ref, near_ref, far_ref, first_near_ref, first_far_ref, up_ref, top_ref, hidden_ref, *rest
):
    parts, full_ref, lines_ref = rest[:-2], rest[-2], rest[-1]
    part = D - count * 128
    wide = count * 128
    full_ref[:, : 3 * part] = both_rows(x_ref, near_ref, far_ref)

    def sums(j, width, a_ref, b_ref):
        lanes = slice(j * width, (j + 1) * width)
        return col_sum(a_ref[:, lanes].astype(F32)) + col_sum(b_ref[:, lanes].astype(F32))

    lines_ref[...] = jnp.zeros_like(lines_ref)
    for n, j in ((0, 0), (1, 2)):
        lines_ref[n : n + 1, :wide] = sums(j, wide, first_near_ref, first_far_ref)
        lines_ref[n : n + 1, wide:] = sums(j, part, near_ref, far_ref)
    lines_ref[2:4, :] = hidden_ref[0:2, :]
    lines_ref[4:8, :] = up_ref[0:4, :]
    lines_ref[8:10, :] = top_ref[0:2, :]
    lines_ref[10:11, :] = hidden_ref[2:3, :]
    lines_ref[11:12, :] = top_ref[2:3, :]
    full_ref[:, 3 * part : 3 * part + 128] = jnp.transpose(lines_ref[...]).astype(BF)
    full_ref[:, 3 * part + 128 :] = jnp.zeros((D, full_ref.shape[1] - 3 * part - 128), BF)
    halves(parts, where_ref[1], full_ref)


def weights(plan, order, kernel, name, us, total, scratch, *args):
    part = total // plan.reps
    return pl.pallas_call(
        kernel,
        grid=(1,),
        out_shape=(far((D, part), BF),) * plan.reps,
        in_specs=[smem()] + [still(a.shape) for a in args],
        out_specs=[still((D, part))] * plan.reps,
        scratch_shapes=[pltpu.VMEM((D, total), BF)] + scratch,
        compiler_params=params(28),
        name=name,
        cost_estimate=behind(us),
    )(order.where, *args)


def gx_of(count, a_ref, b_ref, w_ref, hidden):
    ca, cb = count * 128, D - count * 128
    for j in range(3):
        hidden = hidden + dot_t(a_ref[:, j * ca : (j + 1) * ca], w_ref[:, j * D : j * D + ca])
        hidden = hidden + dot_t(b_ref[:, j * cb : (j + 1) * cb], w_ref[:, j * D + ca : (j + 1) * D])
    return hidden


def far_back_kernel(count, where_ref, ga_ref, proj_ref, probs_ref, w_ref, hidden_ref, a_ref, b_ref, far_ref):
    heads_back(0, count, 0, ga_ref, proj_ref, probs_ref, a_ref)
    heads_back(count, PAIRS - count, 0, ga_ref, proj_ref, probs_ref, b_ref)
    far_ref[...] = gx_of(count, a_ref, b_ref, w_ref, hidden_ref[...]).astype(BF)


def far_back(order, count, ga, proj, probs, w_one, hidden):
    rows = ga.shape[0] // 2
    steps = rows // TILE
    wide = 3 * count * 128
    return pl.pallas_call(
        partial(far_back_kernel, count),
        grid=(steps,),
        out_shape=(shape((rows, wide), BF), shape((rows, 3 * D - wide), BF), shape((rows, D), BF)),
        in_specs=[smem()]
        + tile_specs(steps)
        + [still((D, 3 * D)), pl.BlockSpec((TILE, D), lambda i: (i + steps, 0))],
        out_specs=[rows_at(wide), rows_at(3 * D - wide), rows_at(D)],
        compiler_params=params(24),
        name="far_back",
        cost_estimate=behind(11),
    )(order.where, ga, stay(proj), stay(probs), stay(w_one), stay(hidden))


def token_back_kernel(count, where_ref, a_ref, b_ref, w_ref, hidden_ref, own_ref):
    own_ref[...] = gx_of(count, a_ref, b_ref, w_ref, hidden_ref[...])


def token_back(order, count, ga, gb, w_one, hidden):
    rows = gb.shape[0]
    return pl.pallas_call(
        partial(token_back_kernel, count),
        grid=(rows // TILE,),
        out_shape=shape((rows, D), F32),
        in_specs=[smem(), rows_at(ga.shape[1]), rows_at(gb.shape[1]), still((D, 3 * D)), rows_at(D)],
        out_specs=rows_at(D),
        compiler_params=params(24),
        name="token_back",
        cost_estimate=behind(4),
    )(order.where, ga, gb, stay(w_one), stay(hidden))


def on_device(
    plan, query_tokens, passage_tokens, query_cot, passage_cot, positives, w_qkv, w_out, w_up, w_down, biases, gains
):
    me = lax.axis_index("dp")
    core = lax.axis_index("rep")
    tower = (me >> 2) & 1
    span = jnp.where(tower == 0, query_tokens.shape[1], passage_tokens.shape[1])
    where = jnp.stack([me, core, tower, span]).astype(jnp.int32)
    swap = plan.along(1)

    def exchange(a, b, *others):
        a, b = a.reshape(-1, D), b.reshape(-1, D)
        away = jnp.where(tower == 0, b, a)
        return jnp.where(tower == 0, a, b), send(after(away, *others) if others else away, swap)

    def merged(own, back):
        a = jnp.where(tower == 0, own, back)
        b = jnp.where(tower == 0, back, own)
        return a.reshape(query_tokens.shape), b.reshape(passage_tokens.shape)

    order = Order(where)
    mine, other, mine2, other2, mine3, other3 = shards_of(plan, order, w_qkv, w_out, biases, gains, w_up, w_down)
    z1 = gather_line(plan, mine, other)
    x_mine, x_got = exchange(query_tokens, passage_tokens)
    both2 = jnp.concatenate([mine2, send(other2, swap)], 0)
    z2 = gather_steps(plan, both2, z1)
    p1 = gather_plane(plan, z1, both2)
    x = jnp.concatenate([x_mine, x_got], 0)
    both3 = jnp.concatenate([mine3, send(after(other3, x), swap)], 0)
    p1 = tuple(after(b, z2, both3) for b in p1)
    w_one = gather_cores(plan, order, p1)
    p2 = gather_plane(plan, z2)
    z3 = gather_steps(plan, both3, z2)
    p3 = gather_plane(plan, after(z3, p2[0]))

    order.done(p2[0])
    first = order.done(attend(order, x, w_one, 0))
    proj, probs, attn, hat1, rstd1, norm, vec, cls_b = order.done(attend(order, x, w_one, 1, first[:6]))
    w_two = gather_cores(plan, order, tuple(after(b, first[6]) for b in p2))
    cot_mine, cot_got = exchange(query_cot, passage_cot, z3)
    half_up = order.done(up(order, norm, w_two, vec, 0))
    act, slope = order.done(up(order, norm, w_two, vec, 1, half_up))
    cot = jnp.concatenate([cot_mine, cot_got], 0)
    w_three = gather_cores(plan, order, tuple(after(b, half_up[0]) for b in p3))
    msg = first_rows(order, first[7], cls_b, w_two, w_three, vec, positives)
    loss = Contrast(plan, order, msg, positives.shape[0])
    out_own, out_far, hat2, rstd2 = order.done(down(order, act, w_three, hat1, vec))
    out_back = send(out_far, swap)
    loss.pack()
    order.done(cot)
    loss.join()
    query_loss, cls_grad = loss.loss()

    second, gs, sums_top, g_down = order.done(top(plan, order, cot, cls_grad, hat2, rstd2, vec, act))
    down_part = Scatter(plan, order, g_down, w_down.shape[1])
    acc, sums_up, g_up = order.done(gelu_back(plan, order, gs, w_three, slope, norm, w_two))
    up_part = Scatter(plan, order, g_up, w_up.shape[1])
    order.done(out_back)
    down_part.one()
    hidden, go, ga, sums = order.done(hidden_back(order, acc, second, hat1, rstd1, w_one, vec))
    up_part.one()
    split = 4
    half = ga.shape[0] // 2
    far_a, far_b, gx_far = order.done(far_back(order, split, ga, proj, probs, w_one, hidden))
    gx_back = send(gx_far, swap)
    near_a = order.done(attend_back(order, 0, split, ga, proj, probs, half))
    total = wide(3 * split * 128 + D, plan.reps)
    kernel = first_weights_kernel
    g_a = order.done(weights(plan, order, kernel, "first_weights", 5, total, [], x, near_a, far_a, stay(attn), go))
    a_part = Scatter(plan, order, g_a, w_qkv.shape[1])
    order.done(gx_back)
    down_part.two()
    up_part.two()
    near_b = order.done(attend_back(order, split, PAIRS - split, ga, proj, probs, half))
    down_part.three()
    a_part.one()
    up_part.three()
    total = wide(3 * (D - split * 128) + 128, plan.reps)
    kernel = partial(last_weights_kernel, split)
    scratch = [pltpu.VMEM((128, D), F32)]
    args = (x, near_b, far_b, near_a, far_a, sums_up, sums_top, sums)
    g_b = order.done(weights(plan, order, kernel, "last_weights", 4, total, scratch, *args))
    b_part = Scatter(plan, order, g_b, w_qkv.shape[1])
    gx_own = order.done(token_back(order, split, near_a, near_b, w_one, hidden))
    a_part.two()
    b_part.one()
    down_part.four()
    up_part.four()
    a_part.three()
    b_part.two()
    down_part.last()
    up_part.last()
    a_part.four()
    b_part.three()
    (grad_down,) = finish(plan, order, [down_part], [[(0, D, 0, 0)]], [D])
    (grad_up,) = finish(plan, order, [up_part], [[(0, FF, 0, 0)]], [FF])
    b_part.four()
    query_out, passage_out = merged(out_own, after(out_back, b_part.out))
    query_grad, passage_grad = merged(gx_own, after(gx_back, b_part.out).astype(F32))
    a_part.last()
    b_part.last()
    qa, qb = split * 128, D - split * 128
    spans_a = [(0, D, 1, 0)] + [(D + j * qa, qa, 0, j * D) for j in range(3)]
    spans_b = [(j * qb, qb, 0, j * D + qa) for j in range(3)] + [(3 * qb, 128, 2, 0)]
    grad_qkv, grad_out, grad_vecs = finish(plan, order, [a_part, b_part], [spans_a, spans_b], [3 * D, D, 128])
    grad_vecs = jnp.swapaxes(grad_vecs[:, :, :12], 1, 2)
    return (
        query_out,
        passage_out,
        query_grad,
        passage_grad,
        query_loss,
        grad_qkv,
        grad_out,
        grad_up,
        grad_down,
        grad_vecs[:, :10],
        grad_vecs[:, 10:],
    )


def solution(mesh):
    plan = Plan(mesh.shape["dp"], mesh.shape["rep"])
    rows = P(("dp", "rep"), None, None)
    shards = P(None, "dp", None)
    lanes = P(None, None, "dp")
    return jax.shard_map(
        partial(on_device, plan),
        mesh=mesh,
        in_specs=(rows,) * 4 + (P(("dp", "rep"), None),) + (shards,) * 4 + (lanes,) * 2,
        out_specs=(rows,) * 4 + (P(("dp", "rep")),) + (shards,) * 4 + (lanes,) * 2,
        check_vma=False,
    )
```

```python
from functools import partial

import jax
import jax.numpy as jnp
from jax import lax
from jax.experimental import pallas as pl
from jax.experimental.pallas import tpu as pltpu
from jax.sharding import PartitionSpec as P

AXES = ("dp", "rep")
BF = jnp.bfloat16
F32 = jnp.float32
D = 768
FF = 3072
HEADS = 12
HEAD = 64
PAIRS = HEADS // 2
BLOCK = 128
TILE = 256
EPS = 1e-05
LOSS_WEIGHT = 32.0
MIB = 2**20
O_NEAR1 = "z2,both3"
O_NEAR3 = "p2"
O_X = 'z3'
O_D2 = "first"
O_D3 = "norm"
O_P2 = True
O_FCOST = 1.0
O_COT = 'norm'
O_COTD = "loss"
O_SPLIT = 4
O_GELU = 1
O_GX = 'u3'
O_BCOST = 4.0
O_TAIL = 0
O_OUT = "pick"
O_D2DN = 1
O_V1 = True
O_V2 = True
O_V3 = True
O_V4 = 0
O_V5 = True
O_V6 = False
AT_OUT = 3 * D
AT_VEC = 4 * D


def smem():
    return pl.BlockSpec(memory_space=pltpu.SMEM)


def vmem():
    return pl.BlockSpec(memory_space=pltpu.VMEM)


def cost(us):
    return pl.CostEstimate(flops=int(us * 1.0e9), transcendentals=0, bytes_accessed=int(us * 3.0e6))


def behind(us):
    return cost(O_BCOST * us)


def params(mib):
    return pltpu.CompilerParams(vmem_limit_bytes=mib * MIB)


def still(shape, at=None):
    index = at if at is not None else (0,) * len(shape)
    return pl.BlockSpec(shape, lambda i, *_: index, pipeline_mode=pl.Buffered(1))


def rows_at(width, rows=TILE):
    return pl.BlockSpec((rows, width), lambda i, *_: (i, 0))


def shape(dims, dtype):
    return jax.ShapeDtypeStruct(dims, dtype)


def later(dims, dtype):
    return shape(dims, dtype) if O_V2 else far(dims, dtype)


def far(dims, dtype):
    return pltpu.HBM(dims, dtype)


def stay(v):
    return pltpu.with_memory_space_constraint(v, pltpu.HBM)


def after(v, *others):
    return lax.optimization_barrier((v,) + others)[0]


class Order:
    def __init__(self, where):
        self.where = where

    def done(self, out):
        self.where = after(self.where, out)
        return out


def in_vmem(kernel, name, us, outs, *args, mib=24):
    return pl.pallas_call(
        kernel,
        out_shape=tuple(shape(*o) for o in outs),
        in_specs=[smem() if a.ndim == 1 else vmem() for a in args],
        out_specs=tuple(vmem() for _ in outs),
        compiler_params=params(mib),
        name=name,
        cost_estimate=cost(us),
    )(*args)


def wide(width, reps):
    unit = 128 * reps
    return -(-width // unit) * unit


def by_core(core, reps, width, move):
    if width % 128 == 0:
        move(pl.ds(pl.multiple_of(core * width, 128), width))
        return
    for c in range(reps):

        @pl.when(core == c)
        def one(c=c):
            move(slice(c * width, (c + 1) * width))


def halves(refs, core, source):
    width = refs[0].shape[1]
    for q, ref in enumerate(refs):

        def move(lanes, ref=ref):
            ref[...] = source[:, lanes]

        by_core(core ^ q, len(refs), width, move)


def send(v, pairs):
    return lax.ppermute(v, AXES, pairs)


class Plan:
    def __init__(self, n, reps):
        self.n, self.reps, self.depth = n, reps, n // 4

    def pairs(self, move):
        return [
            (d * self.reps + r, (d ^ move(r)[0]) * self.reps + (r ^ move(r)[1]))
            for d in range(self.n)
            for r in range(self.reps)
        ]

    def along(self, k):
        return self.pairs(lambda r: (4 * k, 0))

    def first(self):
        return self.pairs(lambda r: (1 + r % 2, 0))

    def second(self):
        return self.pairs(lambda r: (2 - r % 2, 0))

    def sibling(self, q):
        return self.pairs(lambda r: (0, q))


def assemble_kernel(depth, reps, width, where_ref, *refs):
    bufs, out = refs[: 2 * reps], refs[2 * reps]
    me, core = where_ref[0], where_ref[1]
    for q in range(reps):
        owner = core ^ q
        p1 = 1 + owner % 2
        p2 = 2 - owner % 2

        def move(lanes, q=q, p1=p1, p2=p2):
            for b in range(2):
                for f in range(2):
                    for k in range(depth):
                        dst = (me ^ (b * p2) ^ (f * p1)) ^ (4 * k)
                        out[pl.ds(dst, 1), :, lanes] = bufs[q * 2 + b][pl.ds(f * depth + k, 1)]

        by_core(owner, reps, width, move)


def shards_kernel(reps, where_ref, qkv_ref, out_ref, bias_ref, gain_ref, up_ref, down_ref, *rest):
    outs, full_ref = rest[:-1], rest[-1]
    core, tower = where_ref[1], where_ref[2]
    spare = full_ref.shape[2] - AT_VEC

    def turned(ref, t, at):
        rows = ref[t][0].astype(F32)
        i = lax.broadcasted_iota(jnp.int32, (rows.shape[0], spare), 0)
        j = lax.broadcasted_iota(jnp.int32, (rows.shape[0], spare), 1)
        return t_dot(rows.astype(BF), jnp.where(i + at == j, 1.0, 0.0).astype(BF))

    for n in range(2):
        t = pl.ds(tower if n == 0 else 1 - tower, 1)
        full_ref[:, :, :AT_OUT] = qkv_ref[t]
        full_ref[:, :, AT_OUT:AT_VEC] = out_ref[t]
        full_ref[0, :, AT_VEC:] = (turned(bias_ref, t, 0) + turned(gain_ref, t, bias_ref.shape[1])).astype(BF)
        for c, ref in enumerate((full_ref, up_ref, down_ref)):
            put = outs[2 * c + n]

            def move(lanes, ref=ref, put=put, t=t):
                put[...] = ref[:, :, lanes] if ref is full_ref else ref[t, :, lanes]

            by_core(core, reps, put.shape[2], move)


def shards_of(plan, order, w_qkv, w_out, biases, gains, w_up, w_down):
    reps = plan.reps
    one = wide(AT_VEC + 128, reps)
    outs = []
    for rows, width in ((w_qkv.shape[1], one), (w_up.shape[1], FF), (w_down.shape[1], D)):
        outs += [shape((1, rows, width // reps), BF)] * 2
    args = (w_qkv, w_out, biases, gains, w_up, w_down)
    got = pl.pallas_call(
        partial(shards_kernel, reps),
        grid=(1,),
        out_shape=tuple(outs),
        in_specs=[smem()] + [still(a.shape) for a in args],
        out_specs=[still(o.shape) for o in outs],
        scratch_shapes=[pltpu.VMEM((1, w_qkv.shape[1], one), BF)],
        compiler_params=params(24),
        name="shards",
        cost_estimate=cost(2),
    )(order.where, *[stay(a) for a in args])
    return order.done(got)


def join_kernel(where_ref, *refs):
    ins, out_ref = refs[:-1], refs[-1]
    at = 0
    for ref in ins:
        out_ref[at : at + ref.shape[0]] = ref[...]
        at += ref.shape[0]


def join(order, *bufs):
    total = sum(b.shape[0] for b in bufs)
    outs = (((total,) + bufs[0].shape[1:], bufs[0].dtype),)
    return order.done(in_vmem(join_kernel, "join", 0.5, outs, order.where, *bufs))[0]


def gather_line(plan, mine, other):
    got = [send(other if k % 2 else mine, plan.along(k)) for k in range(1, plan.depth)]
    return jnp.concatenate([mine] + got, 0)


def gather_steps(plan, both, *others):
    z = both
    k = 2
    while k < plan.depth:
        if others:
            z, others = after(z, *others), ()
        z = jnp.concatenate([z, send(z, plan.along(k))], 0)
        k *= 2
    return z


def gather_plane(plan, z, *others):
    near = jnp.concatenate([z, send(z, plan.first())], 0)
    if others:
        near = after(near, *others)
    return near, send(near, plan.second())


def gather_cores(plan, order, bufs):
    rows, width = bufs[0].shape[1:]
    bufs = list(bufs)
    for q in range(1, plan.reps):
        bufs += [send(b, plan.sibling(q)) for b in bufs[:2]]
    full = pl.pallas_call(
        partial(assemble_kernel, plan.depth, plan.reps, width),
        out_shape=jax.ShapeDtypeStruct((plan.n, rows, width * plan.reps), BF),
        in_specs=[smem()] + [vmem()] * len(bufs),
        out_specs=vmem(),
        compiler_params=params(24),
        name="assemble",
        cost_estimate=cost(2 * O_FCOST),
    )(order.where, *bufs)
    order.done(full)
    return full.reshape(plan.n * rows, width * plan.reps)


def add_kernel(depth, where_ref, a_hbm, b_ref, s_ref, k_ref, a_ref, sem):
    me, core = where_ref[0], where_ref[1]
    p1 = 1 + core % 2
    p2 = 2 - core % 2
    copies = []
    for j in range(4 * depth):
        at = me ^ ((1 - j // (2 * depth)) * p1) ^ ((1 - j // depth % 2) * p2) ^ (4 * (j % depth))
        copy = pltpu.make_async_copy(a_hbm.at[at], a_ref.at[j], sem.at[j])
        copy.start()
        copies.append((at, copy))
    for j, (at, copy) in enumerate(copies):
        copy.wait()
        o_ref, to = (s_ref, j) if j < 2 * depth else (k_ref, j - 2 * depth)
        o_ref[to] = (a_ref[j].astype(F32) + b_ref[at].astype(F32)).astype(BF)


def add_kernel2(depth, where_ref, a_ref, b_ref, s_ref, k_ref):
    me, core = where_ref[0], where_ref[1]
    p1 = 1 + core % 2
    p2 = 2 - core % 2
    for j in range(4 * depth):
        at = me ^ ((1 - j // (2 * depth)) * p1) ^ ((1 - j // depth % 2) * p2) ^ (4 * (j % depth))
        o_ref, to = (s_ref, j) if j < 2 * depth else (k_ref, j - 2 * depth)
        o_ref[to] = (a_ref[at].astype(F32) + b_ref[at].astype(F32)).astype(BF)


def two_kernel(where_ref, k_ref, r_ref, s_ref, o_ref):
    q = s_ref.shape[0]
    for j in range(2 * q):
        total = (k_ref[j].astype(F32) + r_ref[j].astype(F32)).astype(BF)
        if j < q:
            s_ref[j] = total
        else:
            o_ref[j - q] = total


def line_kernel(where_ref, k_ref, r_ref, s_ref, o_ref):
    half = o_ref.shape[0]
    for j in range(2 * half):
        total = (k_ref[j].astype(F32) + r_ref[j].astype(F32)).astype(BF)
        if j < half:
            o_ref[j] = total
        else:
            s_ref[j - half] = total


def last_kernel(where_ref, own_ref, got_ref, out):
    tower = where_ref[2]
    out[pl.ds(tower, 1)] = own_ref[...]
    out[pl.ds(1 - tower, 1)] = got_ref[...]


def plus(a, b):
    return (a.astype(F32) + b.astype(F32)).astype(BF)


def send_cut(v, pairs):
    if O_D2DN == 1:
        return send(v, pairs)
    n = v.shape[0] // O_D2DN
    return jnp.concatenate([send(v[i * n : (i + 1) * n], pairs) for i in range(O_D2DN)], 0)


class Scatter:
    def __init__(self, plan, order, parts, rows):
        self.plan, self.order, self.rows = plan, order, rows
        self.width = parts[0].shape[1]
        parts = [p.reshape(plan.n, rows, self.width) for p in parts]
        self.own = parts[0]
        got = [send_cut(parts[q], plan.sibling(q)) for q in range(1, plan.reps)]
        self.rest = got[0]
        for o in got[1:]:
            self.rest = plus(self.rest, o)

    def run(self, kernel, name, us, outs, *args):
        return self.order.done(in_vmem(kernel, name, us, outs, self.order.where, *args))

    def one(self):
        plan = self.plan
        n = plan.n
        whole = (n, self.rows, self.width)
        half = shape((n // 2, self.rows, self.width), BF)
        if O_V2:
            hs, self.hk = self.order.done(
                pl.pallas_call(
                    partial(add_kernel2, plan.depth),
                    out_shape=(half, half),
                    in_specs=[smem(), vmem(), vmem()],
                    out_specs=(vmem(), vmem()),
                    compiler_params=params(24),
                    name="pick_add",
                    cost_estimate=behind(3),
                )(self.order.where, self.own, self.rest)
            )
            self.r1 = send(hs, plan.first())
            return
        hs, self.hk = self.order.done(
            pl.pallas_call(
                partial(add_kernel, plan.depth),
                out_shape=(half, half),
                in_specs=[smem(), pl.BlockSpec(memory_space=pl.ANY), vmem()],
                out_specs=(vmem(), vmem()),
                scratch_shapes=[pltpu.VMEM(whole, BF), pltpu.SemaphoreType.DMA((n,))],
                compiler_params=params(24),
                name="pick_add",
                cost_estimate=behind(3),
            )(self.order.where, stay(self.own), self.rest)
        )
        self.r1 = send(hs, plan.first())

    def two(self):
        quarter = ((self.plan.n // 4, self.rows, self.width), BF)
        ks, self.kk = self.run(two_kernel, "add_two", 1, (quarter, quarter), self.hk, self.r1)
        self.r2 = send(ks, self.plan.second())

    def line(self):
        n = self.kk.shape[0] // 2
        half = ((n, self.rows, self.width), BF)
        out, self.kk = self.run(line_kernel, "add_line", 1, (half, half), self.kk, self.r2)
        self.r2 = send(out, self.plan.along(n))
        return out

    def three(self):
        self.line()

    def four(self):
        while self.kk.shape[0] > 1:
            self.out = self.line()

    def last(self):
        plan = self.plan
        outs = (((2, self.rows, self.width), BF),)
        (pair,) = self.run(last_kernel, "add_last", 1, outs, self.kk, self.r2)
        self.ends = [pair] + [send(pair, plan.sibling(q)) for q in range(1, plan.reps)]


def finish_kernel(reps, spans, vec, where_ref, *refs):
    chunks = len(spans)
    ins, outs = refs[: chunks * reps], refs[chunks * reps :]
    core = where_ref[1]
    for c in range(chunks):
        parts = ins[c * reps : (c + 1) * reps]
        width = parts[0].shape[2]
        for q in range(reps):
            for mine in range(reps):

                @pl.when((core ^ q) == mine)
                def copy(c=c, parts=parts, q=q, mine=mine):
                    for at, size, out, to in spans[c]:
                        low, high = max(at, mine * width), min(at + size, (mine + 1) * width)
                        if low >= high:
                            continue
                        lanes = slice(low - mine * width, high - mine * width)
                        if out == vec:
                            turn(parts[q], lanes, low - at, outs[out], outs[out + 1])
                        else:
                            outs[out][:, :, to + low - at : to + high - at] = parts[q][:, :, lanes].astype(F32)


def turn(part_ref, lanes, at, bias_ref, gain_ref):
    for t in range(2):
        columns = part_ref[t, :, lanes]
        for ref, start in ((bias_ref, 0), (gain_ref, bias_ref.shape[1])):
            n = ref.shape[1]
            i = lax.broadcasted_iota(jnp.int32, (n, columns.shape[1]), 0)
            j = lax.broadcasted_iota(jnp.int32, (n, columns.shape[1]), 1)
            ref[t] = dot_t(jnp.where(i + start == j + at, 1.0, 0.0).astype(BF), columns)


def finish(plan, order, chunks, spans, shapes, vec=-1):
    outs = tuple((s, F32) for s in shapes)
    args = [p for c in chunks for p in c.ends]
    kernel = partial(finish_kernel, plan.reps, spans, vec)
    return order.done(in_vmem(kernel, "finish", 2, outs, order.where, *args))


def dot(a, b):
    return jnp.dot(a, b, preferred_element_type=F32)


def dot_t(a, b):
    return lax.dot_general(a, b, (((1,), (1,)), ((), ())), preferred_element_type=F32)


def t_dot(a, b):
    return lax.dot_general(a, b, (((0,), (0,)), ((), ())), preferred_element_type=F32)


def normalize(h):
    center = h - jnp.mean(h, -1, keepdims=True)
    rstd = lax.rsqrt(jnp.mean(center * center, -1, keepdims=True) + EPS)
    return center * rstd, rstd


def lane_masks():
    lane = lax.broadcasted_iota(jnp.int32, (1, 2 * HEAD), 1)
    low = (lane < HEAD).astype(F32).astype(BF)
    return low, (1.0 - low.astype(F32)).astype(BF)


def attend_kernel(part, where_ref, x_ref, w_ref, *rest):
    proj_ref, probs_ref, attn_ref, hat_ref, rstd_ref, norm_ref, vec_ref, cls_ref, bias_ref = rest[-9:]

    @pl.when(pl.program_id(0) == 0)
    def prepare():
        vec_ref[...] = jnp.transpose(w_ref[:, AT_VEC : AT_VEC + 128].astype(F32))
        span = where_ref[3]
        row = lax.broadcasted_iota(jnp.int32, (BLOCK, 2 * BLOCK), 0)
        col = lax.broadcasted_iota(jnp.int32, (BLOCK, 2 * BLOCK), 1) % BLOCK
        bias_ref[...] = jnp.where((row ^ col) < span, 0.0, -1e30)

    x = x_ref[...]
    for j in range(3):
        part = dot(x, w_ref[:, j * D : (j + 1) * D])
        if j != 1:
            part = part + vec_ref[j // 2 : j // 2 + 1, :]
        proj_ref[:, j * D : (j + 1) * D] = part.astype(BF)
    low, high = lane_masks()
    bias = bias_ref[...]
    for blk in range(TILE // BLOCK):
        rows = slice(blk * BLOCK, (blk + 1) * BLOCK)
        for pair in range(PAIRS):
            lanes = slice(pair * 128, (pair + 1) * 128)
            q = proj_ref[rows, lanes]
            k = proj_ref[rows, D + pair * 128 : D + (pair + 1) * 128]
            v = proj_ref[rows, 2 * D + pair * 128 : 2 * D + (pair + 1) * 128]
            s = dot_t(k, jnp.concatenate([q * low, q * high], 0)) * HEAD**-0.5 + bias
            e = jnp.exp(s - jnp.max(s, 0, keepdims=True))
            p = (e * (1.0 / jnp.sum(e, 0, keepdims=True))).astype(BF)
            probs_ref[blk, pair] = p
            tall = jnp.concatenate([p[:, :BLOCK], p[:, BLOCK:]], 0)
            attn_ref[rows, lanes] = t_dot(tall, jnp.concatenate([v * low, v * high], 0)).astype(BF)
    hidden = x.astype(F32) + (dot(attn_ref[...], w_ref[:, AT_OUT:AT_VEC]) + vec_ref[2:3, :])
    hat, rstd = normalize(hidden)
    hat_ref[...] = hat
    rstd_ref[...] = rstd
    norm = hat * vec_ref[10:11, :] + vec_ref[3:4, :]
    norm_ref[...] = norm.astype(BF)
    for j in range(TILE // 32):
        cls_ref[j : j + 1, :] = norm[32 * j : 32 * j + 1, :]


def attend(order, x, w_one, part, before=()):
    rows = 2 * x.shape[0]
    per = TILE // BLOCK
    steps = rows // TILE // 2
    first = part * steps

    def here(width):
        return pl.BlockSpec((TILE, width), lambda i: (i + first, 0))

    return pl.pallas_call(
        partial(attend_kernel, part),
        grid=(steps,),
        out_shape=(
            far((rows, 3 * D), BF),
            far((rows // BLOCK, PAIRS, BLOCK, 2 * BLOCK), BF),
            far((rows, D), BF),
            far((rows, D), F32),
            far((rows, 1), F32),
            far((rows, D), BF),
            shape((128, D), F32),
            shape((rows // 64, D), F32),
        ),
        in_specs=[smem(), rows_at(D), vmem()] + [pl.BlockSpec(memory_space=pl.ANY)] * len(before),
        out_specs=[
            here(3 * D),
            pl.BlockSpec((per, PAIRS, BLOCK, 2 * BLOCK), lambda i: (i + first, 0, 0, 0)),
            here(D),
            here(D),
            here(1),
            here(D),
            still((128, D)),
            rows_at(D, TILE // 32),
        ],
        scratch_shapes=[pltpu.VMEM((BLOCK, 2 * BLOCK), F32)],
        input_output_aliases={3 + j: j for j in range(len(before))},
        compiler_params=params(24),
        name="attend",
        cost_estimate=cost(7 * O_FCOST),
    )(order.where, x, w_one, *[stay(b) for b in before])


def gelu_pair(u):
    phi = 0.5 + 0.5 * lax.erf(u * 2**-0.5)
    if O_V4 == 1:
        return u * phi, phi + u * jnp.exp2(u * u * (-0.5 / 0.6931471805599453) - 1.3257480647361595)
    if O_V4 == 2:
        v = u.astype(BF)
        return u * phi, phi.astype(BF) + v * jnp.exp((v * v) * jnp.asarray(-0.5, BF)) * jnp.asarray((2 * jnp.pi) ** -0.5, BF)
    return u * phi, phi + u * (jnp.exp(-0.5 * u * u) * (2 * jnp.pi) ** -0.5)


def up_kernel(first, where_ref, norm_ref, w_ref, vec_ref, *rest):
    act_ref, slope_ref = rest[-2:]
    bias = vec_ref[pl.ds(4 + first + pl.program_id(0), 1), :]
    for m in range(0, norm_ref.shape[0], TILE):
        rows = slice(m, m + TILE)
        act, slope = gelu_pair(dot(norm_ref[rows, :], w_ref[...]) + bias)
        act_ref[rows, :] = act.astype(BF)
        slope_ref[rows, :] = slope.astype(BF)


def up(order, norm, w_up, vec, part, before=()):
    rows = norm.shape[0]
    steps = FF // D // 2
    first = part * steps
    col = pl.BlockSpec((rows, D), lambda i: (0, i + first))
    return pl.pallas_call(
        partial(up_kernel, first),
        grid=(steps,),
        out_shape=(far((rows, FF), BF), far((rows, FF), BF)),
        in_specs=[
            smem(),
            still(norm.shape),
            pl.BlockSpec((D, D), lambda i: (0, i + first)),
            still(vec.shape),
        ]
        + [pl.BlockSpec(memory_space=pl.ANY)] * len(before),
        out_specs=[col, col],
        input_output_aliases={4 + j: j for j in range(len(before))},
        compiler_params=params(24),
        name="up",
        cost_estimate=cost(8 * O_FCOST),
    )(order.where, norm, w_up, vec, *[stay(b) for b in before])


def down_kernel(where_ref, act_ref, w_ref, hat_ref, vec_ref, own_ref, far_ref, hat2_ref, rstd2_ref):
    normed = hat_ref[...] * vec_ref[10:11, :] + vec_ref[3:4, :]
    second = normed + (dot(act_ref[...], w_ref[...]) + vec_ref[8:9, :])
    hat, rstd = normalize(second)
    hat2_ref[...] = hat
    rstd2_ref[...] = rstd
    out = (hat * vec_ref[11:12, :] + vec_ref[9:10, :]).astype(BF)
    half = pl.num_programs(0) // 2

    @pl.when(pl.program_id(0) < half)
    def near():
        own_ref[...] = out

    @pl.when(pl.program_id(0) >= half)
    def away():
        far_ref[...] = out


def down(order, act, w_down, hat, vec):
    rows = act.shape[0]
    half = rows // TILE // 2
    near = pl.BlockSpec((TILE, D), lambda i: (jnp.minimum(i, half - 1), 0))
    away = pl.BlockSpec((TILE, D), lambda i: (jnp.maximum(i - half, 0), 0))
    return pl.pallas_call(
        down_kernel,
        grid=(rows // TILE,),
        out_shape=(far((rows // 2, D), BF), shape((rows // 2, D), BF), shape((rows, D), F32), shape((rows, 1), F32)),
        in_specs=[smem(), rows_at(FF), vmem(), rows_at(D), still(vec.shape)],
        out_specs=[near, away, rows_at(D), rows_at(1)],
        compiler_params=params(24),
        name="down",
        cost_estimate=cost(8 * O_FCOST),
    )(order.where, stay(act), w_down, stay(hat), vec)


def first_kernel(where_ref, a_ref, b_ref, up_ref, down_ref, vec_ref, marks_ref, msg_ref):
    norm = jnp.concatenate([a_ref[...], b_ref[...]], 0)
    second = norm + vec_ref[8:9, :]
    wide = norm.astype(BF)
    for j in range(FF // D):
        u = dot(wide, up_ref[:, j * D : (j + 1) * D]) + vec_ref[4 + j : 5 + j, :]
        second = second + dot(gelu_pair(u)[0].astype(BF), down_ref[j * D : (j + 1) * D, :])
    hat, _ = normalize(second)
    msg_ref[:, :D] = (hat * vec_ref[11:12, :] + vec_ref[9:10, :]).astype(BF)
    marks = marks_ref[...].astype(F32)
    pad = jnp.zeros((32 - marks.shape[0], marks.shape[1]), F32)
    msg_ref[:, D:] = jnp.concatenate([marks, pad], 0).astype(BF)


def first_rows(order, a, b, w_up, w_down, vec, positives):
    outs = (((32, D + positives.shape[1]), BF),)
    return order.done(in_vmem(first_kernel, "first_rows", 4, outs, order.where, a, b, w_up, w_down, vec, positives))[0]


def pack_kernel(per, where_ref, *refs):
    msgs, out_ref = refs[:-1], refs[-1]
    queries = per * 4
    pick_row = lax.broadcasted_iota(jnp.int32, (16, 32), 0)
    pick_col = lax.broadcasted_iota(jnp.int32, (16, 32), 1)
    pick = jnp.where((pick_col == pick_row * (32 // (2 * per))) & (pick_row < 2 * per), 1.0, 0.0).astype(BF)
    for n in range(len(msgs) // 2):
        for tower in range(2):

            @pl.when(where_ref[2] == tower)
            def put(n=n, tower=tower):
                zero, one = msgs[2 * n + tower], msgs[2 * n + 1 - tower]
                out_ref[n, :32, :D] = zero[:, :D]
                out_ref[n, :queries, D:] = zero[:queries, D:]
                out_ref[n, queries:32, D:] = one[:queries, D:]
                out_ref[n, 32:, :D] = dot(pick, one[:, :D]).astype(BF)
                out_ref[n, 32:, D:] = jnp.zeros((16, out_ref.shape[2] - D), BF)


def contrast_kernel(reps, depth, per, where_ref, *refs):
    parts, loss_ref, grad_ref, acc_ref = refs[:reps], refs[reps], refs[reps + 1], refs[reps + 2]
    me, core, tower = where_ref[0], where_ref[1], where_ref[2]
    pieces = parts[0].shape[0]
    passages = parts[0].shape[2] - D
    cls_p = jnp.concatenate([part[:, 32:, :D].reshape(pieces * 16, D) for part in parts], 0)
    cols = cls_p.shape[0]
    col = lax.broadcasted_iota(jnp.int32, (passages, cols), 1)
    row = lax.broadcasted_iota(jnp.int32, (passages, cols), 0)
    j, slot = col // 16, col % 16
    base = (me | 4) ^ (8 * (j % (depth // 2))) ^ ((j // (depth // 2)) % 4)
    owner = jnp.where(slot < per, base, base ^ 4)
    passage = (owner * reps + (core ^ (j // (2 * depth)))) * per + slot % per
    pick = jnp.where((row == passage) & (slot < 2 * per), 1.0, 0.0).astype(BF)
    valid = lax.broadcasted_iota(jnp.int32, (1, cols), 1) % 16 < 2 * per
    acc_ref[...] = jnp.zeros_like(acc_ref)
    group = min(8, pieces)
    for q, part in enumerate(parts):
        for at in range(0, pieces, group):
            cls_q = part[at : at + group, :32, :D].reshape(group * 32, D)
            marks = dot(part[at : at + group, :32, D:].reshape(group * 32, passages), pick)
            raw = jnp.where(valid, dot_t(cls_q, cls_p) * D**-0.5, -1e30)
            e = jnp.exp(raw - jnp.max(raw, -1, keepdims=True))
            total = jnp.sum(e, -1, keepdims=True)
            me_ = marks * e
            marked = jnp.sum(me_, -1, keepdims=True)
            grad = (LOSS_WEIGHT * (e / total - me_ / marked)).astype(BF)
            acc_ref[...] += t_dot(grad[:, :128], cls_q)[:16] * D**-0.5
            if q == 0 and at == 0:
                loss_ref[...] = (jnp.log(total) - jnp.log(marked))[:32]
                grad_ref[...] = dot(grad[:32], cls_p) * D**-0.5

    @pl.when(tower == 1)
    def passages_own():
        grad_ref[...] = jnp.zeros_like(grad_ref)
        for s in range(2 * per):
            at = s * (32 // (2 * per))
            grad_ref[at : at + 1, :] = acc_ref[s : s + 1, :]


class Contrast:
    def __init__(self, plan, order, msg, queries):
        self.plan, self.order, self.queries = plan, order, queries
        self.msgs = [msg] + [send(msg, plan.along(k)) for k in range(1, plan.depth)]

    def pack(self):
        plan = self.plan
        outs = (((plan.depth // 2, 48, self.msgs[0].shape[1]), BF),)
        kernel = partial(pack_kernel, self.queries // 4)
        (buf,) = self.order.done(in_vmem(kernel, "pack", 1, outs, self.order.where, *self.msgs))
        self.bufs = [buf] + [send(buf, plan.pairs(lambda r, m=m: (m, 0))) for m in range(1, 4)]

    def join(self):
        plan = self.plan
        buf = join(self.order, *self.bufs)
        self.parts = [buf] + [send(buf, plan.sibling(s)) for s in range(1, plan.reps)]

    def loss(self):
        plan, order = self.plan, self.order
        loss, grad = order.done(
            pl.pallas_call(
                partial(contrast_kernel, plan.reps, plan.depth, self.queries // 4),
                out_shape=(shape((32, 1), F32), shape((32, D), F32)),
                in_specs=[smem()] + [vmem()] * plan.reps,
                out_specs=(vmem(), vmem()),
                scratch_shapes=[pltpu.VMEM((16, D), F32)],
                compiler_params=params(40),
                name="contrast",
                cost_estimate=cost(2),
            )(order.where, *self.parts)
        )
        at = order.where[2] * self.queries
        return lax.dynamic_slice(loss, (at, 0), (self.queries, 1))[:, 0], grad


def norm_back(grad, hat, rstd, gain):
    scaled = grad * gain
    a = jnp.mean(scaled, -1, keepdims=True)
    b = jnp.mean(scaled * hat, -1, keepdims=True)
    return rstd * (scaled - a - hat * b)


def col_sum(v):
    return jnp.sum(v, 0, keepdims=True)


def top_kernel(
    where_ref, cot_ref, cls_ref, hat_ref, rstd_ref, vec_ref, act_ref, second_ref, gs_ref, sums_ref, *rest
):
    parts, full_ref = rest[:-1], rest[-1]

    @pl.when(pl.program_id(0) == 0)
    def norm():
        groups = TILE // 32
        at_first = lax.broadcasted_iota(jnp.int32, (groups, 32, D), 1) == 0
        sums_ref[...] = jnp.zeros_like(sums_ref)
        for m in range(0, cot_ref.shape[0], TILE):
            rows = slice(m, m + TILE)
            cls = cls_ref[m // 32 : (m + TILE) // 32, :].reshape(groups, 1, D)
            dout = cot_ref[rows, :].astype(F32) + jnp.where(at_first, cls, 0.0).reshape(TILE, D)
            hat = hat_ref[rows, :]
            grad = norm_back(dout, hat, rstd_ref[rows, :], vec_ref[11:12, :])
            second_ref[rows, :] = grad
            gs = grad.astype(BF)
            gs_ref[rows, :] = gs
            sums_ref[0:1, :] += col_sum(gs.astype(F32))
            sums_ref[1:2, :] += col_sum(dout)
            sums_ref[2:3, :] += col_sum(dout * hat)

    full_ref[...] = t_dot(act_ref[...], gs_ref[...]).astype(BF)
    halves(parts, where_ref[1], full_ref)


def top(plan, order, cot, cls_grad, hat2, rstd2, vec, act):
    rows = cot.shape[0]
    part = D // plan.reps
    second, gs, sums, *parts = pl.pallas_call(
        top_kernel,
        grid=(FF // D,),
        out_shape=(shape((rows, D), F32) if O_V6 else far((rows, D), F32), shape((rows, D), BF), shape((8, D), F32))
        + (later((FF, part), BF),) * plan.reps,
        in_specs=[
            smem(),
            vmem(),
            still(cls_grad.shape),
            vmem(),
            vmem(),
            still(vec.shape),
            pl.BlockSpec((rows, D), lambda i: (0, i)),
        ],
        out_specs=[still((rows, D)), still((rows, D)), still((8, D))] + [rows_at(part, D)] * plan.reps,
        scratch_shapes=[pltpu.VMEM((D, D), BF)],
        compiler_params=params(28),
        name="top",
        cost_estimate=behind(11),
    )(order.where, cot, cls_grad, hat2, rstd2, vec, stay(act))
    return second, gs, sums, parts


def gelu_back_kernel(reps, column, where_ref, gs_ref, w_ref, slope_ref, norm_ref, up_ref, acc_ref, sums_ref, *rest):
    parts, gu_ref = rest[:-1], rest[-1]
    i = pl.program_id(0)
    total = jnp.zeros((1, D), F32)
    for m in range(0, gs_ref.shape[0], TILE):
        rows = slice(m, m + TILE)
        gu = (dot_t(gs_ref[rows, :], w_ref[...]) * slope_ref[rows, :].astype(F32)).astype(BF)
        gu_ref[rows, :] = gu
        total = total + col_sum(gu.astype(F32))
    sums_ref[pl.ds(column(i, where_ref), 1), :] = total
    grad = t_dot(norm_ref[...], gu_ref[...]).astype(BF)
    per = (FF // D) // reps
    for q in range(reps):

        @pl.when(i // per == reps - 1 - q)
        def put(q=q):
            parts[q][...] = grad

    @pl.when(i == 0)
    def start():
        acc_ref[...] = dot_t(gu_ref[...], up_ref[...])

    @pl.when(i > 0)
    def add():
        acc_ref[...] += dot_t(gu_ref[...], up_ref[...])


def gelu_back(plan, order, gs, w_down, slope, norm, w_up):
    rows = gs.shape[0]
    reps = plan.reps
    per = (FF // D) // reps

    def column(i, table):
        return (table[1] ^ (reps - 1 - i // per)) * per + i % per

    def held(q):
        return pl.BlockSpec((D, D), lambda i, table: (0, jnp.clip(i - (reps - 1 - q) * per, 0, per - 1)))

    acc, sums, *parts = pl.pallas_call(
        partial(gelu_back_kernel, reps, column),
        out_shape=(shape((rows, D), F32), shape((8, D), F32)) + (later((D, FF // reps), BF),) * reps,
        grid_spec=pltpu.PrefetchScalarGridSpec(
            num_scalar_prefetch=1,
            grid=(FF // D,),
            in_specs=[
                vmem() if O_V5 else still(gs.shape),
                pl.BlockSpec((D, D), lambda i, table: (column(i, table), 0)),
                pl.BlockSpec((rows, D), lambda i, table: (0, column(i, table))),
                vmem() if O_V5 else still(norm.shape),
                pl.BlockSpec((D, D), lambda i, table: (0, column(i, table))),
            ],
            out_specs=[still((rows, D)), still((8, D))] + [held(q) for q in range(reps)],
            scratch_shapes=[pltpu.VMEM((rows, D), BF)],
        ),
        compiler_params=params(28),
        name="gelu_back",
        cost_estimate=behind(20),
    )(order.where, gs, stay(w_down), stay(slope), norm, stay(w_up))
    return acc, sums, parts


def hidden_back_kernel(
    where_ref, acc_ref, second_ref, hat_ref, rstd_ref, w_ref, vec_ref, hidden_ref, go_ref, ga_ref, sums_ref
):
    @pl.when(pl.program_id(0) == 0)
    def clear():
        sums_ref[...] = jnp.zeros_like(sums_ref)

    grad = acc_ref[...] + second_ref[...]
    hat = hat_ref[...]
    hidden = norm_back(grad, hat, rstd_ref[...], vec_ref[10:11, :])
    if not O_V3:
        hidden_ref[...] = hidden
    go = hidden.astype(BF)
    go_ref[...] = go
    sums_ref[0:1, :] += col_sum(go.astype(F32))
    sums_ref[1:2, :] += col_sum(grad)
    sums_ref[2:3, :] += col_sum(grad * hat)
    ga_ref[...] = dot_t(go, w_ref[...]).astype(BF)


def hidden_back(order, acc, second, hat, rstd, w_one, vec):
    rows = acc.shape[0]
    return pl.pallas_call(
        hidden_back_kernel,
        grid=(rows // TILE,),
        out_shape=((shape((8, D), F32) if O_V3 else far((rows, D), F32)), shape((rows, D), BF), shape((rows, D), BF), shape((8, D), F32)),
        in_specs=[smem()]
        + [rows_at(D)] * 3
        + [rows_at(1), still((D, D), (0, AT_OUT // D)), still(vec.shape)],
        out_specs=[still((8, D)) if O_V3 else rows_at(D), rows_at(D), rows_at(D), still((8, D))],
        compiler_params=params(20),
        name="hidden_back",
        cost_estimate=behind(5),
    )(order.where, acc, second if O_V6 else stay(second), stay(hat), stay(rstd), stay(w_one), vec)


def gelu_back2_kernel(reps, column, where_ref, gs_ref, w_ref, slope_ref, norm_ref, gu_ref, sums_ref, *parts):
    i = pl.program_id(0)
    total = jnp.zeros((1, D), F32)
    for m in range(0, gs_ref.shape[0], TILE):
        rows = slice(m, m + TILE)
        gu = (dot_t(gs_ref[rows, :], w_ref[...]) * slope_ref[rows, :].astype(F32)).astype(BF)
        gu_ref[rows, :] = gu
        total = total + col_sum(gu.astype(F32))
    sums_ref[pl.ds(column(i, where_ref), 1), :] = total
    grad = t_dot(norm_ref[...], gu_ref[...]).astype(BF)
    per = (FF // D) // reps
    for q in range(reps):

        @pl.when(i // per == reps - 1 - q)
        def put(q=q):
            parts[q][...] = grad


def gelu_back2(plan, order, gs, w_down, slope, norm):
    rows = gs.shape[0]
    reps = plan.reps
    per = (FF // D) // reps

    def column(i, table):
        return (table[1] ^ (reps - 1 - i // per)) * per + i % per

    def held(q):
        return pl.BlockSpec((D, D), lambda i, table: (0, jnp.clip(i - (reps - 1 - q) * per, 0, per - 1)))

    col = pl.BlockSpec((rows, D), lambda i, table: (0, column(i, table)))
    gu, sums, *parts = pl.pallas_call(
        partial(gelu_back2_kernel, reps, column),
        out_shape=(shape((rows, FF), BF), shape((8, D), F32)) + (later((D, FF // reps), BF),) * reps,
        grid_spec=pltpu.PrefetchScalarGridSpec(
            num_scalar_prefetch=1,
            grid=(FF // D,),
            in_specs=[
                still(gs.shape),
                pl.BlockSpec((D, D), lambda i, table: (column(i, table), 0)),
                col,
                still(norm.shape),
            ],
            out_specs=[col, still((8, D))] + [held(q) for q in range(reps)],
        ),
        compiler_params=params(28),
        name="gelu_back",
        cost_estimate=behind(14),
    )(order.where, gs, stay(w_down), stay(slope), norm)
    return gu, sums, parts


def hidden_back2_kernel(
    where_ref, gu_ref, up_ref, second_ref, hat_ref, rstd_ref, w_ref, vec_ref, hidden_ref, go_ref, ga_ref, sums_ref
):
    @pl.when(pl.program_id(0) == 0)
    def clear():
        sums_ref[...] = jnp.zeros_like(sums_ref)

    grad = dot_t(gu_ref[...], up_ref[...]) + second_ref[...]
    hat = hat_ref[...]
    hidden = norm_back(grad, hat, rstd_ref[...], vec_ref[10:11, :])
    if not O_V3:
        hidden_ref[...] = hidden
    go = hidden.astype(BF)
    go_ref[...] = go
    sums_ref[0:1, :] += col_sum(go.astype(F32))
    sums_ref[1:2, :] += col_sum(grad)
    sums_ref[2:3, :] += col_sum(grad * hat)
    ga_ref[...] = dot_t(go, w_ref[...]).astype(BF)


def hidden_back2(order, gu, w_up, second, hat, rstd, w_one, vec):
    rows = gu.shape[0]
    return pl.pallas_call(
        hidden_back2_kernel,
        grid=(rows // TILE,),
        out_shape=((shape((8, D), F32) if O_V3 else far((rows, D), F32)), shape((rows, D), BF), shape((rows, D), BF), shape((8, D), F32)),
        in_specs=[smem(), rows_at(FF), vmem()]
        + [rows_at(D)] * 2
        + [rows_at(1), still((D, D), (0, AT_OUT // D)), still(vec.shape)],
        out_specs=[still((8, D)) if O_V3 else rows_at(D), rows_at(D), rows_at(D), still((8, D))],
        compiler_params=params(24),
        name="hidden_back",
        cost_estimate=behind(11),
    )(order.where, gu, w_up, stay(second), stay(hat), stay(rstd), stay(w_one), vec)


def pair_back(pair, block, rows, ga_ref, proj_ref, probs_ref, low, high):
    q = proj_ref[rows, pair * 128 : (pair + 1) * 128]
    k = proj_ref[rows, D + pair * 128 : D + (pair + 1) * 128]
    v = proj_ref[rows, 2 * D + pair * 128 : 2 * D + (pair + 1) * 128]
    a = ga_ref[rows, pair * 128 : (pair + 1) * 128]
    a2 = jnp.concatenate([a * low, a * high], 0)
    q2 = jnp.concatenate([q * low, q * high], 0)
    k2 = jnp.concatenate([k * low, k * high], 0)
    p = probs_ref[block, pair]
    dp = dot_t(v, a2)
    pf = p.astype(F32)
    ds = (pf * (dp - jnp.sum(pf * dp, 0, keepdims=True)) * HEAD**-0.5).astype(BF)
    tall = jnp.concatenate([ds[:, :BLOCK], ds[:, BLOCK:]], 0)
    return t_dot(tall, k2).astype(BF), dot(ds, q2).astype(BF), dot(p, a2).astype(BF)


def heads_back(first, count, at, ga_ref, proj_ref, probs_ref, gp_ref):
    low, high = lane_masks()
    for block in range(TILE // BLOCK):
        rows = slice(block * BLOCK, (block + 1) * BLOCK)
        to = pl.ds(pl.multiple_of(at + block * BLOCK, BLOCK), BLOCK)
        for j in range(count):
            three = pair_back(first + j, block, rows, ga_ref, proj_ref, probs_ref, low, high)
            for n, grad in enumerate(three):
                lane = (n * count + j) * 128
                gp_ref[to, lane : lane + 128] = grad


def attend_back_kernel(first, count, where_ref, ga_ref, proj_ref, probs_ref, gp_ref):
    heads_back(first, count, 0, ga_ref, proj_ref, probs_ref, gp_ref)


def tile_specs(first):
    per = TILE // BLOCK
    return [
        pl.BlockSpec((TILE, D), lambda i: (i + first, 0)),
        pl.BlockSpec((TILE, 3 * D), lambda i: (i + first, 0)),
        pl.BlockSpec((per, PAIRS, BLOCK, 2 * BLOCK), lambda i: (i + first, 0, 0, 0)),
    ]


def attend_back(order, first, count, ga, proj, probs, rows):
    wide = 3 * count * 128
    return pl.pallas_call(
        partial(attend_back_kernel, first, count),
        grid=(rows // TILE,),
        out_shape=shape((rows, wide), BF),
        in_specs=[smem()] + tile_specs(0),
        out_specs=rows_at(wide),
        compiler_params=params(20),
        name="attend_back",
        cost_estimate=behind(10 * count * rows // 4096),
    )(order.where, ga, stay(proj), stay(probs))


def both_rows(x_ref, y_ref, near_ref, far_ref):
    return (t_dot(x_ref[...], near_ref[...]) + t_dot(y_ref[...], far_ref[...])).astype(BF)


def first_weights_kernel(where_ref, x_ref, y_ref, near_ref, far_ref, attn_ref, go_ref, *rest):
    parts, full_ref = rest[:-1], rest[-1]
    full_ref[:, :D] = t_dot(attn_ref[...], go_ref[...]).astype(BF)
    end = D + near_ref.shape[1]
    full_ref[:, D:end] = both_rows(x_ref, y_ref, near_ref, far_ref)
    if end < full_ref.shape[1]:
        full_ref[:, end:] = jnp.zeros((D, full_ref.shape[1] - end), BF)
    halves(parts, where_ref[1], full_ref)


def last_weights_kernel(
    count, where_ref, x_ref, y_ref, near_ref, far_ref, first_near_ref, first_far_ref, up_ref, top_ref, hidden_ref, *rest
):
    parts, full_ref, lines_ref = rest[:-2], rest[-2], rest[-1]
    part = D - count * 128
    wide = count * 128
    full_ref[:, : 3 * part] = both_rows(x_ref, y_ref, near_ref, far_ref)

    def sums(j, width, a_ref, b_ref):
        lanes = slice(j * width, (j + 1) * width)
        return col_sum(a_ref[:, lanes].astype(F32)) + col_sum(b_ref[:, lanes].astype(F32))

    lines_ref[...] = jnp.zeros_like(lines_ref)
    for n, j in ((0, 0), (1, 2)):
        lines_ref[n : n + 1, :wide] = sums(j, wide, first_near_ref, first_far_ref)
        lines_ref[n : n + 1, wide:] = sums(j, part, near_ref, far_ref)
    lines_ref[2:4, :] = hidden_ref[0:2, :]
    lines_ref[4:8, :] = up_ref[0:4, :]
    lines_ref[8:10, :] = top_ref[0:2, :]
    lines_ref[10:11, :] = hidden_ref[2:3, :]
    lines_ref[11:12, :] = top_ref[2:3, :]
    full_ref[:, 3 * part : 3 * part + 128] = jnp.transpose(lines_ref[...]).astype(BF)
    if 3 * part + 128 < full_ref.shape[1]:
        full_ref[:, 3 * part + 128 :] = jnp.zeros((D, full_ref.shape[1] - 3 * part - 128), BF)
    halves(parts, where_ref[1], full_ref)


def weights(plan, order, kernel, name, us, total, scratch, *args):
    part = total // plan.reps
    return pl.pallas_call(
        kernel,
        grid=(1,),
        out_shape=(later((D, part), BF),) * plan.reps,
        in_specs=[smem()] + [vmem() if O_V1 else still(a.shape) for a in args],
        out_specs=[still((D, part))] * plan.reps,
        scratch_shapes=[pltpu.VMEM((D, total), BF)] + scratch,
        compiler_params=params(28),
        name=name,
        cost_estimate=behind(us),
    )(order.where, *args)


def gx_of(count, a_ref, b_ref, w_ref, hidden):
    hidden = hidden.astype(F32)
    ca, cb = count * 128, D - count * 128
    for j in range(3):
        hidden = hidden + dot_t(a_ref[:, j * ca : (j + 1) * ca], w_ref[:, j * D : j * D + ca])
        hidden = hidden + dot_t(b_ref[:, j * cb : (j + 1) * cb], w_ref[:, j * D + ca : (j + 1) * D])
    return hidden


def far_back_kernel(count, where_ref, ga_ref, proj_ref, probs_ref, w_ref, hidden_ref, a_ref, b_ref, far_ref):
    heads_back(0, count, 0, ga_ref, proj_ref, probs_ref, a_ref)
    heads_back(count, PAIRS - count, 0, ga_ref, proj_ref, probs_ref, b_ref)
    far_ref[...] = gx_of(count, a_ref, b_ref, w_ref, hidden_ref[...]).astype(BF)


def far_back(order, count, ga, proj, probs, w_one, hidden):
    rows = ga.shape[0] // 2
    steps = rows // TILE
    wide = 3 * count * 128
    return pl.pallas_call(
        partial(far_back_kernel, count),
        grid=(steps,),
        out_shape=(shape((rows, wide), BF), shape((rows, 3 * D - wide), BF), shape((rows, D), BF)),
        in_specs=[smem()]
        + tile_specs(steps)
        + [still((D, 3 * D)), pl.BlockSpec((TILE, D), lambda i: (i + steps, 0))],
        out_specs=[rows_at(wide), rows_at(3 * D - wide), rows_at(D)],
        compiler_params=params(24),
        name="far_back",
        cost_estimate=behind(11),
    )(order.where, ga, stay(proj), stay(probs), stay(w_one), stay(hidden))


def token_back_kernel(count, where_ref, a_ref, b_ref, w_ref, hidden_ref, own_ref):
    own_ref[...] = gx_of(count, a_ref, b_ref, w_ref, hidden_ref[...])


def token_back(order, count, ga, gb, w_one, hidden):
    rows = gb.shape[0]
    return pl.pallas_call(
        partial(token_back_kernel, count),
        grid=(rows // TILE,),
        out_shape=shape((rows, D), F32),
        in_specs=[smem(), rows_at(ga.shape[1]), rows_at(gb.shape[1]), still((D, 3 * D)), rows_at(D)],
        out_specs=rows_at(D),
        compiler_params=params(24),
        name="token_back",
        cost_estimate=behind(4),
    )(order.where, ga, gb, stay(w_one), stay(hidden))


def on_device(
    plan, query_tokens, passage_tokens, query_cot, passage_cot, positives, w_qkv, w_out, w_up, w_down, biases, gains
):
    me = lax.axis_index("dp")
    core = lax.axis_index("rep")
    tower = (me >> 2) & 1
    span = jnp.where(tower == 0, query_tokens.shape[1], passage_tokens.shape[1])
    where = jnp.stack([me, core, tower, span]).astype(jnp.int32)
    swap = plan.along(1)

    def exchange(a, b, *others):
        a, b = a.reshape(-1, D), b.reshape(-1, D)
        away = jnp.where(tower == 0, b, a)
        return jnp.where(tower == 0, a, b), send(after(away, *others) if others else away, swap)

    def merged(own, back):
        a = jnp.where(tower == 0, own, back)
        b = jnp.where(tower == 0, back, own)
        return a.reshape(query_tokens.shape), b.reshape(passage_tokens.shape)

    order = Order(where)
    mine, other, mine2, other2, mine3, other3 = shards_of(plan, order, w_qkv, w_out, biases, gains, w_up, w_down)
    z1 = gather_line(plan, mine, other)
    both2 = jnp.concatenate([mine2, send(other2, swap)], 0)
    both3 = jnp.concatenate([mine3, send(other3, swap)], 0)
    z2 = gather_steps(plan, both2, z1)
    env = {"z1": z1, "z2": z2, "both2": both2, "both3": both3}

    def deps(names):
        return [env[n] for n in names.split(",") if n]

    p1 = gather_plane(plan, z1, *deps(O_NEAR1))
    z3 = gather_steps(plan, both3, z2)
    env["z3"] = z3
    x_mine, x_got = exchange(query_tokens, passage_tokens, *deps(O_X))
    w_one = gather_cores(plan, order, p1)
    p2 = gather_plane(plan, z2)
    env["p2"] = p2[0]
    if O_NEAR3 != "first" and O_NEAR3 != "join":
        p3 = gather_plane(plan, after(z3, *deps(O_NEAR3)) if O_NEAR3 else z3)
    if O_P2:
        order.done(p2[0])
    first = order.done(attend(order, x_mine, w_one, 0))
    if O_NEAR3 == "first":
        p3 = gather_plane(plan, z3, first[6])
    if O_NEAR3 == "join":
        step3 = send(z3, plan.first())
        near3 = join(order, z3, step3)
        p3 = near3, send(near3, plan.second())
    proj, probs, attn, hat1, rstd1, norm, vec, cls_b = order.done(attend(order, x_got, w_one, 1, first[:6]))
    env["first"], env["norm"] = first[6], norm
    w_two = gather_cores(plan, order, tuple(after(b, *deps(O_D2)) for b in p2) if O_D2 else p2)
    half_up = order.done(up(order, norm, w_two, vec, 0))
    env["up"] = half_up[0]
    w_three = gather_cores(plan, order, tuple(after(b, *deps(O_D3)) for b in p3) if O_D3 else p3)
    msg = first_rows(order, first[7], cls_b, w_two, w_three, vec, positives)
    env["msg"] = msg
    if O_COT != "pack":
        cot_mine, cot_got = exchange(query_cot, passage_cot, *deps(O_COT))
    loss = Contrast(plan, order, msg, positives.shape[0])
    act, slope = order.done(up(order, norm, w_two, vec, 1, half_up))
    loss.pack()
    if O_COT == "pack":
        cot_mine, cot_got = exchange(query_cot, passage_cot, loss.bufs[0])
    cot = jnp.concatenate([cot_mine, cot_got], 0)
    if O_COTD == "down":
        order.done(cot)
    out_own, out_far, hat2, rstd2 = order.done(down(order, act, w_three, hat1, vec))
    out_back = send(out_far, swap)
    loss.join()
    if O_COTD == "loss":
        order.done(cot)
    if O_OUT == "loss":
        order.done(out_back)
    query_loss, cls_grad = loss.loss()

    second, gs, sums_top, g_down = order.done(top(plan, order, cot, cls_grad, hat2, rstd2, vec, act))
    down_part = Scatter(plan, order, g_down, w_down.shape[1])
    if O_GELU == 1:
        acc, sums_up, g_up = order.done(gelu_back(plan, order, gs, w_three, slope, norm, w_two))
    else:
        gu, sums_up, g_up = order.done(gelu_back2(plan, order, gs, w_three, slope, norm))
    up_part = Scatter(plan, order, g_up, w_up.shape[1])
    if O_OUT == "pick":
        order.done(out_back)
    down_part.one()
    if O_OUT == "hidden":
        order.done(out_back)
    if O_GELU == 1:
        hidden, go, ga, sums = order.done(hidden_back(order, acc, second, hat1, rstd1, w_one, vec))
    else:
        hidden, go, ga, sums = order.done(hidden_back2(order, gu, w_two, second, hat1, rstd1, w_one, vec))
    if O_OUT == "pick5":
        order.done(out_back)
    up_part.one()
    split = O_SPLIT
    half = ga.shape[0] // 2
    if O_V3:
        hidden = go
    far_a, far_b, gx_far = order.done(far_back(order, split, ga, proj, probs, w_one, hidden))
    gx_back = send(gx_far, swap)
    near_a = order.done(attend_back(order, 0, split, ga, proj, probs, half))
    total = wide(3 * split * 128 + D, plan.reps)
    kernel = first_weights_kernel
    g_a = order.done(weights(plan, order, kernel, "first_weights", 5, total, [], x_mine, x_got, near_a, far_a, stay(attn), go))
    a_part = Scatter(plan, order, g_a, w_qkv.shape[1])
    if O_GX == "fw":
        order.done(gx_back)
    down_part.two()
    if O_GX == "two":
        order.done(gx_back)
    up_part.two()
    near_b = order.done(attend_back(order, split, PAIRS - split, ga, proj, probs, half))
    if O_GX == "nb":
        order.done(gx_back)
    down_part.three()
    a_part.one()
    if O_GX == "a1":
        order.done(gx_back)
    up_part.three()
    if O_GX == "u3":
        order.done(gx_back)
    total = wide(3 * (D - split * 128) + 128, plan.reps)
    kernel = partial(last_weights_kernel, split)
    scratch = [pltpu.VMEM((128, D), F32)]
    args = (x_mine, x_got, near_b, far_b, near_a, far_a, sums_up, sums_top, sums)
    g_b = order.done(weights(plan, order, kernel, "last_weights", 4, total, scratch, *args))
    b_part = Scatter(plan, order, g_b, w_qkv.shape[1])
    gx_own = order.done(token_back(order, split, near_a, near_b, w_one, hidden))
    steps = {
        "a2": a_part.two, "b1": b_part.one, "d4": down_part.four, "u4": up_part.four, "a3": a_part.three,
        "b2": b_part.two, "dl": down_part.last, "ul": up_part.last, "a4": a_part.four, "b3": b_part.three,
        "b4": b_part.four, "al": a_part.last, "bl": b_part.last,
        "fd": lambda: outs.append(finish(plan, order, [down_part], [[(0, D, 0, 0)]], [w_down.shape])[0]),
        "fu": lambda: outs.append(finish(plan, order, [up_part], [[(0, FF, 0, 0)]], [w_up.shape])[0]),
    }
    outs = []
    tails = [
        "a2 b1 d4 u4 a3 b2 dl ul a4 b3 fd fu b4 al bl",
        "b1 a2 d4 u4 b2 a3 dl b3 ul a4 fd b4 fu bl al",
        "a2 b1 d4 b2 u4 a3 b3 dl ul a4 b4 fd fu al bl",
        "a2 d4 b1 u4 a3 dl b2 ul b3 a4 fd fu b4 al bl",
        "b1 a2 d4 u4 a3 b2 dl ul b3 a4 fd fu b4 al bl",
        "a2 b1 d4 u4 a3 b2 b3 dl ul a4 b4 fd fu al bl",
    ]
    for step in tails[O_TAIL].split():
        steps[step]()
    grad_down, grad_up = outs
    query_out, passage_out = merged(out_own, after(out_back, b_part.out))
    query_grad, passage_grad = merged(gx_own, after(gx_back, b_part.out).astype(F32))
    qa, qb = split * 128, D - split * 128
    spans_a = [(0, D, 1, 0)] + [(D + j * qa, qa, 0, j * D) for j in range(3)]
    spans_b = [(j * qb, qb, 0, j * D + qa) for j in range(3)] + [(3 * qb, 128, 2, 0)]
    shapes = [w_qkv.shape, w_out.shape, biases.shape, gains.shape]
    grads = finish(plan, order, [a_part, b_part], [spans_a, spans_b], shapes, 2)
    return (
        query_out,
        passage_out,
        query_grad,
        passage_grad,
        query_loss,
        grads[0],
        grads[1],
        grad_up,
        grad_down,
        grads[2],
        grads[3],
    )


def solution(mesh):
    plan = Plan(mesh.shape["dp"], mesh.shape["rep"])
    rows = P(("dp", "rep"), None, None)
    shards = P(None, "dp", None)
    lanes = P(None, None, "dp")
    return jax.shard_map(
        partial(on_device, plan),
        mesh=mesh,
        in_specs=(rows,) * 4 + (P(("dp", "rep"), None),) + (shards,) * 4 + (lanes,) * 2,
        out_specs=(rows,) * 4 + (P(("dp", "rep")),) + (shards,) * 4 + (lanes,) * 2,
        check_vma=False,
    )
```

```python
from functools import partial
import jax
import jax.numpy as jnp
from jax import lax
from jax.experimental import pallas as pl
from jax.experimental.pallas import tpu as pltpu
from jax.sharding import PartitionSpec as P
AXES = ('dp', 'rep')
BF = jnp.bfloat16
F32 = jnp.float32
D = 768
FF = 3072
HEADS = 12
HEAD = 64
PAIRS = HEADS // 2
BLOCK = 128
TILE = 256
EPS = 1e-05
LOSS_WEIGHT = 32.0
MIB = 2 ** 20
AT_OUT = 3 * D
AT_VEC = 4 * D


def smem():
    return pl.BlockSpec(memory_space=pltpu.SMEM)


def vmem():
    return pl.BlockSpec(memory_space=pltpu.VMEM)


def cost(us):
    return pl.CostEstimate(flops=int(us * 1000000000.0), transcendentals=0, bytes_accessed=int(us * 3000000.0))


def behind(us):
    return cost(4.0 * us)


def params(mib):
    return pltpu.CompilerParams(vmem_limit_bytes=int(mib) * MIB)


def still(shape, at=None):
    index = at if at is not None else (0,) * len(shape)
    return pl.BlockSpec(shape, lambda i, *_: index, pipeline_mode=pl.Buffered(1))


def rows_at(width, rows=TILE):
    return pl.BlockSpec((rows, width), lambda i, *_: (i, 0))


def shape(dims, dtype):
    return jax.ShapeDtypeStruct(dims, dtype)


def far(dims, dtype):
    return pltpu.HBM(dims, dtype)


def stay(v):
    return pltpu.with_memory_space_constraint(v, pltpu.HBM)


def after(v, *others):
    return lax.optimization_barrier((v,) + others)[0]


class Order:
    def __init__(self, where):
        self.where = where

    def done(self, out):
        self.where = after(self.where, out)
        return out


def in_vmem(kernel, name, us, outs, *args, mib=24):
    return pl.pallas_call(kernel, out_shape=tuple((shape(*o) for o in outs)), in_specs=[smem() if a.ndim == 1 else vmem() for a in args], out_specs=tuple((vmem() for _ in outs)), compiler_params=params(mib), name=name, cost_estimate=cost(us))(*args)


def wide(width, reps):
    unit = 128 * reps
    return -(-width // unit) * unit


def by_core(core, reps, width, move):
    if width % 128 == 0:
        move(pl.ds(pl.multiple_of(core * width, 128), width))
        return
    for c in range(reps):

        @pl.when(core == c)
        def one(c=c):
            move(slice(c * width, (c + 1) * width))


def halves(refs, core, source):
    width = refs[0].shape[1]
    for q, ref in enumerate(refs):

        def move(lanes, ref=ref):
            ref[...] = source[:, lanes]
        by_core(core ^ q, len(refs), width, move)


def send(v, pairs):
    return lax.ppermute(v, AXES, pairs)


class Plan:
    def __init__(self, n, reps):
        self.n, self.reps, self.depth = (n, reps, n // 4)

    def pairs(self, move):
        return [(d * self.reps + r, (d ^ move(r)[0]) * self.reps + (r ^ move(r)[1])) for d in range(self.n) for r in range(self.reps)]

    def along(self, k):
        return self.pairs(lambda r: (4 * k, 0))

    def first(self):
        return self.pairs(lambda r: (1 + r % 2, 0))

    def second(self):
        return self.pairs(lambda r: (2 - r % 2, 0))

    def sibling(self, q):
        return self.pairs(lambda r: (0, q))


def assemble_kernel(depth, reps, width, where_ref, *refs):
    bufs, out = (refs[:2 * reps], refs[2 * reps])
    me, core = (where_ref[0], where_ref[1])
    for q in range(reps):
        owner = core ^ q
        p1 = 1 + owner % 2
        p2 = 2 - owner % 2

        def move(lanes, q=q, p1=p1, p2=p2):
            for b in range(2):
                for f in range(2):
                    for k in range(depth):
                        dst = me ^ b * p2 ^ f * p1 ^ 4 * k
                        out[pl.ds(dst, 1), :, lanes] = bufs[q * 2 + b][pl.ds(f * depth + k, 1)]
        by_core(owner, reps, width, move)


def shards_kernel(reps, where_ref, qkv_ref, out_ref, bias_ref, gain_ref, up_ref, down_ref, *rest):
    outs, full_ref = (rest[:-1], rest[-1])
    core, tower = (where_ref[1], where_ref[2])
    spare = full_ref.shape[2] - AT_VEC

    def turned(ref, t, at):
        rows = ref[t][0].astype(F32)
        i = lax.broadcasted_iota(jnp.int32, (rows.shape[0], spare), 0)
        j = lax.broadcasted_iota(jnp.int32, (rows.shape[0], spare), 1)
        return t_dot(rows.astype(BF), jnp.where(i + at == j, 1.0, 0.0).astype(BF))
    for n in range(2):
        t = pl.ds(tower if n == 0 else 1 - tower, 1)
        full_ref[:, :, :AT_OUT] = qkv_ref[t]
        full_ref[:, :, AT_OUT:AT_VEC] = out_ref[t]
        full_ref[0, :, AT_VEC:] = (turned(bias_ref, t, 0) + turned(gain_ref, t, bias_ref.shape[1])).astype(BF)
        for c, ref in enumerate((full_ref, up_ref, down_ref)):
            put = outs[2 * c + n]

            def move(lanes, ref=ref, put=put, t=t):
                put[...] = ref[:, :, lanes] if ref is full_ref else ref[t, :, lanes]
            by_core(core, reps, put.shape[2], move)


def shards_of(plan, order, w_qkv, w_out, biases, gains, w_up, w_down):
    reps = plan.reps
    one = wide(AT_VEC + 128, reps)
    outs = []
    for rows, width in ((w_qkv.shape[1], one), (w_up.shape[1], FF), (w_down.shape[1], D)):
        outs += [shape((1, rows, width // reps), BF)] * 2
    args = (w_qkv, w_out, biases, gains, w_up, w_down)
    got = pl.pallas_call(partial(shards_kernel, reps), grid=(1,), out_shape=tuple(outs), in_specs=[smem()] + [still(a.shape) for a in args], out_specs=[still(o.shape) for o in outs], scratch_shapes=[pltpu.VMEM((1, w_qkv.shape[1], one), BF)], compiler_params=params(24), name='shards', cost_estimate=cost(2))(order.where, *[stay(a) for a in args])
    return order.done(got)


def join_kernel(where_ref, *refs):
    ins, out_ref = (refs[:-1], refs[-1])
    at = 0
    for ref in ins:
        out_ref[at:at + ref.shape[0]] = ref[...]
        at += ref.shape[0]


def join(order, *bufs):
    total = sum((b.shape[0] for b in bufs))
    outs = (((total,) + bufs[0].shape[1:], bufs[0].dtype),)
    return order.done(in_vmem(join_kernel, 'join', 0.5, outs, order.where, *bufs))[0]


def gather_line(plan, mine, other):
    got = [send(other if k % 2 else mine, plan.along(k)) for k in range(1, plan.depth)]
    return jnp.concatenate([mine] + got, 0)


def gather_steps(plan, both, *others):
    z = both
    k = 2
    while k < plan.depth:
        if others:
            z, others = (after(z, *others), ())
        z = jnp.concatenate([z, send(z, plan.along(k))], 0)
        k *= 2
    return z


def gather_plane(plan, z, *others):
    near = jnp.concatenate([z, send(z, plan.first())], 0)
    if others:
        near = after(near, *others)
    return (near, send(near, plan.second()))


def gather_cores(plan, order, bufs):
    rows, width = bufs[0].shape[1:]
    bufs = list(bufs)
    for q in range(1, plan.reps):
        bufs += [send(b, plan.sibling(q)) for b in bufs[:2]]
    full = pl.pallas_call(partial(assemble_kernel, plan.depth, plan.reps, width), out_shape=jax.ShapeDtypeStruct((plan.n, rows, width * plan.reps), BF), in_specs=[smem()] + [vmem()] * len(bufs), out_specs=vmem(), compiler_params=params(24), name='assemble', cost_estimate=cost(2))(order.where, *bufs)
    order.done(full)
    return full.reshape(plan.n * rows, width * plan.reps)


def add_kernel(depth, where_ref, a_ref, b_ref, s_ref, k_ref):
    me, core = (where_ref[0], where_ref[1])
    p1 = 1 + core % 2
    p2 = 2 - core % 2
    for j in range(4 * depth):
        at = me ^ (1 - j // (2 * depth)) * p1 ^ (1 - j // depth % 2) * p2 ^ 4 * (j % depth)
        o_ref, to = (s_ref, j) if j < 2 * depth else (k_ref, j - 2 * depth)
        o_ref[to] = (a_ref[at].astype(F32) + b_ref[at].astype(F32)).astype(BF)


def two_kernel(where_ref, k_ref, r_ref, s_ref, o_ref):
    q = s_ref.shape[0]
    for j in range(2 * q):
        total = (k_ref[j].astype(F32) + r_ref[j].astype(F32)).astype(BF)
        if j < q:
            s_ref[j] = total
        else:
            o_ref[j - q] = total


def line_kernel(where_ref, k_ref, r_ref, s_ref, o_ref):
    half = o_ref.shape[0]
    for j in range(2 * half):
        total = (k_ref[j].astype(F32) + r_ref[j].astype(F32)).astype(BF)
        if j < half:
            o_ref[j] = total
        else:
            s_ref[j - half] = total


def last_kernel(where_ref, own_ref, got_ref, out):
    tower = where_ref[2]
    out[pl.ds(tower, 1)] = own_ref[...]
    out[pl.ds(1 - tower, 1)] = got_ref[...]


def plus(a, b):
    return (a.astype(F32) + b.astype(F32)).astype(BF)


class Scatter:
    def __init__(self, plan, order, parts, rows):
        self.plan, self.order, self.rows = (plan, order, rows)
        self.width = parts[0].shape[1]
        parts = [p.reshape(plan.n, rows, self.width) for p in parts]
        self.own = parts[0]
        got = [send(parts[q], plan.sibling(q)) for q in range(1, plan.reps)]
        self.rest = got[0]
        for o in got[1:]:
            self.rest = plus(self.rest, o)

    def run(self, kernel, name, us, outs, *args):
        return self.order.done(in_vmem(kernel, name, us, outs, self.order.where, *args))

    def one(self):
        plan = self.plan
        n = plan.n
        whole = (n, self.rows, self.width)
        half = shape((n // 2, self.rows, self.width), BF)
        hs, self.hk = self.order.done(pl.pallas_call(partial(add_kernel, plan.depth), out_shape=(half, half), in_specs=[smem(), vmem(), vmem()], out_specs=(vmem(), vmem()), compiler_params=params(24), name='pick_add', cost_estimate=behind(3))(self.order.where, self.own, self.rest))
        self.r1 = send(hs, plan.first())
        return

    def two(self):
        quarter = ((self.plan.n // 4, self.rows, self.width), BF)
        ks, self.kk = self.run(two_kernel, 'add_two', 1, (quarter, quarter), self.hk, self.r1)
        self.r2 = send(ks, self.plan.second())

    def line(self):
        n = self.kk.shape[0] // 2
        half = ((n, self.rows, self.width), BF)
        out, self.kk = self.run(line_kernel, 'add_line', 1, (half, half), self.kk, self.r2)
        self.r2 = send(out, self.plan.along(n))
        return out

    def three(self):
        self.line()

    def four(self):
        while self.kk.shape[0] > 1:
            self.out = self.line()

    def last(self):
        plan = self.plan
        outs = (((2, self.rows, self.width), BF),)
        pair, = self.run(last_kernel, 'add_last', 1, outs, self.kk, self.r2)
        self.ends = [pair] + [send(pair, plan.sibling(q)) for q in range(1, plan.reps)]


def finish_kernel(reps, spans, vec, where_ref, *refs):
    chunks = len(spans)
    ins, outs = (refs[:chunks * reps], refs[chunks * reps:])
    core = where_ref[1]
    for c in range(chunks):
        parts = ins[c * reps:(c + 1) * reps]
        width = parts[0].shape[2]
        for q in range(reps):
            for mine in range(reps):

                @pl.when(core ^ q == mine)
                def copy(c=c, parts=parts, q=q, mine=mine):
                    for at, size, out, to in spans[c]:
                        low, high = (max(at, mine * width), min(at + size, (mine + 1) * width))
                        if low >= high:
                            continue
                        lanes = slice(low - mine * width, high - mine * width)
                        if out == vec:
                            turn(parts[q], lanes, low - at, outs[out], outs[out + 1])
                        else:
                            outs[out][:, :, to + low - at:to + high - at] = parts[q][:, :, lanes].astype(F32)


def turn(part_ref, lanes, at, bias_ref, gain_ref):
    for t in range(2):
        columns = part_ref[t, :, lanes]
        for ref, start in ((bias_ref, 0), (gain_ref, bias_ref.shape[1])):
            n = ref.shape[1]
            i = lax.broadcasted_iota(jnp.int32, (n, columns.shape[1]), 0)
            j = lax.broadcasted_iota(jnp.int32, (n, columns.shape[1]), 1)
            ref[t] = dot_t(jnp.where(i + start == j + at, 1.0, 0.0).astype(BF), columns)


def finish(plan, order, chunks, spans, shapes, vec=-1):
    outs = tuple(((s, F32) for s in shapes))
    args = [p for c in chunks for p in c.ends]
    kernel = partial(finish_kernel, plan.reps, spans, vec)
    return order.done(in_vmem(kernel, 'finish', 2, outs, order.where, *args))


def dot(a, b):
    return jnp.dot(a, b, preferred_element_type=F32)


def dot_t(a, b):
    return lax.dot_general(a, b, (((1,), (1,)), ((), ())), preferred_element_type=F32)


def t_dot(a, b):
    return lax.dot_general(a, b, (((0,), (0,)), ((), ())), preferred_element_type=F32)


def normalize(h):
    center = h - jnp.mean(h, -1, keepdims=True)
    rstd = lax.rsqrt(jnp.mean(center * center, -1, keepdims=True) + EPS)
    return (center * rstd, rstd)


def lane_masks():
    lane = lax.broadcasted_iota(jnp.int32, (1, 2 * HEAD), 1)
    low = (lane < HEAD).astype(F32).astype(BF)
    return (low, (1.0 - low.astype(F32)).astype(BF))


def attend_kernel(part, where_ref, x_ref, w_ref, *rest):
    proj_ref, probs_ref, attn_ref, hat_ref, rstd_ref, norm_ref, vec_ref, cls_ref, bias_ref = rest[-9:]

    @pl.when(pl.program_id(0) == 0)
    def prepare():
        vec_ref[...] = jnp.transpose(w_ref[:, AT_VEC:AT_VEC + 128].astype(F32))
        span = where_ref[3]
        row = lax.broadcasted_iota(jnp.int32, (BLOCK, 2 * BLOCK), 0)
        col = lax.broadcasted_iota(jnp.int32, (BLOCK, 2 * BLOCK), 1) % BLOCK
        bias_ref[...] = jnp.where(row ^ col < span, 0.0, -1e+30)
    x = x_ref[...]
    for j in range(3):
        part = dot(x, w_ref[:, j * D:(j + 1) * D])
        if j != 1:
            part = part + vec_ref[j // 2:j // 2 + 1, :]
        proj_ref[:, j * D:(j + 1) * D] = part.astype(BF)
    low, high = lane_masks()
    bias = bias_ref[...]
    for blk in range(256 // BLOCK):
        rows = slice(blk * BLOCK, (blk + 1) * BLOCK)
        for pair in range(PAIRS):
            lanes = slice(pair * 128, (pair + 1) * 128)
            q = proj_ref[rows, lanes]
            k = proj_ref[rows, D + pair * 128:D + (pair + 1) * 128]
            v = proj_ref[rows, 2 * D + pair * 128:2 * D + (pair + 1) * 128]
            s = dot_t(k, jnp.concatenate([q * low, q * high], 0)) * HEAD ** (-0.5) + bias
            e = jnp.exp(s - jnp.max(s, 0, keepdims=True))
            p = (e * (1.0 / jnp.sum(e, 0, keepdims=True))).astype(BF)
            probs_ref[blk, pair] = p
            tall = jnp.concatenate([p[:, :BLOCK], p[:, BLOCK:]], 0)
            attn_ref[rows, lanes] = t_dot(tall, jnp.concatenate([v * low, v * high], 0)).astype(BF)
    hidden = x.astype(F32) + (dot(attn_ref[...], w_ref[:, AT_OUT:AT_VEC]) + vec_ref[2:3, :])
    hat, rstd = normalize(hidden)
    hat_ref[...] = hat
    rstd_ref[...] = rstd
    norm = hat * vec_ref[10:11, :] + vec_ref[3:4, :]
    norm_ref[...] = norm.astype(BF)
    for j in range(8):
        cls_ref[j:j + 1, :] = norm[32 * j:32 * j + 1, :]


def attend(order, x, w_one, part, before=()):
    rows = 2 * x.shape[0]
    per = 256 // BLOCK
    steps = rows // 256 // 2
    first = part * steps

    def here(width):
        return pl.BlockSpec((256, width), lambda i: (i + first, 0))
    return pl.pallas_call(partial(attend_kernel, part), grid=(steps,), out_shape=(far((rows, 3 * D), BF), far((rows // BLOCK, PAIRS, BLOCK, 2 * BLOCK), BF), far((rows, D), BF), far((rows, D), F32), far((rows, 1), F32), far((rows, D), BF), shape((128, D), F32), shape((rows // 64, D), F32)), in_specs=[smem(), rows_at(D, 256), vmem()] + [pl.BlockSpec(memory_space=pl.ANY)] * len(before), out_specs=[here(3 * D), pl.BlockSpec((per, PAIRS, BLOCK, 2 * BLOCK), lambda i: (i + first, 0, 0, 0)), here(D), here(D), here(1), here(D), still((128, D)), rows_at(D, 8)], scratch_shapes=[pltpu.VMEM((BLOCK, 2 * BLOCK), F32)], input_output_aliases={3 + j: j for j in range(len(before))}, compiler_params=params(24), name='attend', cost_estimate=cost(7))(order.where, x, w_one, *[b for b in before])


def gelu_pair(u):
    phi = 0.5 + 0.5 * lax.erf(u * 2 ** (-0.5))
    return (u * phi, phi + u * (jnp.exp(-0.5 * u * u) * (2 * jnp.pi) ** (-0.5)))


def up_kernel(first, where_ref, norm_ref, w_ref, vec_ref, *rest):
    act_ref, slope_ref = rest[-2:]
    bias = vec_ref[pl.ds(4 + first + pl.program_id(0), 1), :]
    for m in range(0, norm_ref.shape[0], 256):
        rows = slice(m, m + 256)
        act, slope = gelu_pair(dot(norm_ref[rows, :], w_ref[...]) + bias)
        act_ref[rows, :] = act.astype(BF)
        slope_ref[rows, :] = slope.astype(BF)


def up(order, norm, w_up, vec, part, before=()):
    rows = norm.shape[0]
    steps = FF // D // 2
    first = part * steps
    col = pl.BlockSpec((rows, D), lambda i: (0, i + first))
    return pl.pallas_call(partial(up_kernel, first), grid=(steps,), out_shape=(shape((rows, FF), BF), far((rows, FF), BF)), in_specs=[smem(), still(norm.shape), pl.BlockSpec((D, D), lambda i: (0, i + first)), still(vec.shape)] + [pl.BlockSpec(memory_space=pl.ANY)] * len(before), out_specs=[col, col], input_output_aliases={4 + j: j for j in range(len(before))}, compiler_params=params(24), name='up', cost_estimate=cost(8))(order.where, norm, w_up, vec, *[b for b in before])


def down_kernel(where_ref, act_ref, w_ref, hat_ref, vec_ref, own_ref, far_ref, hat2_ref, rstd2_ref):
    normed = hat_ref[...] * vec_ref[10:11, :] + vec_ref[3:4, :]
    second = normed + (dot(act_ref[...], w_ref[...]) + vec_ref[8:9, :])
    hat, rstd = normalize(second)
    hat2_ref[...] = hat
    rstd2_ref[...] = rstd
    out = (hat * vec_ref[11:12, :] + vec_ref[9:10, :]).astype(BF)
    half = pl.num_programs(0) // 2

    @pl.when(pl.program_id(0) < half)
    def near():
        own_ref[...] = out

    @pl.when(pl.program_id(0) >= half)
    def away():
        far_ref[...] = out


def down(order, act, w_down, hat, vec):
    rows = act.shape[0]
    half = rows // 256 // 2
    near = pl.BlockSpec((256, D), lambda i: (jnp.minimum(i, half - 1), 0))
    away = pl.BlockSpec((256, D), lambda i: (jnp.maximum(i - half, 0), 0))
    return pl.pallas_call(down_kernel, grid=(rows // 256,), out_shape=(far((rows // 2, D), BF), shape((rows // 2, D), BF), shape((rows, D), F32), shape((rows, 1), F32)), in_specs=[smem(), rows_at(FF, 256), vmem(), rows_at(D, 256), still(vec.shape)], out_specs=[near, away, rows_at(D, 256), rows_at(1, 256)], compiler_params=params(24), name='down', cost_estimate=cost(8))(order.where, act, w_down, stay(hat), vec)


def first_kernel(where_ref, a_ref, b_ref, up_ref, down_ref, vec_ref, marks_ref, msg_ref):
    norm = jnp.concatenate([a_ref[...], b_ref[...]], 0)
    second = norm + vec_ref[8:9, :]
    wide = norm.astype(BF)
    for j in range(FF // D):
        u = dot(wide, up_ref[:, j * D:(j + 1) * D]) + vec_ref[4 + j:5 + j, :]
        second = second + dot(gelu_pair(u)[0].astype(BF), down_ref[j * D:(j + 1) * D, :])
    hat, _ = normalize(second)
    msg_ref[:, :D] = (hat * vec_ref[11:12, :] + vec_ref[9:10, :]).astype(BF)
    marks = marks_ref[...].astype(F32)
    pad = jnp.zeros((32 - marks.shape[0], marks.shape[1]), F32)
    msg_ref[:, D:] = jnp.concatenate([marks, pad], 0).astype(BF)


def first_rows(order, a, b, w_up, w_down, vec, positives):
    outs = (((32, D + positives.shape[1]), BF),)
    return order.done(in_vmem(first_kernel, 'first_rows', 4, outs, order.where, a, b, w_up, w_down, vec, positives))[0]


def pack_kernel(per, where_ref, *refs):
    msgs, out_ref = (refs[:-1], refs[-1])
    queries = per * 4
    pick_row = lax.broadcasted_iota(jnp.int32, (16, 32), 0)
    pick_col = lax.broadcasted_iota(jnp.int32, (16, 32), 1)
    pick = jnp.where((pick_col == pick_row * (32 // (2 * per))) & (pick_row < 2 * per), 1.0, 0.0).astype(BF)
    for n in range(len(msgs) // 2):
        for tower in range(2):

            @pl.when(where_ref[2] == tower)
            def put(n=n, tower=tower):
                zero, one = (msgs[2 * n + tower], msgs[2 * n + 1 - tower])
                out_ref[n, :32, :D] = zero[:, :D]
                out_ref[n, :queries, D:] = zero[:queries, D:]
                out_ref[n, queries:32, D:] = one[:queries, D:]
                out_ref[n, 32:, :D] = dot(pick, one[:, :D]).astype(BF)
                out_ref[n, 32:, D:] = jnp.zeros((16, out_ref.shape[2] - D), BF)


def contrast_kernel(reps, depth, per, where_ref, *refs):
    parts, loss_ref, grad_ref, acc_ref = (refs[:reps], refs[reps], refs[reps + 1], refs[reps + 2])
    me, core, tower = (where_ref[0], where_ref[1], where_ref[2])
    pieces = parts[0].shape[0]
    passages = parts[0].shape[2] - D
    cls_p = jnp.concatenate([part[:, 32:, :D].reshape(pieces * 16, D) for part in parts], 0)
    cols = cls_p.shape[0]
    col = lax.broadcasted_iota(jnp.int32, (passages, cols), 1)
    row = lax.broadcasted_iota(jnp.int32, (passages, cols), 0)
    j, slot = (col // 16, col % 16)
    base = (me | 4) ^ 8 * (j % (depth // 2)) ^ j // (depth // 2) % 4
    owner = jnp.where(slot < per, base, base ^ 4)
    passage = (owner * reps + (core ^ j // (2 * depth))) * per + slot % per
    pick = jnp.where((row == passage) & (slot < 2 * per), 1.0, 0.0).astype(BF)
    valid = lax.broadcasted_iota(jnp.int32, (1, cols), 1) % 16 < 2 * per
    acc_ref[...] = jnp.zeros_like(acc_ref)
    group = min(8, pieces)
    for q, part in enumerate(parts):
        for at in range(0, pieces, group):
            cls_q = part[at:at + group, :32, :D].reshape(group * 32, D)
            marks = dot(part[at:at + group, :32, D:].reshape(group * 32, passages), pick)
            raw = jnp.where(valid, dot_t(cls_q, cls_p) * D ** (-0.5), -1e+30)
            e = jnp.exp(raw - jnp.max(raw, -1, keepdims=True))
            total = jnp.sum(e, -1, keepdims=True)
            me_ = marks * e
            marked = jnp.sum(me_, -1, keepdims=True)
            grad = (LOSS_WEIGHT * (e / total - me_ / marked)).astype(BF)
            acc_ref[...] += t_dot(grad[:, :128], cls_q)[:16] * D ** (-0.5)
            if q == 0 and at == 0:
                loss_ref[...] = (jnp.log(total) - jnp.log(marked))[:32]
                grad_ref[...] = dot(grad[:32], cls_p) * D ** (-0.5)

    @pl.when(tower == 1)
    def passages_own():
        grad_ref[...] = jnp.zeros_like(grad_ref)
        for s in range(2 * per):
            at = s * (32 // (2 * per))
            grad_ref[at:at + 1, :] = acc_ref[s:s + 1, :]


class Contrast:

    def __init__(self, plan, order, msg, queries):
        self.plan, self.order, self.queries = (plan, order, queries)
        self.msgs = [msg] + [send(msg, plan.along(k)) for k in range(1, plan.depth)]

    def pack(self):
        plan = self.plan
        outs = (((plan.depth // 2, 48, self.msgs[0].shape[1]), BF),)
        kernel = partial(pack_kernel, self.queries // 4)
        buf, = self.order.done(in_vmem(kernel, 'pack', 1, outs, self.order.where, *self.msgs))
        self.bufs = [buf] + [send(buf, plan.pairs(lambda r, m=m: (m, 0))) for m in range(1, 4)]

    def join(self):
        plan = self.plan
        buf = join(self.order, *self.bufs)
        self.parts = [buf] + [send(buf, plan.sibling(s)) for s in range(1, plan.reps)]

    def loss(self):
        plan, order = (self.plan, self.order)
        loss, grad = order.done(pl.pallas_call(partial(contrast_kernel, plan.reps, plan.depth, self.queries // 4), out_shape=(shape((32, 1), F32), shape((32, D), F32)), in_specs=[smem()] + [vmem()] * plan.reps, out_specs=(vmem(), vmem()), scratch_shapes=[pltpu.VMEM((16, D), F32)], compiler_params=params(40), name='contrast', cost_estimate=cost(2))(order.where, *self.parts))
        at = order.where[2] * self.queries
        return (lax.dynamic_slice(loss, (at, 0), (self.queries, 1))[:, 0], grad)


def norm_back(grad, hat, rstd, gain):
    scaled = grad * gain
    a = jnp.mean(scaled, -1, keepdims=True)
    b = jnp.mean(scaled * hat, -1, keepdims=True)
    return rstd * (scaled - a - hat * b)


def col_sum(v):
    return jnp.sum(v, 0, keepdims=True)


def top_kernel(where_ref, cot_ref, cls_ref, hat_ref, rstd_ref, vec_ref, act_ref, second_ref, gs_ref, sums_ref, *rest):
    parts, full_ref = (rest[:-1], rest[-1])

    @pl.when(pl.program_id(0) == 0)
    def norm():
        groups = TILE // 32
        at_first = lax.broadcasted_iota(jnp.int32, (groups, 32, D), 1) == 0
        sums_ref[...] = jnp.zeros_like(sums_ref)
        for m in range(0, cot_ref.shape[0], TILE):
            rows = slice(m, m + TILE)
            cls = cls_ref[m // 32:(m + TILE) // 32, :].reshape(groups, 1, D)
            dout = cot_ref[rows, :].astype(F32) + jnp.where(at_first, cls, 0.0).reshape(TILE, D)
            hat = hat_ref[rows, :]
            grad = norm_back(dout, hat, rstd_ref[rows, :], vec_ref[11:12, :])
            second_ref[rows, :] = grad
            gs = grad.astype(BF)
            gs_ref[rows, :] = gs
            sums_ref[0:1, :] += col_sum(gs.astype(F32))
            sums_ref[1:2, :] += col_sum(dout)
            sums_ref[2:3, :] += col_sum(dout * hat)
    full_ref[...] = t_dot(act_ref[...], gs_ref[...]).astype(BF)
    halves(parts, where_ref[1], full_ref)


def top(plan, order, cot, cls_grad, hat2, rstd2, vec, act):
    rows = cot.shape[0]
    part = D // plan.reps
    second, gs, sums, *parts = pl.pallas_call(top_kernel, grid=(FF // D,), out_shape=(far((rows, D), F32), shape((rows, D), BF), shape((8, D), F32)) + (shape((FF, part), BF),) * plan.reps, in_specs=[smem(), vmem(), still(cls_grad.shape), vmem(), vmem(), still(vec.shape), pl.BlockSpec((rows, D), lambda i: (0, i))], out_specs=[still((rows, D)), still((rows, D)), still((8, D))] + [rows_at(part, D)] * plan.reps, scratch_shapes=[pltpu.VMEM((D, D), BF)], compiler_params=params(28), name='top', cost_estimate=behind(11))(order.where, cot, cls_grad, hat2, rstd2, vec, act)
    return (second, gs, sums, parts)


def gelu_back_kernel(reps, column, where_ref, gs_ref, w_ref, slope_ref, norm_ref, up_ref, acc_ref, sums_ref, *rest):
    parts, gu_ref = (rest[:-1], rest[-1])
    i = pl.program_id(0)
    total = jnp.zeros((1, D), F32)
    for m in range(0, gs_ref.shape[0], TILE):
        rows = slice(m, m + TILE)
        gu = (dot_t(gs_ref[rows, :], w_ref[...]) * slope_ref[rows, :].astype(F32)).astype(BF)
        gu_ref[rows, :] = gu
        total = total + col_sum(gu.astype(F32))
    sums_ref[pl.ds(column(i, where_ref), 1), :] = total
    for m in range(0, gs_ref.shape[0], TILE):
        rows = slice(m, m + TILE)
        before = jnp.where(i == 0, 0.0, acc_ref[rows, :])
        acc_ref[rows, :] = before + dot_t(gu_ref[rows, :], up_ref[...])
    grad = t_dot(norm_ref[...], gu_ref[...]).astype(BF)
    per = FF // D // reps
    for q in range(reps):

        @pl.when(i // per == reps - 1 - q)
        def put(q=q):
            parts[q][...] = grad


def gelu_back(plan, order, gs, w_down, slope, norm, w_up):
    rows = gs.shape[0]
    reps = plan.reps
    per = FF // D // reps

    def column(i, table):
        return (table[1] ^ reps - 1 - i // per) * per + i % per

    def held(q):
        return pl.BlockSpec((D, D), lambda i, table: (0, jnp.clip(i - (reps - 1 - q) * per, 0, per - 1)))
    acc, sums, *parts = pl.pallas_call(partial(gelu_back_kernel, reps, column), out_shape=(shape((rows, D), F32), shape((8, D), F32)) + (shape((D, FF // reps), BF),) * reps, grid_spec=pltpu.PrefetchScalarGridSpec(num_scalar_prefetch=1, grid=(FF // D,), in_specs=[vmem(), pl.BlockSpec((D, D), lambda i, table: (column(i, table), 0)), pl.BlockSpec((rows, D), lambda i, table: (0, column(i, table))), vmem(), pl.BlockSpec((D, D), lambda i, table: (0, column(i, table)))], out_specs=[still((rows, D)), still((8, D))] + [held(q) for q in range(reps)], scratch_shapes=[pltpu.VMEM((rows, D), BF)]), compiler_params=params(28), name='gelu_back', cost_estimate=behind(20))(order.where, gs, stay(w_down), stay(slope), norm, stay(w_up))
    return (acc, sums, parts)


def hidden_back_kernel(where_ref, acc_ref, second_ref, hat_ref, rstd_ref, w_ref, vec_ref, go_ref, ga_ref, sums_ref):

    @pl.when(pl.program_id(0) == 0)
    def clear():
        sums_ref[...] = jnp.zeros_like(sums_ref)
    grad = acc_ref[...] + second_ref[...]
    hat = hat_ref[...]
    hidden = norm_back(grad, hat, rstd_ref[...], vec_ref[10:11, :])
    go = hidden.astype(BF)
    go_ref[...] = go
    sums_ref[0:1, :] += col_sum(go.astype(F32))
    sums_ref[1:2, :] += col_sum(grad)
    sums_ref[2:3, :] += col_sum(grad * hat)
    ga_ref[...] = dot_t(go, w_ref[...]).astype(BF)


def hidden_back(order, acc, second, hat, rstd, w_one, vec):
    rows = acc.shape[0]
    return pl.pallas_call(hidden_back_kernel, grid=(rows // TILE,), out_shape=(shape((rows, D), BF), shape((rows, D), BF), shape((8, D), F32)), in_specs=[smem()] + [rows_at(D)] * 3 + [rows_at(1), still((D, D), (0, AT_OUT // D)), still(vec.shape)], out_specs=[rows_at(D), rows_at(D), still((8, D))], compiler_params=params(20), name='hidden_back', cost_estimate=behind(5))(order.where, acc, stay(second), stay(hat), stay(rstd), stay(w_one), vec)


def pair_back(pair, block, rows, ga_ref, proj_ref, probs_ref, low, high):
    q = proj_ref[rows, pair * 128:(pair + 1) * 128]
    k = proj_ref[rows, D + pair * 128:D + (pair + 1) * 128]
    v = proj_ref[rows, 2 * D + pair * 128:2 * D + (pair + 1) * 128]
    a = ga_ref[rows, pair * 128:(pair + 1) * 128]
    a2 = jnp.concatenate([a * low, a * high], 0)
    q2 = jnp.concatenate([q * low, q * high], 0)
    k2 = jnp.concatenate([k * low, k * high], 0)
    p = probs_ref[block, pair]
    dp = dot_t(v, a2)
    pf = p.astype(F32)
    ds = (pf * (dp - jnp.sum(pf * dp, 0, keepdims=True)) * HEAD ** (-0.5)).astype(BF)
    tall = jnp.concatenate([ds[:, :BLOCK], ds[:, BLOCK:]], 0)
    return (t_dot(tall, k2).astype(BF), dot(ds, q2).astype(BF), dot(p, a2).astype(BF))


def heads_back(first, count, at, ga_ref, proj_ref, probs_ref, gp_ref):
    low, high = lane_masks()
    for block in range(256 // BLOCK):
        rows = slice(block * BLOCK, (block + 1) * BLOCK)
        to = pl.ds(pl.multiple_of(at + block * BLOCK, BLOCK), BLOCK)
        for j in range(count):
            three = pair_back(first + j, block, rows, ga_ref, proj_ref, probs_ref, low, high)
            for n, grad in enumerate(three):
                lane = (n * count + j) * 128
                gp_ref[to, lane:lane + 128] = grad


def attend_back_kernel(first, count, where_ref, ga_ref, proj_ref, probs_ref, gp_ref):
    heads_back(first, count, 0, ga_ref, proj_ref, probs_ref, gp_ref)


def tile_specs(first):
    per = 256 // BLOCK
    return [pl.BlockSpec((256, D), lambda i: (i + first, 0)), pl.BlockSpec((256, 3 * D), lambda i: (i + first, 0)), pl.BlockSpec((per, PAIRS, BLOCK, 2 * BLOCK), lambda i: (i + first, 0, 0, 0))]


def attend_back(order, first, count, ga, proj, probs, rows, weight=1.0):
    wide = 3 * count * 128
    return pl.pallas_call(partial(attend_back_kernel, first, count), grid=(rows // 256,), out_shape=shape((rows, wide), BF), in_specs=[smem()] + tile_specs(0), out_specs=rows_at(wide, 256), compiler_params=params(20), name='attend_back', cost_estimate=behind(10 * count * rows / 4096 * weight))(order.where, ga, stay(proj), stay(probs))


def both_rows(x_ref, y_ref, near_ref, far_ref):
    return (t_dot(x_ref[...], near_ref[...]) + t_dot(y_ref[...], far_ref[...])).astype(BF)


def first_weights_kernel(where_ref, x_ref, y_ref, near_ref, far_ref, attn_ref, go_ref, *rest):
    parts, full_ref = (rest[:-1], rest[-1])
    full_ref[:, :D] = t_dot(attn_ref[...], go_ref[...]).astype(BF)
    end = D + near_ref.shape[1]
    full_ref[:, D:end] = both_rows(x_ref, y_ref, near_ref, far_ref)
    if end < full_ref.shape[1]:
        full_ref[:, end:] = jnp.zeros((D, full_ref.shape[1] - end), BF)
    halves(parts, where_ref[1], full_ref)


def last_weights_kernel(count, where_ref, x_ref, y_ref, near_ref, far_ref, first_near_ref, first_far_ref, up_ref, top_ref, hidden_ref, *rest):
    parts, full_ref, lines_ref = (rest[:-2], rest[-2], rest[-1])
    part = D - count * 128
    wide = count * 128
    full_ref[:, :3 * part] = both_rows(x_ref, y_ref, near_ref, far_ref)

    def sums(j, width, a_ref, b_ref):
        lanes = slice(j * width, (j + 1) * width)
        return col_sum(a_ref[:, lanes].astype(F32)) + col_sum(b_ref[:, lanes].astype(F32))
    lines_ref[...] = jnp.zeros_like(lines_ref)
    for n, j in ((0, 0), (1, 2)):
        lines_ref[n:n + 1, :wide] = sums(j, wide, first_near_ref, first_far_ref)
        lines_ref[n:n + 1, wide:] = sums(j, part, near_ref, far_ref)
    lines_ref[2:4, :] = hidden_ref[0:2, :]
    lines_ref[4:8, :] = up_ref[0:4, :]
    lines_ref[8:10, :] = top_ref[0:2, :]
    lines_ref[10:11, :] = hidden_ref[2:3, :]
    lines_ref[11:12, :] = top_ref[2:3, :]
    full_ref[:, 3 * part:3 * part + 128] = jnp.transpose(lines_ref[...]).astype(BF)
    if 3 * part + 128 < full_ref.shape[1]:
        full_ref[:, 3 * part + 128:] = jnp.zeros((D, full_ref.shape[1] - 3 * part - 128), BF)
    halves(parts, where_ref[1], full_ref)


def weights(plan, order, kernel, name, us, total, scratch, *args):
    part = total // plan.reps
    return pl.pallas_call(kernel, grid=(1,), out_shape=(shape((D, part), BF),) * plan.reps, in_specs=[smem()] + [vmem() for a in args], out_specs=[still((D, part))] * plan.reps, scratch_shapes=[pltpu.VMEM((D, total), BF)] + scratch, compiler_params=params(28), name=name, cost_estimate=behind(us))(order.where, *args)


def gx_of(count, a_ref, b_ref, w_ref, hidden):
    hidden = hidden.astype(F32)
    ca, cb = (count * 128, D - count * 128)
    for j in range(3):
        hidden = hidden + dot_t(a_ref[:, j * ca:(j + 1) * ca], w_ref[:, j * D:j * D + ca])
        hidden = hidden + dot_t(b_ref[:, j * cb:(j + 1) * cb], w_ref[:, j * D + ca:(j + 1) * D])
    return hidden


def far_back_kernel(count, where_ref, ga_ref, proj_ref, probs_ref, w_ref, hidden_ref, a_ref, b_ref, far_ref):
    heads_back(0, count, 0, ga_ref, proj_ref, probs_ref, a_ref)
    heads_back(count, PAIRS - count, 0, ga_ref, proj_ref, probs_ref, b_ref)
    far_ref[...] = gx_of(count, a_ref, b_ref, w_ref, hidden_ref[...]).astype(BF)


def far_back(order, count, ga, proj, probs, w_one, hidden):
    rows = ga.shape[0] // 2
    steps = rows // 256
    wide = 3 * count * 128
    return pl.pallas_call(partial(far_back_kernel, count), grid=(steps,), out_shape=(shape((rows, wide), BF), shape((rows, 3 * D - wide), BF), shape((rows, D), BF)), in_specs=[smem()] + tile_specs(steps) + [still((D, 3 * D)), pl.BlockSpec((256, D), lambda i: (i + steps, 0))], out_specs=[rows_at(wide, 256), rows_at(3 * D - wide, 256), rows_at(D, 256)], compiler_params=params(24), name='far_back', cost_estimate=behind(11))(order.where, ga, stay(proj), stay(probs), stay(w_one), stay(hidden))


def token_back_kernel(count, where_ref, a_ref, b_ref, w_ref, hidden_ref, own_ref):
    own_ref[...] = gx_of(count, a_ref, b_ref, w_ref, hidden_ref[...])


def token_back(order, count, ga, gb, w_one, hidden):
    rows = gb.shape[0]
    return pl.pallas_call(partial(token_back_kernel, count), grid=(rows // TILE,), out_shape=shape((rows, D), F32), in_specs=[smem(), rows_at(ga.shape[1]), rows_at(gb.shape[1]), still((D, 3 * D)), rows_at(D)], out_specs=rows_at(D), compiler_params=params(24), name='token_back', cost_estimate=behind(4))(order.where, ga, gb, stay(w_one), stay(hidden))


def on_device(plan, query_tokens, passage_tokens, query_cot, passage_cot, positives, w_qkv, w_out, w_up, w_down, biases, gains):
    me = lax.axis_index('dp')
    core = lax.axis_index('rep')
    tower = me >> 2 & 1
    span = jnp.where(tower == 0, query_tokens.shape[1], passage_tokens.shape[1])
    where = jnp.stack([me, core, tower, span]).astype(jnp.int32)
    swap = plan.along(1)

    def exchange(a, b, *others):
        a, b = (a.reshape(-1, D), b.reshape(-1, D))
        away = jnp.where(tower == 0, b, a)
        return (jnp.where(tower == 0, a, b), send(after(away, *others) if others else away, swap))

    def merged(own, back):
        a = jnp.where(tower == 0, own, back)
        b = jnp.where(tower == 0, back, own)
        return (a.reshape(query_tokens.shape), b.reshape(passage_tokens.shape))
    order = Order(where)
    mine, other, mine2, other2, mine3, other3 = shards_of(plan, order, w_qkv, w_out, biases, gains, w_up, w_down)
    z1 = gather_line(plan, mine, other)
    both2 = jnp.concatenate([mine2, send(other2, swap)], 0)
    both3 = jnp.concatenate([mine3, send(other3, swap)], 0)
    z2 = gather_steps(plan, both2, z1)
    p1 = gather_plane(plan, z1, z2, both3)
    z3 = gather_steps(plan, both3, z2)
    x_mine, x_got = exchange(query_tokens, passage_tokens, z3)
    w_one = gather_cores(plan, order, p1)
    p2 = gather_plane(plan, z2)
    p3 = gather_plane(plan, after(z3, p2[0]))
    order.done(p2[0])
    first = order.done(attend(order, x_mine, w_one, 0))
    proj, probs, attn, hat1, rstd1, norm, vec, cls_b = order.done(attend(order, x_got, w_one, 1, first[:6]))
    w_two = gather_cores(plan, order, tuple((after(b, first[6]) for b in p2)))
    half_up = order.done(up(order, norm, w_two, vec, 0))
    w_three = gather_cores(plan, order, tuple((after(b, norm) for b in p3)))
    msg = first_rows(order, first[7], cls_b, w_two, w_three, vec, positives)
    cot_mine, cot_got = exchange(query_cot, passage_cot, norm)
    loss = Contrast(plan, order, msg, positives.shape[0])
    act, slope = order.done(up(order, norm, w_two, vec, 1, half_up))
    loss.pack()
    cot = jnp.concatenate([cot_mine, cot_got], 0)
    out_own, out_far, hat2, rstd2 = order.done(down(order, act, w_three, hat1, vec))
    out_back = send(out_far, swap)
    loss.join()
    order.done(cot)
    query_loss, cls_grad = loss.loss()
    second, gs, sums_top, g_down = order.done(top(plan, order, cot, cls_grad, hat2, rstd2, vec, act))
    down_part = Scatter(plan, order, g_down, w_down.shape[1])
    acc, sums_up, g_up = order.done(gelu_back(plan, order, gs, w_three, slope, norm, w_two))
    up_part = Scatter(plan, order, g_up, w_up.shape[1])
    order.done(out_back)
    down_part.one()
    go, ga, sums = order.done(hidden_back(order, acc, second, hat1, rstd1, w_one, vec))
    up_part.one()
    split = 4
    half = ga.shape[0] // 2
    hidden = go
    far_a, far_b, gx_far = order.done(far_back(order, split, ga, proj, probs, w_one, go))
    gx_back = send(gx_far, swap)
    near_a = order.done(attend_back(order, 0, split, ga, proj, probs, half))
    total = wide(3 * split * 128 + D, plan.reps)
    args = (x_mine, x_got, near_a, far_a, stay(attn), go)
    g_a = order.done(weights(plan, order, first_weights_kernel, 'first_weights', 5, total, [], *args))
    a_part = Scatter(plan, order, g_a, w_qkv.shape[1])
    down_part.two()
    up_part.two()
    order.done(gx_back)
    near_b = order.done(attend_back(order, split, PAIRS - split, ga, proj, probs, half))
    down_part.three()
    a_part.one()
    up_part.three()
    total = wide(3 * (D - split * 128) + 128, plan.reps)
    scratch = [pltpu.VMEM((128, D), F32)]
    args = (x_mine, x_got, near_b, far_b, near_a, far_a, sums_up, sums_top, sums)
    kernel = partial(last_weights_kernel, split)
    g_b = order.done(weights(plan, order, kernel, 'last_weights', 4, total, scratch, *args))
    b_part = Scatter(plan, order, g_b, w_qkv.shape[1])
    gx_own = order.done(token_back(order, split, near_a, near_b, w_one, go))
    a_part.two()
    b_part.one()
    down_part.four()
    up_part.four()
    a_part.three()
    b_part.two()
    down_part.last()
    up_part.last()
    a_part.four()
    b_part.three()
    grad_down, = finish(plan, order, [down_part], [[(0, D, 0, 0)]], [w_down.shape])
    grad_up, = finish(plan, order, [up_part], [[(0, FF, 0, 0)]], [w_up.shape])
    b_part.four()
    a_part.last()
    b_part.last()
    query_out, passage_out = merged(out_own, after(out_back, b_part.out))
    query_grad, passage_grad = merged(gx_own, after(gx_back, b_part.out).astype(F32))
    qa, qb = (split * 128, D - split * 128)
    spans_a = [(0, D, 1, 0)] + [(D + j * qa, qa, 0, j * D) for j in range(3)]
    spans_b = [(j * qb, qb, 0, j * D + qa) for j in range(3)] + [(3 * qb, 128, 2, 0)]
    shapes = [w_qkv.shape, w_out.shape, biases.shape, gains.shape]
    grads = finish(plan, order, [a_part, b_part], [spans_a, spans_b], shapes, 2)
    return (query_out, passage_out, query_grad, passage_grad, query_loss, grads[0], grads[1], grad_up, grad_down, grads[2], grads[3])


def solution(mesh):
    plan = Plan(mesh.shape['dp'], mesh.shape['rep'])
    rows = P(('dp', 'rep'), None, None)
    shards = P(None, 'dp', None)
    lanes = P(None, None, 'dp')
    return jax.shard_map(partial(on_device, plan), mesh=mesh, in_specs=(rows,) * 4 + (P(('dp', 'rep'), None),) + (shards,) * 4 + (lanes,) * 2, out_specs=(rows,) * 4 + (P(('dp', 'rep')),) + (shards,) * 4 + (lanes,) * 2, check_vma=False)
```

```python
from functools import partial
import jax
import jax.numpy as jnp
from jax import lax
from jax.experimental import pallas as pl
from jax.experimental.pallas import tpu as pltpu
from jax.sharding import PartitionSpec as P
AXES = ('dp', 'rep')
BF = jnp.bfloat16
F32 = jnp.float32
D = 768
FF = 3072
HEADS = 12
HEAD = 64
PAIRS = HEADS // 2
BLOCK = 128
TILE = 256
EPS = 1e-05
LOSS_WEIGHT = 32.0
MIB = 2 ** 20
AT_OUT = 3 * D
AT_VEC = 4 * D


def smem():
    return pl.BlockSpec(memory_space=pltpu.SMEM)


def vmem():
    return pl.BlockSpec(memory_space=pltpu.VMEM)


def cost(us):
    return pl.CostEstimate(flops=int(us * 1000000000.0), transcendentals=0, bytes_accessed=int(us * 3000000.0))


def behind(us):
    return cost(4.0 * us)


def params(mib):
    return pltpu.CompilerParams(vmem_limit_bytes=int(mib) * MIB)


def still(shape, at=None):
    index = at if at is not None else (0,) * len(shape)
    return pl.BlockSpec(shape, lambda i, *_: index, pipeline_mode=pl.Buffered(1))


def rows_at(width, rows=TILE):
    return pl.BlockSpec((rows, width), lambda i, *_: (i, 0))


def shape(dims, dtype):
    return jax.ShapeDtypeStruct(dims, dtype)


def far(dims, dtype):
    return pltpu.HBM(dims, dtype)


def stay(v):
    return pltpu.with_memory_space_constraint(v, pltpu.HBM)


def after(v, *others):
    return lax.optimization_barrier((v,) + others)[0]


class Order:
    def __init__(self, where):
        self.where = where

    def done(self, out):
        self.where = after(self.where, out)
        return out


def in_vmem(kernel, name, us, outs, *args, mib=24):
    return pl.pallas_call(kernel, out_shape=tuple((shape(*o) for o in outs)), in_specs=[smem() if a.ndim == 1 else vmem() for a in args], out_specs=tuple((vmem() for _ in outs)), compiler_params=params(mib), name=name, cost_estimate=cost(us))(*args)


def wide(width, reps):
    unit = 128 * reps
    return -(-width // unit) * unit


def by_core(core, reps, width, move):
    if width % 128 == 0:
        move(pl.ds(pl.multiple_of(core * width, 128), width))
        return
    for c in range(reps):

        @pl.when(core == c)
        def one(c=c):
            move(slice(c * width, (c + 1) * width))


def halves(refs, core, source):
    width = refs[0].shape[1]
    for q, ref in enumerate(refs):

        def move(lanes, ref=ref):
            ref[...] = source[:, lanes]
        by_core(core ^ q, len(refs), width, move)


def send(v, pairs):
    return lax.ppermute(v, AXES, pairs)


class Plan:
    def __init__(self, n, reps):
        self.n, self.reps, self.depth = (n, reps, n // 4)

    def pairs(self, move):
        return [(d * self.reps + r, (d ^ move(r)[0]) * self.reps + (r ^ move(r)[1])) for d in range(self.n) for r in range(self.reps)]

    def along(self, k):
        return self.pairs(lambda r: (4 * k, 0))

    def first(self):
        return self.pairs(lambda r: (1 + r % 2, 0))

    def second(self):
        return self.pairs(lambda r: (2 - r % 2, 0))

    def sibling(self, q):
        return self.pairs(lambda r: (0, q))


def assemble_kernel(depth, reps, width, where_ref, *refs):
    bufs, out = (refs[:2 * reps], refs[2 * reps])
    me, core = (where_ref[0], where_ref[1])
    for q in range(reps):
        owner = core ^ q
        p1 = 1 + owner % 2
        p2 = 2 - owner % 2

        def move(lanes, q=q, p1=p1, p2=p2):
            for b in range(2):
                for f in range(2):
                    for k in range(depth):
                        dst = me ^ b * p2 ^ f * p1 ^ 4 * k
                        out[pl.ds(dst, 1), :, lanes] = bufs[q * 2 + b][pl.ds(f * depth + k, 1)]
        by_core(owner, reps, width, move)


def shards_kernel(reps, where_ref, qkv_ref, out_ref, bias_ref, gain_ref, up_ref, down_ref, *rest):
    outs, full_ref = (rest[:-1], rest[-1])
    core, tower = (where_ref[1], where_ref[2])
    spare = full_ref.shape[2] - AT_VEC

    def turned(rows, at):
        i = lax.broadcasted_iota(jnp.int32, (rows.shape[0], spare), 0)
        j = lax.broadcasted_iota(jnp.int32, (rows.shape[0], spare), 1)
        return t_dot(rows.astype(BF), jnp.where(i + at == j, 1.0, 0.0).astype(BF))
    for n in range(2):
        t = pl.ds(tower if n == 0 else 1 - tower, 1)
        full_ref[:, :, :AT_OUT] = qkv_ref[t]
        full_ref[:, :, AT_OUT:AT_VEC] = out_ref[t]
        biases = bias_ref[...].astype(F32)
        biases = jnp.where(tower == n, biases[:, 0, :], biases[:, 1, :])
        gains = gain_ref[t][0].astype(F32)
        full_ref[0, :, AT_VEC:] = (turned(biases, 0) + turned(gains, biases.shape[0])).astype(BF)
        for c, ref in enumerate((full_ref, up_ref, down_ref)):
            put = outs[2 * c + n]

            def move(lanes, ref=ref, put=put, t=t):
                put[...] = ref[:, :, lanes] if ref is full_ref else ref[t, :, lanes]
            by_core(core, reps, put.shape[2], move)


def shards_of(plan, order, w_qkv, w_out, biases, gains, w_up, w_down):
    reps = plan.reps
    one = wide(AT_VEC + 128, reps)
    outs = []
    for rows, width in ((w_qkv.shape[1], one), (w_up.shape[1], FF), (w_down.shape[1], D)):
        outs += [shape((1, rows, width // reps), BF)] * 2
    args = (w_qkv, w_out, biases, gains, w_up, w_down)
    got = pl.pallas_call(partial(shards_kernel, reps), grid=(1,), out_shape=tuple(outs), in_specs=[smem()] + [still(a.shape) for a in args], out_specs=[still(o.shape) for o in outs], scratch_shapes=[pltpu.VMEM((1, w_qkv.shape[1], one), BF)], compiler_params=params(24), name='shards', cost_estimate=cost(2))(order.where, *[stay(a) for a in args])
    return order.done(got)


def join_kernel(where_ref, *refs):
    ins, out_ref = (refs[:-1], refs[-1])
    at = 0
    for ref in ins:
        out_ref[at:at + ref.shape[0]] = ref[...]
        at += ref.shape[0]


def join(order, *bufs):
    total = sum((b.shape[0] for b in bufs))
    outs = (((total,) + bufs[0].shape[1:], bufs[0].dtype),)
    return order.done(in_vmem(join_kernel, 'join', 0.5, outs, order.where, *bufs))[0]


def gather_line(plan, mine, other):
    got = [send(other if k % 2 else mine, plan.along(k)) for k in range(1, plan.depth)]
    return jnp.concatenate([mine] + got, 0)


def gather_steps(plan, both, *others):
    z = both
    k = 2
    while k < plan.depth:
        if others:
            z, others = (after(z, *others), ())
        z = jnp.concatenate([z, send(z, plan.along(k))], 0)
        k *= 2
    return z


def gather_plane(plan, z, *others):
    near = jnp.concatenate([z, send(z, plan.first())], 0)
    if others:
        near = after(near, *others)
    return (near, send(near, plan.second()))


def gather_cores(plan, order, bufs):
    rows, width = bufs[0].shape[1:]
    bufs = list(bufs)
    for q in range(1, plan.reps):
        bufs += [send(b, plan.sibling(q)) for b in bufs[:2]]
    full = pl.pallas_call(partial(assemble_kernel, plan.depth, plan.reps, width), out_shape=jax.ShapeDtypeStruct((plan.n, rows, width * plan.reps), BF), in_specs=[smem()] + [vmem()] * len(bufs), out_specs=vmem(), compiler_params=params(24), name='assemble', cost_estimate=cost(2))(order.where, *bufs)
    order.done(full)
    return full.reshape(plan.n * rows, width * plan.reps)


def add_kernel(depth, where_ref, a_ref, b_ref, s_ref, k_ref):
    me, core = (where_ref[0], where_ref[1])
    p1 = 1 + core % 2
    p2 = 2 - core % 2
    for j in range(4 * depth):
        at = me ^ (1 - j // (2 * depth)) * p1 ^ (1 - j // depth % 2) * p2 ^ 4 * (j % depth)
        o_ref, to = (s_ref, j) if j < 2 * depth else (k_ref, j - 2 * depth)
        o_ref[to] = (a_ref[at].astype(F32) + b_ref[at].astype(F32)).astype(BF)


def two_kernel(where_ref, k_ref, r_ref, s_ref, o_ref):
    q = s_ref.shape[0]
    for j in range(2 * q):
        total = (k_ref[j].astype(F32) + r_ref[j].astype(F32)).astype(BF)
        if j < q:
            s_ref[j] = total
        else:
            o_ref[j - q] = total


def line_kernel(where_ref, k_ref, r_ref, s_ref, o_ref):
    half = o_ref.shape[0]
    for j in range(2 * half):
        total = (k_ref[j].astype(F32) + r_ref[j].astype(F32)).astype(BF)
        if j < half:
            o_ref[j] = total
        else:
            s_ref[j - half] = total


def last_kernel(where_ref, own_ref, got_ref, out):
    tower = where_ref[2]
    out[pl.ds(tower, 1)] = own_ref[...]
    out[pl.ds(1 - tower, 1)] = got_ref[...]


def plus(a, b):
    return (a.astype(F32) + b.astype(F32)).astype(BF)


class Scatter:
    def __init__(self, plan, order, parts, rows):
        self.plan, self.order, self.rows = (plan, order, rows)
        self.width = parts[0].shape[1]
        parts = [p.reshape(plan.n, rows, self.width) for p in parts]
        self.own = parts[0]
        got = [send(parts[q], plan.sibling(q)) for q in range(1, plan.reps)]
        self.rest = got[0]
        for o in got[1:]:
            self.rest = plus(self.rest, o)

    def run(self, kernel, name, us, outs, *args):
        return self.order.done(in_vmem(kernel, name, us, outs, self.order.where, *args))

    def one(self):
        plan = self.plan
        n = plan.n
        whole = (n, self.rows, self.width)
        half = shape((n // 2, self.rows, self.width), BF)
        hs, self.hk = self.order.done(pl.pallas_call(partial(add_kernel, plan.depth), out_shape=(half, half), in_specs=[smem(), vmem(), vmem()], out_specs=(vmem(), vmem()), compiler_params=params(24), name='pick_add', cost_estimate=behind(3))(self.order.where, self.own, self.rest))
        self.r1 = send(hs, plan.first())
        return

    def two(self):
        quarter = ((self.plan.n // 4, self.rows, self.width), BF)
        ks, self.kk = self.run(two_kernel, 'add_two', 1, (quarter, quarter), self.hk, self.r1)
        self.r2 = send(ks, self.plan.second())

    def line(self):
        n = self.kk.shape[0] // 2
        half = ((n, self.rows, self.width), BF)
        out, self.kk = self.run(line_kernel, 'add_line', 1, (half, half), self.kk, self.r2)
        self.r2 = send(out, self.plan.along(n))
        return out

    def three(self):
        self.out = self.line()

    def four(self):
        while self.kk.shape[0] > 1:
            self.out = self.line()

    def last(self):
        plan = self.plan
        outs = (((2, self.rows, self.width), BF),)
        pair, = self.run(last_kernel, 'add_last', 1, outs, self.kk, self.r2)
        self.ends = [pair] + [send(pair, plan.sibling(q)) for q in range(1, plan.reps)]


def finish_kernel(reps, spans, vec, where_ref, *refs):
    chunks = len(spans)
    ins, outs = (refs[:chunks * reps], refs[chunks * reps:])
    core = where_ref[1]
    for c in range(chunks):
        parts = ins[c * reps:(c + 1) * reps]
        width = parts[0].shape[2]
        for q in range(reps):
            for mine in range(reps):

                @pl.when(core ^ q == mine)
                def copy(c=c, parts=parts, q=q, mine=mine):
                    for at, size, out, to in spans[c]:
                        low, high = (max(at, mine * width), min(at + size, (mine + 1) * width))
                        if low >= high:
                            continue
                        lanes = slice(low - mine * width, high - mine * width)
                        if out == vec:
                            turn(parts[q], lanes, low - at, outs[out], outs[out + 1])
                        else:
                            outs[out][:, :, to + low - at:to + high - at] = parts[q][:, :, lanes].astype(F32)


def turn(part_ref, lanes, at, bias_ref, gain_ref):
    for t in range(2):
        columns = part_ref[t, :, lanes]
        count = bias_ref.shape[0]
        for start, n in ((0, count), (count, gain_ref.shape[1])):
            i = lax.broadcasted_iota(jnp.int32, (n, columns.shape[1]), 0)
            j = lax.broadcasted_iota(jnp.int32, (n, columns.shape[1]), 1)
            rows = dot_t(jnp.where(i + start == j + at, 1.0, 0.0).astype(BF), columns)
            if start == 0:
                bias_ref[:, t, :] = rows
            else:
                gain_ref[t] = rows


def finish(plan, order, chunks, spans, shapes, vec=-1):
    outs = tuple(((s, F32) for s in shapes))
    args = [p for c in chunks for p in c.ends]
    kernel = partial(finish_kernel, plan.reps, spans, vec)
    return order.done(in_vmem(kernel, 'finish', 2, outs, order.where, *args))


def dot(a, b):
    return jnp.dot(a, b, preferred_element_type=F32)


def dot_t(a, b):
    return lax.dot_general(a, b, (((1,), (1,)), ((), ())), preferred_element_type=F32)


def t_dot(a, b):
    return lax.dot_general(a, b, (((0,), (0,)), ((), ())), preferred_element_type=F32)


def normalize(h):
    center = h - jnp.mean(h, -1, keepdims=True)
    rstd = lax.rsqrt(jnp.mean(center * center, -1, keepdims=True) + EPS)
    return (center * rstd, rstd)


def lane_masks():
    lane = lax.broadcasted_iota(jnp.int32, (1, 2 * HEAD), 1)
    low = (lane < HEAD).astype(F32).astype(BF)
    return (low, (1.0 - low.astype(F32)).astype(BF))


def attend_kernel(part, where_ref, x_ref, w_ref, *rest):
    proj_ref, probs_ref, attn_ref, hat_ref, rstd_ref, norm_ref, vec_ref, cls_ref, bias_ref = rest[-9:]

    @pl.when(pl.program_id(0) == 0)
    def prepare():
        vec_ref[...] = jnp.transpose(w_ref[:, AT_VEC:AT_VEC + 128].astype(F32))
        span = where_ref[3]
        row = lax.broadcasted_iota(jnp.int32, (BLOCK, 2 * BLOCK), 0)
        col = lax.broadcasted_iota(jnp.int32, (BLOCK, 2 * BLOCK), 1) % BLOCK
        bias_ref[...] = jnp.where(row ^ col < span, 0.0, -1e+30)
    x = x_ref[...]
    for j in range(3):
        part = dot(x, w_ref[:, j * D:(j + 1) * D])
        if j != 1:
            part = part + vec_ref[j // 2:j // 2 + 1, :]
        proj_ref[:, j * D:(j + 1) * D] = part.astype(BF)
    low, high = lane_masks()
    bias = bias_ref[...]
    for blk in range(256 // BLOCK):
        rows = slice(blk * BLOCK, (blk + 1) * BLOCK)
        for pair in range(PAIRS):
            lanes = slice(pair * 128, (pair + 1) * 128)
            q = proj_ref[rows, lanes]
            k = proj_ref[rows, D + pair * 128:D + (pair + 1) * 128]
            v = proj_ref[rows, 2 * D + pair * 128:2 * D + (pair + 1) * 128]
            s = dot_t(k, jnp.concatenate([q * low, q * high], 0)) * HEAD ** (-0.5) + bias
            e = jnp.exp(s - jnp.max(s, 0, keepdims=True))
            p = (e * (1.0 / jnp.sum(e, 0, keepdims=True))).astype(BF)
            probs_ref[blk, pair] = p
            tall = jnp.concatenate([p[:, :BLOCK], p[:, BLOCK:]], 0)
            attn_ref[rows, lanes] = t_dot(tall, jnp.concatenate([v * low, v * high], 0)).astype(BF)
    hidden = x.astype(F32) + (dot(attn_ref[...], w_ref[:, AT_OUT:AT_VEC]) + vec_ref[2:3, :])
    hat, rstd = normalize(hidden)
    hat_ref[...] = hat
    rstd_ref[...] = rstd
    norm = hat * vec_ref[10:11, :] + vec_ref[3:4, :]
    norm_ref[...] = norm.astype(BF)
    for j in range(8):
        cls_ref[j:j + 1, :] = norm[32 * j:32 * j + 1, :]


def attend(order, x, w_one, part, before=()):
    rows = 2 * x.shape[0]
    per = 256 // BLOCK
    steps = rows // 256 // 2
    first = part * steps

    def here(width):
        return pl.BlockSpec((256, width), lambda i: (i + first, 0))
    return pl.pallas_call(partial(attend_kernel, part), grid=(steps,), out_shape=(far((rows, 3 * D), BF), far((rows // BLOCK, PAIRS, BLOCK, 2 * BLOCK), BF), far((rows, D), BF), far((rows, D), F32), far((rows, 1), F32), far((rows, D), BF), shape((128, D), F32), shape((rows // 64, D), F32)), in_specs=[smem(), rows_at(D, 256), vmem()] + [pl.BlockSpec(memory_space=pl.ANY)] * len(before), out_specs=[here(3 * D), pl.BlockSpec((per, PAIRS, BLOCK, 2 * BLOCK), lambda i: (i + first, 0, 0, 0)), here(D), here(D), here(1), here(D), still((128, D)), rows_at(D, 8)], scratch_shapes=[pltpu.VMEM((BLOCK, 2 * BLOCK), F32)], input_output_aliases={3 + j: j for j in range(len(before))}, compiler_params=params(24), name='attend', cost_estimate=cost(7))(order.where, x, w_one, *[b for b in before])


def gelu_pair(u):
    phi = 0.5 + 0.5 * lax.erf(u * 2 ** (-0.5))
    return (u * phi, phi + u * (jnp.exp(-0.5 * u * u) * (2 * jnp.pi) ** (-0.5)))


def up_kernel(first, where_ref, norm_ref, w_ref, vec_ref, *rest):
    act_ref, slope_ref = rest[-2:]
    bias = vec_ref[pl.ds(4 + first + pl.program_id(0), 1), :]
    for m in range(0, norm_ref.shape[0], 256):
        rows = slice(m, m + 256)
        act, slope = gelu_pair(dot(norm_ref[rows, :], w_ref[...]) + bias)
        act_ref[rows, :] = act.astype(BF)
        slope_ref[rows, :] = slope.astype(BF)


def up(order, norm, w_up, vec, part, before=()):
    rows = norm.shape[0]
    steps = FF // D // 2
    first = part * steps
    col = pl.BlockSpec((rows, D), lambda i: (0, i + first))
    return pl.pallas_call(partial(up_kernel, first), grid=(steps,), out_shape=(shape((rows, FF), BF), far((rows, FF), BF)), in_specs=[smem(), still(norm.shape), pl.BlockSpec((D, D), lambda i: (0, i + first)), still(vec.shape)] + [pl.BlockSpec(memory_space=pl.ANY)] * len(before), out_specs=[col, col], input_output_aliases={4 + j: j for j in range(len(before))}, compiler_params=params(24), name='up', cost_estimate=cost(8))(order.where, norm, w_up, vec, *[b for b in before])


def down_kernel(where_ref, act_ref, w_ref, hat_ref, vec_ref, own_ref, far_ref, hat2_ref, rstd2_ref):
    normed = hat_ref[...] * vec_ref[10:11, :] + vec_ref[3:4, :]
    second = normed + (dot(act_ref[...], w_ref[...]) + vec_ref[8:9, :])
    hat, rstd = normalize(second)
    hat2_ref[...] = hat
    rstd2_ref[...] = rstd
    out = (hat * vec_ref[11:12, :] + vec_ref[9:10, :]).astype(BF)
    half = pl.num_programs(0) // 2

    @pl.when(pl.program_id(0) < half)
    def near():
        own_ref[...] = out

    @pl.when(pl.program_id(0) >= half)
    def away():
        far_ref[...] = out


def down(order, act, w_down, hat, vec):
    rows = act.shape[0]
    half = rows // 256 // 2
    near = pl.BlockSpec((256, D), lambda i: (jnp.minimum(i, half - 1), 0))
    away = pl.BlockSpec((256, D), lambda i: (jnp.maximum(i - half, 0), 0))
    return pl.pallas_call(down_kernel, grid=(rows // 256,), out_shape=(far((rows // 2, D), BF), shape((rows // 2, D), BF), shape((rows, D), F32), shape((rows, 1), F32)), in_specs=[smem(), rows_at(FF, 256), vmem(), rows_at(D, 256), still(vec.shape)], out_specs=[near, away, rows_at(D, 256), rows_at(1, 256)], compiler_params=params(24), name='down', cost_estimate=cost(8))(order.where, act, w_down, stay(hat), vec)


def first_kernel(where_ref, a_ref, b_ref, up_ref, down_ref, vec_ref, marks_ref, msg_ref):
    norm = jnp.concatenate([a_ref[...], b_ref[...]], 0)
    second = norm + vec_ref[8:9, :]
    wide = norm.astype(BF)
    for j in range(FF // D):
        u = dot(wide, up_ref[:, j * D:(j + 1) * D]) + vec_ref[4 + j:5 + j, :]
        second = second + dot(gelu_pair(u)[0].astype(BF), down_ref[j * D:(j + 1) * D, :])
    hat, _ = normalize(second)
    msg_ref[:, :D] = (hat * vec_ref[11:12, :] + vec_ref[9:10, :]).astype(BF)
    marks = marks_ref[...].astype(F32)
    pad = jnp.zeros((32 - marks.shape[0], marks.shape[1]), F32)
    msg_ref[:, D:] = jnp.concatenate([marks, pad], 0).astype(BF)


def first_rows(order, a, b, w_up, w_down, vec, positives):
    outs = (((32, D + positives.shape[1]), BF),)
    return order.done(in_vmem(first_kernel, 'first_rows', 4, outs, order.where, a, b, w_up, w_down, vec, positives))[0]


def pack_kernel(per, where_ref, *refs):
    msgs, out_ref = (refs[:-1], refs[-1])
    queries = per * 4
    pick_row = lax.broadcasted_iota(jnp.int32, (16, 32), 0)
    pick_col = lax.broadcasted_iota(jnp.int32, (16, 32), 1)
    pick = jnp.where((pick_col == pick_row * (32 // (2 * per))) & (pick_row < 2 * per), 1.0, 0.0).astype(BF)
    for n in range(len(msgs) // 2):
        for tower in range(2):

            @pl.when(where_ref[2] == tower)
            def put(n=n, tower=tower):
                zero, one = (msgs[2 * n + tower], msgs[2 * n + 1 - tower])
                out_ref[n, :32, :D] = zero[:, :D]
                out_ref[n, :queries, D:] = zero[:queries, D:]
                out_ref[n, queries:32, D:] = one[:queries, D:]
                out_ref[n, 32:, :D] = dot(pick, one[:, :D]).astype(BF)
                out_ref[n, 32:, D:] = jnp.zeros((16, out_ref.shape[2] - D), BF)


def contrast_kernel(reps, depth, per, where_ref, *refs):
    parts, loss_ref, grad_ref, acc_ref = (refs[:reps], refs[reps], refs[reps + 1], refs[reps + 2])
    me, core, tower = (where_ref[0], where_ref[1], where_ref[2])
    pieces = parts[0].shape[0]
    passages = parts[0].shape[2] - D
    cls_p = jnp.concatenate([part[:, 32:, :D].reshape(pieces * 16, D) for part in parts], 0)
    cols = cls_p.shape[0]
    col = lax.broadcasted_iota(jnp.int32, (passages, cols), 1)
    row = lax.broadcasted_iota(jnp.int32, (passages, cols), 0)
    j, slot = (col // 16, col % 16)
    base = (me | 4) ^ 8 * (j % (depth // 2)) ^ j // (depth // 2) % 4
    owner = jnp.where(slot < per, base, base ^ 4)
    passage = (owner * reps + (core ^ j // (2 * depth))) * per + slot % per
    pick = jnp.where((row == passage) & (slot < 2 * per), 1.0, 0.0).astype(BF)
    valid = lax.broadcasted_iota(jnp.int32, (1, cols), 1) % 16 < 2 * per
    acc_ref[...] = jnp.zeros_like(acc_ref)
    group = min(8, pieces)
    for q, part in enumerate(parts):
        for at in range(0, pieces, group):
            cls_q = part[at:at + group, :32, :D].reshape(group * 32, D)
            marks = dot(part[at:at + group, :32, D:].reshape(group * 32, passages), pick)
            raw = jnp.where(valid, dot_t(cls_q, cls_p) * D ** (-0.5), -1e+30)
            e = jnp.exp(raw - jnp.max(raw, -1, keepdims=True))
            total = jnp.sum(e, -1, keepdims=True)
            me_ = marks * e
            marked = jnp.sum(me_, -1, keepdims=True)
            grad = (LOSS_WEIGHT * (e / total - me_ / marked)).astype(BF)
            acc_ref[...] += t_dot(grad[:, :128], cls_q)[:16] * D ** (-0.5)
            if q == 0 and at == 0:
                loss_ref[...] = (jnp.log(total) - jnp.log(marked))[:32]
                grad_ref[...] = dot(grad[:32], cls_p) * D ** (-0.5)

    @pl.when(tower == 1)
    def passages_own():
        grad_ref[...] = jnp.zeros_like(grad_ref)
        for s in range(2 * per):
            at = s * (32 // (2 * per))
            grad_ref[at:at + 1, :] = acc_ref[s:s + 1, :]


class Contrast:

    def __init__(self, plan, order, msg, queries):
        self.plan, self.order, self.queries = (plan, order, queries)
        self.msgs = [msg] + [send(msg, plan.along(k)) for k in range(1, plan.depth)]

    def pack(self):
        plan = self.plan
        outs = (((plan.depth // 2, 48, self.msgs[0].shape[1]), BF),)
        kernel = partial(pack_kernel, self.queries // 4)
        buf, = self.order.done(in_vmem(kernel, 'pack', 1, outs, self.order.where, *self.msgs))
        self.bufs = [buf] + [send(buf, plan.pairs(lambda r, m=m: (m, 0))) for m in range(1, 4)]

    def join(self):
        plan = self.plan
        buf = join(self.order, *self.bufs)
        self.parts = [buf] + [send(buf, plan.sibling(s)) for s in range(1, plan.reps)]

    def loss(self):
        plan, order = (self.plan, self.order)
        loss, grad = order.done(pl.pallas_call(partial(contrast_kernel, plan.reps, plan.depth, self.queries // 4), out_shape=(shape((32, 1), F32), shape((32, D), F32)), in_specs=[smem()] + [vmem()] * plan.reps, out_specs=(vmem(), vmem()), scratch_shapes=[pltpu.VMEM((16, D), F32)], compiler_params=params(40), name='contrast', cost_estimate=cost(2))(order.where, *self.parts))
        at = order.where[2] * self.queries
        return (lax.dynamic_slice(loss, (at, 0), (self.queries, 1))[:, 0], grad)


def norm_back(grad, hat, rstd, gain):
    scaled = grad * gain
    a = jnp.mean(scaled, -1, keepdims=True)
    b = jnp.mean(scaled * hat, -1, keepdims=True)
    return rstd * (scaled - a - hat * b)


def col_sum(v):
    return jnp.sum(v, 0, keepdims=True)


def top_kernel(where_ref, cot_ref, cls_ref, hat_ref, rstd_ref, vec_ref, act_ref, second_ref, gs_ref, sums_ref, *rest):
    parts, full_ref = (rest[:-1], rest[-1])

    @pl.when(pl.program_id(0) == 0)
    def norm():
        groups = TILE // 32
        at_first = lax.broadcasted_iota(jnp.int32, (groups, 32, D), 1) == 0
        sums_ref[...] = jnp.zeros_like(sums_ref)
        for m in range(0, cot_ref.shape[0], TILE):
            rows = slice(m, m + TILE)
            cls = cls_ref[m // 32:(m + TILE) // 32, :].reshape(groups, 1, D)
            dout = cot_ref[rows, :].astype(F32) + jnp.where(at_first, cls, 0.0).reshape(TILE, D)
            hat = hat_ref[rows, :]
            grad = norm_back(dout, hat, rstd_ref[rows, :], vec_ref[11:12, :])
            second_ref[rows, :] = grad
            gs = grad.astype(BF)
            gs_ref[rows, :] = gs
            sums_ref[0:1, :] += col_sum(gs.astype(F32))
            sums_ref[1:2, :] += col_sum(dout)
            sums_ref[2:3, :] += col_sum(dout * hat)
    full_ref[...] = t_dot(act_ref[...], gs_ref[...]).astype(BF)
    halves(parts, where_ref[1], full_ref)


def top(plan, order, cot, cls_grad, hat2, rstd2, vec, act):
    rows = cot.shape[0]
    part = D // plan.reps
    second, gs, sums, *parts = pl.pallas_call(top_kernel, grid=(FF // D,), out_shape=(far((rows, D), F32), shape((rows, D), BF), shape((8, D), F32)) + (shape((FF, part), BF),) * plan.reps, in_specs=[smem(), vmem(), still(cls_grad.shape), vmem(), vmem(), still(vec.shape), pl.BlockSpec((rows, D), lambda i: (0, i))], out_specs=[still((rows, D)), still((rows, D)), still((8, D))] + [rows_at(part, D)] * plan.reps, scratch_shapes=[pltpu.VMEM((D, D), BF)], compiler_params=params(28), name='top', cost_estimate=behind(11))(order.where, cot, cls_grad, hat2, rstd2, vec, act)
    return (second, gs, sums, parts)


def gelu_back_kernel(reps, column, where_ref, gs_ref, w_ref, slope_ref, norm_ref, up_ref, acc_ref, sums_ref, *rest):
    parts, gu_ref = (rest[:-1], rest[-1])
    i = pl.program_id(0)
    total = jnp.zeros((1, D), F32)
    for m in range(0, gs_ref.shape[0], TILE):
        rows = slice(m, m + TILE)
        gu = (dot_t(gs_ref[rows, :], w_ref[...]) * slope_ref[rows, :].astype(F32)).astype(BF)
        gu_ref[rows, :] = gu
        total = total + col_sum(gu.astype(F32))
    sums_ref[pl.ds(column(i, where_ref), 1), :] = total
    for m in range(0, gs_ref.shape[0], TILE):
        rows = slice(m, m + TILE)
        before = jnp.where(i == 0, 0.0, acc_ref[rows, :])
        acc_ref[rows, :] = before + dot_t(gu_ref[rows, :], up_ref[...])
    grad = t_dot(norm_ref[...], gu_ref[...]).astype(BF)
    per = FF // D // reps
    for q in range(reps):

        @pl.when(i // per == reps - 1 - q)
        def put(q=q):
            parts[q][...] = grad


def gelu_back(plan, order, gs, w_down, slope, norm, w_up):
    rows = gs.shape[0]
    reps = plan.reps
    per = FF // D // reps

    def column(i, table):
        return (table[1] ^ reps - 1 - i // per) * per + i % per

    def held(q):
        return pl.BlockSpec((D, D), lambda i, table: (0, jnp.clip(i - (reps - 1 - q) * per, 0, per - 1)))
    acc, sums, *parts = pl.pallas_call(partial(gelu_back_kernel, reps, column), out_shape=(shape((rows, D), F32), shape((8, D), F32)) + (shape((D, FF // reps), BF),) * reps, grid_spec=pltpu.PrefetchScalarGridSpec(num_scalar_prefetch=1, grid=(FF // D,), in_specs=[vmem(), pl.BlockSpec((D, D), lambda i, table: (column(i, table), 0)), pl.BlockSpec((rows, D), lambda i, table: (0, column(i, table))), vmem(), pl.BlockSpec((D, D), lambda i, table: (0, column(i, table)))], out_specs=[still((rows, D)), still((8, D))] + [held(q) for q in range(reps)], scratch_shapes=[pltpu.VMEM((rows, D), BF)]), compiler_params=params(28), name='gelu_back', cost_estimate=behind(20))(order.where, gs, stay(w_down), stay(slope), norm, stay(w_up))
    return (acc, sums, parts)


def hidden_back_kernel(where_ref, acc_ref, second_ref, hat_ref, rstd_ref, w_ref, vec_ref, go_ref, ga_ref, sums_ref):

    @pl.when(pl.program_id(0) == 0)
    def clear():
        sums_ref[...] = jnp.zeros_like(sums_ref)
    grad = acc_ref[...] + second_ref[...]
    hat = hat_ref[...]
    hidden = norm_back(grad, hat, rstd_ref[...], vec_ref[10:11, :])
    go = hidden.astype(BF)
    go_ref[...] = go
    sums_ref[0:1, :] += col_sum(go.astype(F32))
    sums_ref[1:2, :] += col_sum(grad)
    sums_ref[2:3, :] += col_sum(grad * hat)
    ga_ref[...] = dot_t(go, w_ref[...]).astype(BF)


def hidden_back(order, acc, second, hat, rstd, w_one, vec):
    rows = acc.shape[0]
    return pl.pallas_call(hidden_back_kernel, grid=(rows // TILE,), out_shape=(shape((rows, D), BF), shape((rows, D), BF), shape((8, D), F32)), in_specs=[smem()] + [rows_at(D)] * 3 + [rows_at(1), still((D, D), (0, AT_OUT // D)), still(vec.shape)], out_specs=[rows_at(D), rows_at(D), still((8, D))], compiler_params=params(20), name='hidden_back', cost_estimate=behind(5))(order.where, acc, stay(second), stay(hat), stay(rstd), stay(w_one), vec)


def pair_back(pair, block, rows, ga_ref, proj_ref, probs_ref, low, high):
    q = proj_ref[rows, pair * 128:(pair + 1) * 128]
    k = proj_ref[rows, D + pair * 128:D + (pair + 1) * 128]
    v = proj_ref[rows, 2 * D + pair * 128:2 * D + (pair + 1) * 128]
    a = ga_ref[rows, pair * 128:(pair + 1) * 128]
    a2 = jnp.concatenate([a * low, a * high], 0)
    q2 = jnp.concatenate([q * low, q * high], 0)
    k2 = jnp.concatenate([k * low, k * high], 0)
    p = probs_ref[block, pair]
    dp = dot_t(v, a2)
    pf = p.astype(F32)
    ds = (pf * (dp - jnp.sum(pf * dp, 0, keepdims=True)) * HEAD ** (-0.5)).astype(BF)
    tall = jnp.concatenate([ds[:, :BLOCK], ds[:, BLOCK:]], 0)
    return (t_dot(tall, k2).astype(BF), dot(ds, q2).astype(BF), dot(p, a2).astype(BF))


def heads_back(first, count, at, ga_ref, proj_ref, probs_ref, gp_ref):
    low, high = lane_masks()
    for block in range(256 // BLOCK):
        rows = slice(block * BLOCK, (block + 1) * BLOCK)
        to = pl.ds(pl.multiple_of(at + block * BLOCK, BLOCK), BLOCK)
        for j in range(count):
            three = pair_back(first + j, block, rows, ga_ref, proj_ref, probs_ref, low, high)
            for n, grad in enumerate(three):
                lane = (n * count + j) * 128
                gp_ref[to, lane:lane + 128] = grad


def attend_back_kernel(first, count, where_ref, ga_ref, proj_ref, probs_ref, gp_ref):
    heads_back(first, count, 0, ga_ref, proj_ref, probs_ref, gp_ref)


def tile_specs(first):
    per = 256 // BLOCK
    return [pl.BlockSpec((256, D), lambda i: (i + first, 0)), pl.BlockSpec((256, 3 * D), lambda i: (i + first, 0)), pl.BlockSpec((per, PAIRS, BLOCK, 2 * BLOCK), lambda i: (i + first, 0, 0, 0))]


def attend_back(order, first, count, ga, proj, probs, rows, weight=1.0):
    wide = 3 * count * 128
    return pl.pallas_call(partial(attend_back_kernel, first, count), grid=(rows // 256,), out_shape=shape((rows, wide), BF), in_specs=[smem()] + tile_specs(0), out_specs=rows_at(wide, 256), compiler_params=params(20), name='attend_back', cost_estimate=behind(10 * count * rows / 4096 * weight))(order.where, ga, stay(proj), stay(probs))


def both_rows(x_ref, y_ref, near_ref, far_ref):
    return (t_dot(x_ref[...], near_ref[...]) + t_dot(y_ref[...], far_ref[...])).astype(BF)


def first_weights_kernel(where_ref, x_ref, y_ref, near_ref, far_ref, attn_ref, go_ref, *rest):
    parts, full_ref = (rest[:-1], rest[-1])
    full_ref[:, :D] = t_dot(attn_ref[...], go_ref[...]).astype(BF)
    end = D + near_ref.shape[1]
    full_ref[:, D:end] = both_rows(x_ref, y_ref, near_ref, far_ref)
    if end < full_ref.shape[1]:
        full_ref[:, end:] = jnp.zeros((D, full_ref.shape[1] - end), BF)
    halves(parts, where_ref[1], full_ref)


def last_weights_kernel(count, where_ref, x_ref, y_ref, near_ref, far_ref, first_near_ref, first_far_ref, up_ref, top_ref, hidden_ref, *rest):
    parts, full_ref, lines_ref = (rest[:-2], rest[-2], rest[-1])
    part = D - count * 128
    wide = count * 128
    full_ref[:, :3 * part] = both_rows(x_ref, y_ref, near_ref, far_ref)

    def sums(j, width, a_ref, b_ref):
        lanes = slice(j * width, (j + 1) * width)
        return col_sum(a_ref[:, lanes].astype(F32)) + col_sum(b_ref[:, lanes].astype(F32))
    lines_ref[...] = jnp.zeros_like(lines_ref)
    for n, j in ((0, 0), (1, 2)):
        lines_ref[n:n + 1, :wide] = sums(j, wide, first_near_ref, first_far_ref)
        lines_ref[n:n + 1, wide:] = sums(j, part, near_ref, far_ref)
    lines_ref[2:4, :] = hidden_ref[0:2, :]
    lines_ref[4:8, :] = up_ref[0:4, :]
    lines_ref[8:10, :] = top_ref[0:2, :]
    lines_ref[10:11, :] = hidden_ref[2:3, :]
    lines_ref[11:12, :] = top_ref[2:3, :]
    full_ref[:, 3 * part:3 * part + 128] = jnp.transpose(lines_ref[...]).astype(BF)
    if 3 * part + 128 < full_ref.shape[1]:
        full_ref[:, 3 * part + 128:] = jnp.zeros((D, full_ref.shape[1] - 3 * part - 128), BF)
    halves(parts, where_ref[1], full_ref)


def weights(plan, order, kernel, name, us, total, scratch, *args):
    part = total // plan.reps
    return pl.pallas_call(kernel, grid=(1,), out_shape=(shape((D, part), BF),) * plan.reps, in_specs=[smem()] + [vmem() for a in args], out_specs=[still((D, part))] * plan.reps, scratch_shapes=[pltpu.VMEM((D, total), BF)] + scratch, compiler_params=params(28), name=name, cost_estimate=behind(us))(order.where, *args)


def gx_of(count, a_ref, b_ref, w_ref, hidden):
    hidden = hidden.astype(F32)
    ca, cb = (count * 128, D - count * 128)
    for j in range(3):
        hidden = hidden + dot_t(a_ref[:, j * ca:(j + 1) * ca], w_ref[:, j * D:j * D + ca])
        hidden = hidden + dot_t(b_ref[:, j * cb:(j + 1) * cb], w_ref[:, j * D + ca:(j + 1) * D])
    return hidden


def far_back_kernel(count, where_ref, ga_ref, proj_ref, probs_ref, w_ref, hidden_ref, a_ref, b_ref, far_ref):
    heads_back(0, count, 0, ga_ref, proj_ref, probs_ref, a_ref)
    heads_back(count, PAIRS - count, 0, ga_ref, proj_ref, probs_ref, b_ref)
    far_ref[...] = gx_of(count, a_ref, b_ref, w_ref, hidden_ref[...]).astype(BF)


def far_back(order, count, ga, proj, probs, w_one, hidden):
    rows = ga.shape[0] // 2
    steps = rows // 256
    wide = 3 * count * 128
    return pl.pallas_call(partial(far_back_kernel, count), grid=(steps,), out_shape=(shape((rows, wide), BF), shape((rows, 3 * D - wide), BF), shape((rows, D), BF)), in_specs=[smem()] + tile_specs(steps) + [still((D, 3 * D)), pl.BlockSpec((256, D), lambda i: (i + steps, 0))], out_specs=[rows_at(wide, 256), rows_at(3 * D - wide, 256), rows_at(D, 256)], compiler_params=params(24), name='far_back', cost_estimate=behind(11))(order.where, ga, stay(proj), stay(probs), stay(w_one), stay(hidden))


def token_back_kernel(count, where_ref, a_ref, b_ref, w_ref, hidden_ref, own_ref):
    own_ref[...] = gx_of(count, a_ref, b_ref, w_ref, hidden_ref[...])


def token_back(order, count, ga, gb, w_one, hidden):
    rows = gb.shape[0]
    return pl.pallas_call(partial(token_back_kernel, count), grid=(rows // TILE,), out_shape=shape((rows, D), F32), in_specs=[smem(), rows_at(ga.shape[1]), rows_at(gb.shape[1]), still((D, 3 * D)), rows_at(D)], out_specs=rows_at(D), compiler_params=params(24), name='token_back', cost_estimate=behind(4))(order.where, ga, gb, stay(w_one), stay(hidden))


def on_device(plan, query_tokens, passage_tokens, query_cot, passage_cot, positives, w_qkv, w_out, w_up, w_down, biases, gains):
    me = lax.axis_index('dp')
    core = lax.axis_index('rep')
    tower = me >> 2 & 1
    span = jnp.where(tower == 0, query_tokens.shape[1], passage_tokens.shape[1])
    where = jnp.stack([me, core, tower, span]).astype(jnp.int32)
    swap = plan.along(1)

    def exchange(a, b, *others):
        a, b = (a.reshape(-1, D), b.reshape(-1, D))
        away = jnp.where(tower == 0, b, a)
        return (jnp.where(tower == 0, a, b), send(after(away, *others) if others else away, swap))

    def merged(own, back):
        a = jnp.where(tower == 0, own, back)
        b = jnp.where(tower == 0, back, own)
        return (a.reshape(query_tokens.shape), b.reshape(passage_tokens.shape))
    order = Order(where)
    mine, other, mine2, other2, mine3, other3 = shards_of(plan, order, w_qkv, w_out, jnp.swapaxes(biases, 0, 1), gains, w_up, w_down)
    z1 = gather_line(plan, mine, other)
    both2 = jnp.concatenate([mine2, send(other2, swap)], 0)
    both3 = jnp.concatenate([mine3, send(other3, swap)], 0)
    z2 = gather_steps(plan, both2, z1)
    p1 = gather_plane(plan, z1, z2, both3)
    z3 = gather_steps(plan, both3, z2)
    x_mine, x_got = exchange(query_tokens, passage_tokens, z3)
    w_one = gather_cores(plan, order, p1)
    p2 = gather_plane(plan, z2)
    p3 = gather_plane(plan, after(z3, p2[0]))
    order.done(p2[0])
    first = order.done(attend(order, x_mine, w_one, 0))
    proj, probs, attn, hat1, rstd1, norm, vec, cls_b = order.done(attend(order, x_got, w_one, 1, first[:6]))
    w_two = gather_cores(plan, order, tuple((after(b, first[6]) for b in p2)))
    half_up = order.done(up(order, norm, w_two, vec, 0))
    w_three = gather_cores(plan, order, tuple((after(b, norm) for b in p3)))
    msg = first_rows(order, first[7], cls_b, w_two, w_three, vec, positives)
    cot_mine, cot_got = exchange(query_cot, passage_cot, norm)
    loss = Contrast(plan, order, msg, positives.shape[0])
    act, slope = order.done(up(order, norm, w_two, vec, 1, half_up))
    loss.pack()
    cot = jnp.concatenate([cot_mine, cot_got], 0)
    out_own, out_far, hat2, rstd2 = order.done(down(order, act, w_three, hat1, vec))
    out_back = send(out_far, swap)
    loss.join()
    order.done(cot)
    query_loss, cls_grad = loss.loss()
    second, gs, sums_top, g_down = order.done(top(plan, order, cot, cls_grad, hat2, rstd2, vec, act))
    down_part = Scatter(plan, order, g_down, w_down.shape[1])
    acc, sums_up, g_up = order.done(gelu_back(plan, order, gs, w_three, slope, norm, w_two))
    up_part = Scatter(plan, order, g_up, w_up.shape[1])
    order.done(out_back)
    down_part.one()
    go, ga, sums = order.done(hidden_back(order, acc, second, hat1, rstd1, w_one, vec))
    up_part.one()
    split = 4
    half = ga.shape[0] // 2
    hidden = go
    far_a, far_b, gx_far = order.done(far_back(order, split, ga, proj, probs, w_one, go))
    gx_back = send(gx_far, swap)
    near_a = order.done(attend_back(order, 0, split, ga, proj, probs, half))
    total = wide(3 * split * 128 + D, plan.reps)
    args = (x_mine, x_got, near_a, far_a, stay(attn), go)
    g_a = order.done(weights(plan, order, first_weights_kernel, 'first_weights', 5, total, [], *args))
    a_part = Scatter(plan, order, g_a, w_qkv.shape[1])
    down_part.two()
    up_part.two()
    order.done(gx_back)
    near_b = order.done(attend_back(order, split, PAIRS - split, ga, proj, probs, half))
    down_part.three()
    a_part.one()
    up_part.three()
    total = wide(3 * (D - split * 128) + 128, plan.reps)
    scratch = [pltpu.VMEM((128, D), F32)]
    args = (x_mine, x_got, near_b, far_b, near_a, far_a, sums_up, sums_top, sums)
    kernel = partial(last_weights_kernel, split)
    g_b = order.done(weights(plan, order, kernel, 'last_weights', 4, total, scratch, *args))
    b_part = Scatter(plan, order, g_b, w_qkv.shape[1])
    gx_own = order.done(token_back(order, split, near_a, near_b, w_one, go))
    a_part.two()
    b_part.one()
    down_part.four()
    up_part.four()
    a_part.three()
    b_part.two()
    down_part.last()
    up_part.last()
    b_part.three()
    a_part.four()
    (grad_down,) = finish(plan, order, [down_part], [[(0, D, 0, 0)]], [w_down.shape])
    (grad_up,) = finish(plan, order, [up_part], [[(0, FF, 0, 0)]], [w_up.shape])
    b_part.four()
    a_part.last()
    b_part.last()
    query_out, passage_out = merged(out_own, after(out_back, b_part.out))
    query_grad, passage_grad = merged(gx_own, after(gx_back, b_part.out).astype(F32))
    qa, qb = (split * 128, D - split * 128)
    spans_a = [(0, D, 1, 0)] + [(D + j * qa, qa, 0, j * D) for j in range(3)]
    spans_b = [(j * qb, qb, 0, j * D + qa) for j in range(3)] + [(3 * qb, 128, 2, 0)]
    shapes = [w_qkv.shape, w_out.shape, (biases.shape[1], 2, biases.shape[2]), gains.shape]
    grads = finish(plan, order, [a_part, b_part], [spans_a, spans_b], shapes, 2)
    return (query_out, passage_out, query_grad, passage_grad, query_loss, grads[0], grads[1], grad_up, grad_down, jnp.swapaxes(grads[2], 0, 1), grads[3])


def solution(mesh):
    plan = Plan(mesh.shape['dp'], mesh.shape['rep'])
    rows = P(('dp', 'rep'), None, None)
    shards = P(None, 'dp', None)
    lanes = P(None, None, 'dp')
    return jax.shard_map(partial(on_device, plan), mesh=mesh, in_specs=(rows,) * 4 + (P(('dp', 'rep'), None),) + (shards,) * 4 + (lanes,) * 2, out_specs=(rows,) * 4 + (P(('dp', 'rep')),) + (shards,) * 4 + (lanes,) * 2, check_vma=False)
```

```python
from functools import partial
import jax
import jax.numpy as jnp
from jax import lax
from jax.experimental import pallas as pl
from jax.experimental.pallas import tpu as pltpu
from jax.sharding import PartitionSpec as P
AXES = ('dp', 'rep')
BF = jnp.bfloat16
F32 = jnp.float32
D = 768
FF = 3072
HEADS = 12
HEAD = 64
PAIRS = HEADS // 2
BLOCK = 128
TILE = 256
EPS = 1e-05
LOSS_WEIGHT = 32.0
MIB = 2 ** 20
AT_OUT = 3 * D
AT_VEC = 4 * D


def smem():
    return pl.BlockSpec(memory_space=pltpu.SMEM)


def vmem():
    return pl.BlockSpec(memory_space=pltpu.VMEM)


def cost(us):
    return pl.CostEstimate(flops=int(us * 1000000000.0), transcendentals=0, bytes_accessed=int(us * 3000000.0))


def behind(us):
    return cost(4.0 * us)


def params(mib):
    return pltpu.CompilerParams(vmem_limit_bytes=int(mib) * MIB)


def still(shape, at=None):
    index = at if at is not None else (0,) * len(shape)
    return pl.BlockSpec(shape, lambda i, *_: index, pipeline_mode=pl.Buffered(1))


def rows_at(width, rows=TILE):
    return pl.BlockSpec((rows, width), lambda i, *_: (i, 0))


def shape(dims, dtype):
    return jax.ShapeDtypeStruct(dims, dtype)


def far(dims, dtype):
    return pltpu.HBM(dims, dtype)


def stay(v):
    return pltpu.with_memory_space_constraint(v, pltpu.HBM)


def after(v, *others):
    return lax.optimization_barrier((v,) + others)[0]


class Order:
    def __init__(self, where):
        self.where = where

    def done(self, out):
        self.where = after(self.where, out)
        return out


def in_vmem(kernel, name, us, outs, *args, mib=24):
    return pl.pallas_call(kernel, out_shape=tuple((shape(*o) for o in outs)), in_specs=[smem() if a.ndim == 1 else vmem() for a in args], out_specs=tuple((vmem() for _ in outs)), compiler_params=params(mib), name=name, cost_estimate=cost(us))(*args)


def wide(width, reps):
    unit = 128 * reps
    return -(-width // unit) * unit


def by_core(core, reps, width, move):
    if width % 128 == 0:
        move(pl.ds(pl.multiple_of(core * width, 128), width))
        return
    for c in range(reps):

        @pl.when(core == c)
        def one(c=c):
            move(slice(c * width, (c + 1) * width))


def halves(refs, core, source):
    width = refs[0].shape[1]
    for q, ref in enumerate(refs):

        def move(lanes, ref=ref):
            ref[...] = source[:, lanes]
        by_core(core ^ q, len(refs), width, move)


def send(v, pairs):
    return lax.ppermute(v, AXES, pairs)


class Plan:
    def __init__(self, n, reps):
        self.n, self.reps, self.depth = (n, reps, n // 4)

    def pairs(self, move):
        return [(d * self.reps + r, (d ^ move(r)[0]) * self.reps + (r ^ move(r)[1])) for d in range(self.n) for r in range(self.reps)]

    def along(self, k):
        return self.pairs(lambda r: (4 * k, 0))

    def first(self):
        return self.pairs(lambda r: (1 + r % 2, 0))

    def second(self):
        return self.pairs(lambda r: (2 - r % 2, 0))

    def sibling(self, q):
        return self.pairs(lambda r: (0, q))


def assemble_kernel(depth, reps, width, where_ref, *refs):
    bufs, out = (refs[:2 * reps], refs[2 * reps])
    me, core = (where_ref[0], where_ref[1])
    for q in range(reps):
        owner = core ^ q
        p1 = 1 + owner % 2
        p2 = 2 - owner % 2

        def move(lanes, q=q, p1=p1, p2=p2):
            for b in range(2):
                for f in range(2):
                    for k in range(depth):
                        dst = me ^ b * p2 ^ f * p1 ^ 4 * k
                        out[pl.ds(dst, 1), :, lanes] = bufs[q * 2 + b][pl.ds(f * depth + k, 1)]
        by_core(owner, reps, width, move)


def shards_kernel(reps, where_ref, qkv_ref, out_ref, bias_ref, gain_ref, up_ref, down_ref, *rest):
    outs, full_ref = (rest[:-1], rest[-1])
    core, tower = (where_ref[1], where_ref[2])
    spare = full_ref.shape[2] - AT_VEC

    def turned(rows, at):
        i = lax.broadcasted_iota(jnp.int32, (rows.shape[0], spare), 0)
        j = lax.broadcasted_iota(jnp.int32, (rows.shape[0], spare), 1)
        return t_dot(rows.astype(BF), jnp.where(i + at == j, 1.0, 0.0).astype(BF))
    for n in range(2):
        t = pl.ds(tower if n == 0 else 1 - tower, 1)
        full_ref[:, :, :AT_OUT] = qkv_ref[t]
        full_ref[:, :, AT_OUT:AT_VEC] = out_ref[t]
        biases = bias_ref[...].astype(F32)
        biases = jnp.where(tower == n, biases[:, 0, :], biases[:, 1, :])
        gains = gain_ref[t][0].astype(F32)
        full_ref[0, :, AT_VEC:] = (turned(biases, 0) + turned(gains, biases.shape[0])).astype(BF)
        for c, ref in enumerate((full_ref, up_ref, down_ref)):
            put = outs[2 * c + n]

            def move(lanes, ref=ref, put=put, t=t):
                put[...] = ref[:, :, lanes] if ref is full_ref else ref[t, :, lanes]
            by_core(core, reps, put.shape[2], move)


def shards_of(plan, order, w_qkv, w_out, biases, gains, w_up, w_down):
    reps = plan.reps
    one = wide(AT_VEC + 128, reps)
    outs = []
    for rows, width in ((w_qkv.shape[1], one), (w_up.shape[1], FF), (w_down.shape[1], D)):
        outs += [shape((1, rows, width // reps), BF)] * 2
    args = (w_qkv, w_out, biases, gains, w_up, w_down)
    got = pl.pallas_call(partial(shards_kernel, reps), grid=(1,), out_shape=tuple(outs), in_specs=[smem()] + [still(a.shape) for a in args], out_specs=[still(o.shape) for o in outs], scratch_shapes=[pltpu.VMEM((1, w_qkv.shape[1], one), BF)], compiler_params=params(24), name='shards', cost_estimate=cost(2))(order.where, *[stay(a) for a in args])
    return order.done(got)


def join_kernel(where_ref, *refs):
    ins, out_ref = (refs[:-1], refs[-1])
    at = 0
    for ref in ins:
        out_ref[at:at + ref.shape[0]] = ref[...]
        at += ref.shape[0]


def join(order, *bufs):
    total = sum((b.shape[0] for b in bufs))
    outs = (((total,) + bufs[0].shape[1:], bufs[0].dtype),)
    return order.done(in_vmem(join_kernel, 'join', 0.5, outs, order.where, *bufs))[0]


def gather_line(plan, mine, other):
    got = [send(other if k % 2 else mine, plan.along(k)) for k in range(1, plan.depth)]
    return jnp.concatenate([mine] + got, 0)


def gather_steps(plan, both, *others):
    z = both
    k = 2
    while k < plan.depth:
        if others:
            z, others = (after(z, *others), ())
        z = jnp.concatenate([z, send(z, plan.along(k))], 0)
        k *= 2
    return z


def gather_plane(plan, z, *others):
    near = jnp.concatenate([z, send(z, plan.first())], 0)
    if others:
        near = after(near, *others)
    return (near, send(near, plan.second()))


def gather_cores(plan, order, bufs):
    rows, width = bufs[0].shape[1:]
    bufs = list(bufs)
    for q in range(1, plan.reps):
        bufs += [send(b, plan.sibling(q)) for b in bufs[:2]]
    full = pl.pallas_call(partial(assemble_kernel, plan.depth, plan.reps, width), out_shape=jax.ShapeDtypeStruct((plan.n, rows, width * plan.reps), BF), in_specs=[smem()] + [vmem()] * len(bufs), out_specs=vmem(), compiler_params=params(24), name='assemble', cost_estimate=cost(2))(order.where, *bufs)
    order.done(full)
    return full.reshape(plan.n * rows, width * plan.reps)


def add_kernel(depth, where_ref, a_ref, b_ref, s_ref, k_ref):
    me, core = (where_ref[0], where_ref[1])
    p1 = 1 + core % 2
    p2 = 2 - core % 2
    for j in range(4 * depth):
        at = me ^ (1 - j // (2 * depth)) * p1 ^ (1 - j // depth % 2) * p2 ^ 4 * (j % depth)
        o_ref, to = (s_ref, j) if j < 2 * depth else (k_ref, j - 2 * depth)
        o_ref[to] = (a_ref[at].astype(F32) + b_ref[at].astype(F32)).astype(BF)


def two_kernel(where_ref, k_ref, r_ref, s_ref, o_ref):
    q = s_ref.shape[0]
    for j in range(2 * q):
        total = (k_ref[j].astype(F32) + r_ref[j].astype(F32)).astype(BF)
        if j < q:
            s_ref[j] = total
        else:
            o_ref[j - q] = total


def line_kernel(where_ref, k_ref, r_ref, s_ref, o_ref):
    half = o_ref.shape[0]
    for j in range(2 * half):
        total = (k_ref[j].astype(F32) + r_ref[j].astype(F32)).astype(BF)
        if j < half:
            o_ref[j] = total
        else:
            s_ref[j - half] = total


def last_kernel(where_ref, own_ref, got_ref, out):
    tower = where_ref[2]
    out[pl.ds(tower, 1)] = own_ref[...]
    out[pl.ds(1 - tower, 1)] = got_ref[...]


def plus(a, b):
    return (a.astype(F32) + b.astype(F32)).astype(BF)


class Scatter:
    def __init__(self, plan, order, parts, rows):
        self.plan, self.order, self.rows = (plan, order, rows)
        self.width = parts[0].shape[1]
        parts = [p.reshape(plan.n, rows, self.width) for p in parts]
        self.own = parts[0]
        got = [send(parts[q], plan.sibling(q)) for q in range(1, plan.reps)]
        self.rest = got[0]
        for o in got[1:]:
            self.rest = plus(self.rest, o)

    def run(self, kernel, name, us, outs, *args):
        return self.order.done(in_vmem(kernel, name, us, outs, self.order.where, *args))

    def one(self):
        plan = self.plan
        n = plan.n
        whole = (n, self.rows, self.width)
        half = shape((n // 2, self.rows, self.width), BF)
        hs, self.hk = self.order.done(pl.pallas_call(partial(add_kernel, plan.depth), out_shape=(half, half), in_specs=[smem(), vmem(), vmem()], out_specs=(vmem(), vmem()), compiler_params=params(24), name='pick_add', cost_estimate=behind(3))(self.order.where, self.own, self.rest))
        self.r1 = send(hs, plan.first())
        return

    def two(self):
        quarter = ((self.plan.n // 4, self.rows, self.width), BF)
        ks, self.kk = self.run(two_kernel, 'add_two', 1, (quarter, quarter), self.hk, self.r1)
        self.r2 = send(ks, self.plan.second())

    def line(self):
        n = self.kk.shape[0] // 2
        half = ((n, self.rows, self.width), BF)
        out, self.kk = self.run(line_kernel, 'add_line', 1, (half, half), self.kk, self.r2)
        self.r2 = send(out, self.plan.along(n))
        return out

    def three(self):
        self.out = self.line()

    def four(self):
        while self.kk.shape[0] > 1:
            self.out = self.line()

    def last(self):
        plan = self.plan
        outs = (((2, self.rows, self.width), BF),)
        pair, = self.run(last_kernel, 'add_last', 1, outs, self.kk, self.r2)
        self.ends = [pair] + [send(pair, plan.sibling(q)) for q in range(1, plan.reps)]


def finish_kernel(reps, spans, vec, where_ref, *refs):
    chunks = len(spans)
    ins, outs = (refs[:chunks * reps], refs[chunks * reps:])
    core = where_ref[1]
    for c in range(chunks):
        parts = ins[c * reps:(c + 1) * reps]
        width = parts[0].shape[2]
        for q in range(reps):
            for mine in range(reps):

                @pl.when(core ^ q == mine)
                def copy(c=c, parts=parts, q=q, mine=mine):
                    for at, size, out, to in spans[c]:
                        low, high = (max(at, mine * width), min(at + size, (mine + 1) * width))
                        if low >= high:
                            continue
                        lanes = slice(low - mine * width, high - mine * width)
                        if out == vec:
                            turn(parts[q], lanes, low - at, outs[out], outs[out + 1])
                        else:
                            outs[out][:, :, to + low - at:to + high - at] = parts[q][:, :, lanes].astype(F32)


def turn(part_ref, lanes, at, bias_ref, gain_ref):
    for t in range(2):
        columns = part_ref[t, :, lanes]
        count = bias_ref.shape[0]
        for start, n in ((0, count), (count, gain_ref.shape[1])):
            i = lax.broadcasted_iota(jnp.int32, (n, columns.shape[1]), 0)
            j = lax.broadcasted_iota(jnp.int32, (n, columns.shape[1]), 1)
            rows = dot_t(jnp.where(i + start == j + at, 1.0, 0.0).astype(BF), columns)
            if start == 0:
                bias_ref[:, t, :] = rows
            else:
                gain_ref[t] = rows


def finish(plan, order, chunks, spans, shapes, vec=-1):
    outs = tuple(((s, F32) for s in shapes))
    args = [p for c in chunks for p in c.ends]
    kernel = partial(finish_kernel, plan.reps, spans, vec)
    return order.done(in_vmem(kernel, 'finish', 2, outs, order.where, *args))


def dot(a, b):
    return jnp.dot(a, b, preferred_element_type=F32)


def dot_t(a, b):
    return lax.dot_general(a, b, (((1,), (1,)), ((), ())), preferred_element_type=F32)


def t_dot(a, b):
    return lax.dot_general(a, b, (((0,), (0,)), ((), ())), preferred_element_type=F32)


def normalize(h):
    center = h - jnp.mean(h, -1, keepdims=True)
    rstd = lax.rsqrt(jnp.mean(center * center, -1, keepdims=True) + EPS)
    return (center * rstd, rstd)


def lane_masks():
    lane = lax.broadcasted_iota(jnp.int32, (1, 2 * HEAD), 1)
    low = (lane < HEAD).astype(F32).astype(BF)
    return (low, (1.0 - low.astype(F32)).astype(BF))


def attend_kernel(part, where_ref, x_ref, w_ref, *rest):
    proj_ref, probs_ref, attn_ref, hat_ref, rstd_ref, norm_ref, vec_ref, cls_ref, bias_ref = rest[-9:]

    @pl.when(pl.program_id(0) == 0)
    def prepare():
        vec_ref[...] = jnp.transpose(w_ref[:, AT_VEC:AT_VEC + 128].astype(F32))
        span = where_ref[3]
        row = lax.broadcasted_iota(jnp.int32, (BLOCK, 2 * BLOCK), 0)
        col = lax.broadcasted_iota(jnp.int32, (BLOCK, 2 * BLOCK), 1) % BLOCK
        bias_ref[...] = jnp.where(row ^ col < span, 0.0, -1e+30)
    x = x_ref[...]
    for j in range(3):
        part = dot(x, w_ref[:, j * D:(j + 1) * D])
        if j != 1:
            part = part + vec_ref[j // 2:j // 2 + 1, :]
        proj_ref[:, j * D:(j + 1) * D] = part.astype(BF)
    low, high = lane_masks()
    bias = bias_ref[...]
    for blk in range(256 // BLOCK):
        rows = slice(blk * BLOCK, (blk + 1) * BLOCK)
        for pair in range(PAIRS):
            lanes = slice(pair * 128, (pair + 1) * 128)
            q = proj_ref[rows, lanes]
            k = proj_ref[rows, D + pair * 128:D + (pair + 1) * 128]
            v = proj_ref[rows, 2 * D + pair * 128:2 * D + (pair + 1) * 128]
            s = dot_t(k, jnp.concatenate([q * low, q * high], 0)) * HEAD ** (-0.5) + bias
            e = jnp.exp(s - jnp.max(s, 0, keepdims=True))
            p = (e * (1.0 / jnp.sum(e, 0, keepdims=True))).astype(BF)
            probs_ref[blk, pair] = p
            tall = jnp.concatenate([p[:, :BLOCK], p[:, BLOCK:]], 0)
            attn_ref[rows, lanes] = t_dot(tall, jnp.concatenate([v * low, v * high], 0)).astype(BF)
    hidden = x.astype(F32) + (dot(attn_ref[...], w_ref[:, AT_OUT:AT_VEC]) + vec_ref[2:3, :])
    hat, rstd = normalize(hidden)
    hat_ref[...] = hat
    rstd_ref[...] = rstd
    norm = hat * vec_ref[10:11, :] + vec_ref[3:4, :]
    norm_ref[...] = norm.astype(BF)
    for j in range(8):
        cls_ref[j:j + 1, :] = norm[32 * j:32 * j + 1, :]


def attend(order, x, w_one, part, before=()):
    rows = 2 * x.shape[0]
    per = 256 // BLOCK
    steps = rows // 256 // 2
    first = part * steps

    def here(width):
        return pl.BlockSpec((256, width), lambda i: (i + first, 0))
    return pl.pallas_call(partial(attend_kernel, part), grid=(steps,), out_shape=(far((rows, 3 * D), BF), far((rows // BLOCK, PAIRS, BLOCK, 2 * BLOCK), BF), far((rows, D), BF), far((rows, D), F32), far((rows, 1), F32), far((rows, D), BF), shape((128, D), F32), shape((rows // 64, D), F32)), in_specs=[smem(), rows_at(D, 256), vmem()] + [pl.BlockSpec(memory_space=pl.ANY)] * len(before), out_specs=[here(3 * D), pl.BlockSpec((per, PAIRS, BLOCK, 2 * BLOCK), lambda i: (i + first, 0, 0, 0)), here(D), here(D), here(1), here(D), still((128, D)), rows_at(D, 8)], scratch_shapes=[pltpu.VMEM((BLOCK, 2 * BLOCK), F32)], input_output_aliases={3 + j: j for j in range(len(before))}, compiler_params=params(24), name='attend', cost_estimate=cost(7))(order.where, x, w_one, *[b for b in before])


def gelu_pair(u):
    phi = 0.5 + 0.5 * lax.erf(u * 2 ** (-0.5))
    return (u * phi, phi + u * (jnp.exp(-0.5 * u * u) * (2 * jnp.pi) ** (-0.5)))


def up_kernel(first, where_ref, norm_ref, w_ref, vec_ref, *rest):
    act_ref, slope_ref = rest[-2:]
    bias = vec_ref[pl.ds(4 + first + pl.program_id(0), 1), :]
    for m in range(0, norm_ref.shape[0], 256):
        rows = slice(m, m + 256)
        act, slope = gelu_pair(dot(norm_ref[rows, :], w_ref[...]) + bias)
        act_ref[rows, :] = act.astype(BF)
        slope_ref[rows, :] = slope.astype(BF)


def up(order, norm, w_up, vec, part, before=()):
    rows = norm.shape[0]
    steps = FF // D // 2
    first = part * steps
    col = pl.BlockSpec((rows, D), lambda i: (0, i + first))
    return pl.pallas_call(partial(up_kernel, first), grid=(steps,), out_shape=(shape((rows, FF), BF), far((rows, FF), BF)), in_specs=[smem(), still(norm.shape), pl.BlockSpec((D, D), lambda i: (0, i + first)), still(vec.shape)] + [pl.BlockSpec(memory_space=pl.ANY)] * len(before), out_specs=[col, col], input_output_aliases={4 + j: j for j in range(len(before))}, compiler_params=params(24), name='up', cost_estimate=cost(8))(order.where, norm, w_up, vec, *[b for b in before])


def down_kernel(where_ref, act_ref, w_ref, hat_ref, vec_ref, own_ref, far_ref, hat2_ref, rstd2_ref):
    normed = hat_ref[...] * vec_ref[10:11, :] + vec_ref[3:4, :]
    second = normed + (dot(act_ref[...], w_ref[...]) + vec_ref[8:9, :])
    hat, rstd = normalize(second)
    hat2_ref[...] = hat
    rstd2_ref[...] = rstd
    out = (hat * vec_ref[11:12, :] + vec_ref[9:10, :]).astype(BF)
    half = pl.num_programs(0) // 2

    @pl.when(pl.program_id(0) < half)
    def near():
        own_ref[...] = out

    @pl.when(pl.program_id(0) >= half)
    def away():
        far_ref[...] = out


def down(order, act, w_down, hat, vec):
    rows = act.shape[0]
    half = rows // 256 // 2
    near = pl.BlockSpec((256, D), lambda i: (jnp.minimum(i, half - 1), 0))
    away = pl.BlockSpec((256, D), lambda i: (jnp.maximum(i - half, 0), 0))
    return pl.pallas_call(down_kernel, grid=(rows // 256,), out_shape=(far((rows // 2, D), BF), shape((rows // 2, D), BF), shape((rows, D), F32), shape((rows, 1), F32)), in_specs=[smem(), rows_at(FF, 256), vmem(), rows_at(D, 256), still(vec.shape)], out_specs=[near, away, rows_at(D, 256), rows_at(1, 256)], compiler_params=params(24), name='down', cost_estimate=cost(8))(order.where, act, w_down, stay(hat), vec)


def first_kernel(where_ref, a_ref, b_ref, up_ref, down_ref, vec_ref, marks_ref, msg_ref):
    norm = jnp.concatenate([a_ref[...], b_ref[...]], 0)
    second = norm + vec_ref[8:9, :]
    wide = norm.astype(BF)
    for j in range(FF // D):
        u = dot(wide, up_ref[:, j * D:(j + 1) * D]) + vec_ref[4 + j:5 + j, :]
        second = second + dot(gelu_pair(u)[0].astype(BF), down_ref[j * D:(j + 1) * D, :])
    hat, _ = normalize(second)
    msg_ref[:, :D] = (hat * vec_ref[11:12, :] + vec_ref[9:10, :]).astype(BF)
    marks = marks_ref[...].astype(F32)
    pad = jnp.zeros((32 - marks.shape[0], marks.shape[1]), F32)
    msg_ref[:, D:] = jnp.concatenate([marks, pad], 0).astype(BF)


def first_rows(order, a, b, w_up, w_down, vec, positives):
    outs = (((32, D + positives.shape[1]), BF),)
    return order.done(in_vmem(first_kernel, 'first_rows', 4, outs, order.where, a, b, w_up, w_down, vec, positives))[0]


def pack_kernel(per, where_ref, *refs):
    msgs, out_ref = (refs[:-1], refs[-1])
    queries = per * 4
    pick_row = lax.broadcasted_iota(jnp.int32, (16, 32), 0)
    pick_col = lax.broadcasted_iota(jnp.int32, (16, 32), 1)
    pick = jnp.where((pick_col == pick_row * (32 // (2 * per))) & (pick_row < 2 * per), 1.0, 0.0).astype(BF)
    for n in range(len(msgs) // 2):
        for tower in range(2):

            @pl.when(where_ref[2] == tower)
            def put(n=n, tower=tower):
                zero, one = (msgs[2 * n + tower], msgs[2 * n + 1 - tower])
                out_ref[n, :32, :D] = zero[:, :D]
                out_ref[n, :queries, D:] = zero[:queries, D:]
                out_ref[n, queries:32, D:] = one[:queries, D:]
                out_ref[n, 32:, :D] = dot(pick, one[:, :D]).astype(BF)
                out_ref[n, 32:, D:] = jnp.zeros((16, out_ref.shape[2] - D), BF)


def contrast_kernel(reps, depth, per, where_ref, *refs):
    parts, loss_ref, grad_ref, acc_ref = (refs[:reps], refs[reps], refs[reps + 1], refs[reps + 2])
    me, core, tower = (where_ref[0], where_ref[1], where_ref[2])
    pieces = parts[0].shape[0]
    passages = parts[0].shape[2] - D
    cls_p = jnp.concatenate([part[:, 32:, :D].reshape(pieces * 16, D) for part in parts], 0)
    cols = cls_p.shape[0]
    col = lax.broadcasted_iota(jnp.int32, (passages, cols), 1)
    row = lax.broadcasted_iota(jnp.int32, (passages, cols), 0)
    j, slot = (col // 16, col % 16)
    base = (me | 4) ^ 8 * (j % (depth // 2)) ^ j // (depth // 2) % 4
    owner = jnp.where(slot < per, base, base ^ 4)
    passage = (owner * reps + (core ^ j // (2 * depth))) * per + slot % per
    pick = jnp.where((row == passage) & (slot < 2 * per), 1.0, 0.0).astype(BF)
    valid = lax.broadcasted_iota(jnp.int32, (1, cols), 1) % 16 < 2 * per
    acc_ref[...] = jnp.zeros_like(acc_ref)
    group = min(8, pieces)
    for q, part in enumerate(parts):
        for at in range(0, pieces, group):
            cls_q = part[at:at + group, :32, :D].reshape(group * 32, D)
            marks = dot(part[at:at + group, :32, D:].reshape(group * 32, passages), pick)
            raw = jnp.where(valid, dot_t(cls_q, cls_p) * D ** (-0.5), -1e+30)
            e = jnp.exp(raw - jnp.max(raw, -1, keepdims=True))
            total = jnp.sum(e, -1, keepdims=True)
            me_ = marks * e
            marked = jnp.sum(me_, -1, keepdims=True)
            grad = (LOSS_WEIGHT * (e / total - me_ / marked)).astype(BF)
            acc_ref[...] += t_dot(grad[:, :128], cls_q)[:16] * D ** (-0.5)
            if q == 0 and at == 0:
                loss_ref[...] = (jnp.log(total) - jnp.log(marked))[:32]
                grad_ref[...] = dot(grad[:32], cls_p) * D ** (-0.5)

    @pl.when(tower == 1)
    def passages_own():
        grad_ref[...] = jnp.zeros_like(grad_ref)
        for s in range(2 * per):
            at = s * (32 // (2 * per))
            grad_ref[at:at + 1, :] = acc_ref[s:s + 1, :]


class Contrast:

    def __init__(self, plan, order, msg, queries):
        self.plan, self.order, self.queries = (plan, order, queries)
        self.msgs = [msg] + [send(msg, plan.along(k)) for k in range(1, plan.depth)]

    def pack(self):
        plan = self.plan
        outs = (((plan.depth // 2, 48, self.msgs[0].shape[1]), BF),)
        kernel = partial(pack_kernel, self.queries // 4)
        buf, = self.order.done(in_vmem(kernel, 'pack', 1, outs, self.order.where, *self.msgs))
        self.bufs = [buf] + [send(buf, plan.pairs(lambda r, m=m: (m, 0))) for m in range(1, 4)]

    def join(self):
        plan = self.plan
        buf = join(self.order, *self.bufs)
        self.parts = [buf] + [send(buf, plan.sibling(s)) for s in range(1, plan.reps)]

    def loss(self):
        plan, order = (self.plan, self.order)
        loss, grad = order.done(pl.pallas_call(partial(contrast_kernel, plan.reps, plan.depth, self.queries // 4), out_shape=(shape((32, 1), F32), shape((32, D), F32)), in_specs=[smem()] + [vmem()] * plan.reps, out_specs=(vmem(), vmem()), scratch_shapes=[pltpu.VMEM((16, D), F32)], compiler_params=params(40), name='contrast', cost_estimate=cost(2))(order.where, *self.parts))
        at = order.where[2] * self.queries
        return (lax.dynamic_slice(loss, (at, 0), (self.queries, 1))[:, 0], grad)


def norm_back(grad, hat, rstd, gain):
    scaled = grad * gain
    a = jnp.mean(scaled, -1, keepdims=True)
    b = jnp.mean(scaled * hat, -1, keepdims=True)
    return rstd * (scaled - a - hat * b)


def col_sum(v):
    return jnp.sum(v, 0, keepdims=True)


def top_kernel(where_ref, cot_ref, cls_ref, hat_ref, rstd_ref, vec_ref, act_ref, second_ref, gs_ref, sums_ref, *rest):
    parts, full_ref = (rest[:-1], rest[-1])

    @pl.when(pl.program_id(0) == 0)
    def norm():
        groups = TILE // 32
        at_first = lax.broadcasted_iota(jnp.int32, (groups, 32, D), 1) == 0
        sums_ref[...] = jnp.zeros_like(sums_ref)
        for m in range(0, cot_ref.shape[0], TILE):
            rows = slice(m, m + TILE)
            cls = cls_ref[m // 32:(m + TILE) // 32, :].reshape(groups, 1, D)
            dout = cot_ref[rows, :].astype(F32) + jnp.where(at_first, cls, 0.0).reshape(TILE, D)
            hat = hat_ref[rows, :]
            grad = norm_back(dout, hat, rstd_ref[rows, :], vec_ref[11:12, :])
            second_ref[rows, :] = grad
            gs = grad.astype(BF)
            gs_ref[rows, :] = gs
            sums_ref[0:1, :] += col_sum(gs.astype(F32))
            sums_ref[1:2, :] += col_sum(dout)
            sums_ref[2:3, :] += col_sum(dout * hat)
    full_ref[...] = t_dot(act_ref[...], gs_ref[...]).astype(BF)
    halves(parts, where_ref[1], full_ref)


def top(plan, order, cot, cls_grad, hat2, rstd2, vec, act):
    rows = cot.shape[0]
    part = D // plan.reps
    second, gs, sums, *parts = pl.pallas_call(top_kernel, grid=(FF // D,), out_shape=(far((rows, D), F32), shape((rows, D), BF), shape((8, D), F32)) + (shape((FF, part), BF),) * plan.reps, in_specs=[smem(), vmem(), still(cls_grad.shape), vmem(), vmem(), still(vec.shape), pl.BlockSpec((rows, D), lambda i: (0, i))], out_specs=[still((rows, D)), still((rows, D)), still((8, D))] + [rows_at(part, D)] * plan.reps, scratch_shapes=[pltpu.VMEM((D, D), BF)], compiler_params=params(28), name='top', cost_estimate=behind(11))(order.where, cot, cls_grad, hat2, rstd2, vec, act)
    return (second, gs, sums, parts)


def gelu_back_kernel(reps, column, where_ref, gs_ref, w_ref, slope_ref, norm_ref, up_ref, acc_ref, sums_ref, *rest):
    parts, gu_ref = (rest[:-1], rest[-1])
    i = pl.program_id(0)
    total = jnp.zeros((1, D), F32)
    for m in range(0, gs_ref.shape[0], TILE):
        rows = slice(m, m + TILE)
        gu = (dot_t(gs_ref[rows, :], w_ref[...]) * slope_ref[rows, :].astype(F32)).astype(BF)
        gu_ref[rows, :] = gu
        total = total + col_sum(gu.astype(F32))
    sums_ref[pl.ds(column(i, where_ref), 1), :] = total
    for m in range(0, gs_ref.shape[0], TILE):
        rows = slice(m, m + TILE)
        before = jnp.where(i == 0, 0.0, acc_ref[rows, :])
        acc_ref[rows, :] = before + dot_t(gu_ref[rows, :], up_ref[...])
    grad = t_dot(norm_ref[...], gu_ref[...]).astype(BF)
    per = FF // D // reps
    for q in range(reps):

        @pl.when(i // per == reps - 1 - q)
        def put(q=q):
            parts[q][...] = grad


def gelu_back(plan, order, gs, w_down, slope, norm, w_up):
    rows = gs.shape[0]
    reps = plan.reps
    per = FF // D // reps

    def column(i, table):
        return (table[1] ^ reps - 1 - i // per) * per + i % per

    def held(q):
        return pl.BlockSpec((D, D), lambda i, table: (0, jnp.clip(i - (reps - 1 - q) * per, 0, per - 1)))
    acc, sums, *parts = pl.pallas_call(partial(gelu_back_kernel, reps, column), out_shape=(shape((rows, D), F32), shape((8, D), F32)) + (shape((D, FF // reps), BF),) * reps, grid_spec=pltpu.PrefetchScalarGridSpec(num_scalar_prefetch=1, grid=(FF // D,), in_specs=[vmem(), pl.BlockSpec((D, D), lambda i, table: (column(i, table), 0)), pl.BlockSpec((rows, D), lambda i, table: (0, column(i, table))), vmem(), pl.BlockSpec((D, D), lambda i, table: (0, column(i, table)))], out_specs=[still((rows, D)), still((8, D))] + [held(q) for q in range(reps)], scratch_shapes=[pltpu.VMEM((rows, D), BF)]), compiler_params=params(28), name='gelu_back', cost_estimate=behind(20))(order.where, gs, stay(w_down), stay(slope), norm, stay(w_up))
    return (acc, sums, parts)


def hidden_back_kernel(where_ref, acc_ref, second_ref, hat_ref, rstd_ref, w_ref, vec_ref, go_ref, ga_ref, sums_ref):

    @pl.when(pl.program_id(0) == 0)
    def clear():
        sums_ref[...] = jnp.zeros_like(sums_ref)
    grad = acc_ref[...] + second_ref[...]
    hat = hat_ref[...]
    hidden = norm_back(grad, hat, rstd_ref[...], vec_ref[10:11, :])
    go = hidden.astype(BF)
    go_ref[...] = go
    sums_ref[0:1, :] += col_sum(go.astype(F32))
    sums_ref[1:2, :] += col_sum(grad)
    sums_ref[2:3, :] += col_sum(grad * hat)
    ga_ref[...] = dot_t(go, w_ref[...]).astype(BF)


def hidden_back(order, acc, second, hat, rstd, w_one, vec):
    rows = acc.shape[0]
    return pl.pallas_call(hidden_back_kernel, grid=(rows // TILE,), out_shape=(shape((rows, D), BF), shape((rows, D), BF), shape((8, D), F32)), in_specs=[smem()] + [rows_at(D)] * 3 + [rows_at(1), still((D, D), (0, AT_OUT // D)), still(vec.shape)], out_specs=[rows_at(D), rows_at(D), still((8, D))], compiler_params=params(20), name='hidden_back', cost_estimate=behind(5))(order.where, acc, stay(second), stay(hat), stay(rstd), stay(w_one), vec)


def pair_back(pair, block, rows, ga_ref, proj_ref, probs_ref, low, high):
    q = proj_ref[rows, pair * 128:(pair + 1) * 128]
    k = proj_ref[rows, D + pair * 128:D + (pair + 1) * 128]
    v = proj_ref[rows, 2 * D + pair * 128:2 * D + (pair + 1) * 128]
    a = ga_ref[rows, pair * 128:(pair + 1) * 128]
    a2 = jnp.concatenate([a * low, a * high], 0)
    q2 = jnp.concatenate([q * low, q * high], 0)
    k2 = jnp.concatenate([k * low, k * high], 0)
    p = probs_ref[block, pair]
    dp = dot_t(v, a2)
    pf = p.astype(F32)
    ds = (pf * (dp - jnp.sum(pf * dp, 0, keepdims=True)) * HEAD ** (-0.5)).astype(BF)
    tall = jnp.concatenate([ds[:, :BLOCK], ds[:, BLOCK:]], 0)
    return (t_dot(tall, k2).astype(BF), dot(ds, q2).astype(BF), dot(p, a2).astype(BF))


def heads_back(first, count, at, ga_ref, proj_ref, probs_ref, gp_ref):
    low, high = lane_masks()
    for block in range(256 // BLOCK):
        rows = slice(block * BLOCK, (block + 1) * BLOCK)
        to = pl.ds(pl.multiple_of(at + block * BLOCK, BLOCK), BLOCK)
        for j in range(count):
            three = pair_back(first + j, block, rows, ga_ref, proj_ref, probs_ref, low, high)
            for n, grad in enumerate(three):
                lane = (n * count + j) * 128
                gp_ref[to, lane:lane + 128] = grad


def attend_back_kernel(first, count, where_ref, ga_ref, proj_ref, probs_ref, gp_ref):
    heads_back(first, count, 0, ga_ref, proj_ref, probs_ref, gp_ref)


def tile_specs(first):
    per = 256 // BLOCK
    return [pl.BlockSpec((256, D), lambda i: (i + first, 0)), pl.BlockSpec((256, 3 * D), lambda i: (i + first, 0)), pl.BlockSpec((per, PAIRS, BLOCK, 2 * BLOCK), lambda i: (i + first, 0, 0, 0))]


def attend_back(order, first, count, ga, proj, probs, rows, weight=1.0):
    wide = 3 * count * 128
    return pl.pallas_call(partial(attend_back_kernel, first, count), grid=(rows // 256,), out_shape=shape((rows, wide), BF), in_specs=[smem()] + tile_specs(0), out_specs=rows_at(wide, 256), compiler_params=params(20), name='attend_back', cost_estimate=behind(10 * count * rows / 4096 * weight))(order.where, ga, stay(proj), stay(probs))


def both_rows(x_ref, y_ref, near_ref, far_ref):
    return (t_dot(x_ref[...], near_ref[...]) + t_dot(y_ref[...], far_ref[...])).astype(BF)


def first_weights_kernel(where_ref, x_ref, y_ref, near_ref, far_ref, attn_ref, go_ref, *rest):
    parts, full_ref = (rest[:-1], rest[-1])
    full_ref[:, :D] = t_dot(attn_ref[...], go_ref[...]).astype(BF)
    end = D + near_ref.shape[1]
    full_ref[:, D:end] = both_rows(x_ref, y_ref, near_ref, far_ref)
    if end < full_ref.shape[1]:
        full_ref[:, end:] = jnp.zeros((D, full_ref.shape[1] - end), BF)
    halves(parts, where_ref[1], full_ref)


def last_weights_kernel(count, where_ref, x_ref, y_ref, near_ref, far_ref, first_near_ref, first_far_ref, up_ref, top_ref, hidden_ref, *rest):
    parts, full_ref, lines_ref = (rest[:-2], rest[-2], rest[-1])
    part = D - count * 128
    wide = count * 128
    full_ref[:, :3 * part] = both_rows(x_ref, y_ref, near_ref, far_ref)

    def sums(j, width, a_ref, b_ref):
        lanes = slice(j * width, (j + 1) * width)
        return col_sum(a_ref[:, lanes].astype(F32)) + col_sum(b_ref[:, lanes].astype(F32))
    lines_ref[...] = jnp.zeros_like(lines_ref)
    for n, j in ((0, 0), (1, 2)):
        lines_ref[n:n + 1, :wide] = sums(j, wide, first_near_ref, first_far_ref)
        lines_ref[n:n + 1, wide:] = sums(j, part, near_ref, far_ref)
    lines_ref[2:4, :] = hidden_ref[0:2, :]
    lines_ref[4:8, :] = up_ref[0:4, :]
    lines_ref[8:10, :] = top_ref[0:2, :]
    lines_ref[10:11, :] = hidden_ref[2:3, :]
    lines_ref[11:12, :] = top_ref[2:3, :]
    full_ref[:, 3 * part:3 * part + 128] = jnp.transpose(lines_ref[...]).astype(BF)
    if 3 * part + 128 < full_ref.shape[1]:
        full_ref[:, 3 * part + 128:] = jnp.zeros((D, full_ref.shape[1] - 3 * part - 128), BF)
    halves(parts, where_ref[1], full_ref)


def weights(plan, order, kernel, name, us, total, scratch, *args):
    part = total // plan.reps
    return pl.pallas_call(kernel, grid=(1,), out_shape=(shape((D, part), BF),) * plan.reps, in_specs=[smem()] + [vmem() for a in args], out_specs=[still((D, part))] * plan.reps, scratch_shapes=[pltpu.VMEM((D, total), BF)] + scratch, compiler_params=params(28), name=name, cost_estimate=behind(us))(order.where, *args)


def gx_of(count, a_ref, b_ref, w_ref, hidden):
    hidden = hidden.astype(F32)
    ca, cb = (count * 128, D - count * 128)
    for j in range(3):
        hidden = hidden + dot_t(a_ref[:, j * ca:(j + 1) * ca], w_ref[:, j * D:j * D + ca])
        hidden = hidden + dot_t(b_ref[:, j * cb:(j + 1) * cb], w_ref[:, j * D + ca:(j + 1) * D])
    return hidden


def far_back_kernel(count, where_ref, ga_ref, proj_ref, probs_ref, w_ref, hidden_ref, a_ref, b_ref, far_ref):
    heads_back(0, count, 0, ga_ref, proj_ref, probs_ref, a_ref)
    heads_back(count, PAIRS - count, 0, ga_ref, proj_ref, probs_ref, b_ref)
    far_ref[...] = gx_of(count, a_ref, b_ref, w_ref, hidden_ref[...]).astype(BF)


def far_back(order, count, ga, proj, probs, w_one, hidden):
    rows = ga.shape[0] // 2
    steps = rows // 256
    wide = 3 * count * 128
    return pl.pallas_call(partial(far_back_kernel, count), grid=(steps,), out_shape=(shape((rows, wide), BF), shape((rows, 3 * D - wide), BF), shape((rows, D), BF)), in_specs=[smem()] + tile_specs(steps) + [still((D, 3 * D)), pl.BlockSpec((256, D), lambda i: (i + steps, 0))], out_specs=[rows_at(wide, 256), rows_at(3 * D - wide, 256), rows_at(D, 256)], compiler_params=params(24), name='far_back', cost_estimate=behind(11))(order.where, ga, stay(proj), stay(probs), stay(w_one), stay(hidden))


def token_back_kernel(count, where_ref, a_ref, b_ref, w_ref, hidden_ref, own_ref):
    own_ref[...] = gx_of(count, a_ref, b_ref, w_ref, hidden_ref[...])


def token_back(order, count, ga, gb, w_one, hidden):
    rows = gb.shape[0]
    return pl.pallas_call(partial(token_back_kernel, count), grid=(rows // TILE,), out_shape=shape((rows, D), F32), in_specs=[smem(), rows_at(ga.shape[1]), rows_at(gb.shape[1]), still((D, 3 * D)), rows_at(D)], out_specs=rows_at(D), compiler_params=params(24), name='token_back', cost_estimate=behind(4))(order.where, ga, gb, stay(w_one), stay(hidden))


def on_device(plan, query_tokens, passage_tokens, query_cot, passage_cot, positives, w_qkv, w_out, w_up, w_down, biases, gains):
    me = lax.axis_index('dp')
    core = lax.axis_index('rep')
    tower = me >> 2 & 1
    span = jnp.where(tower == 0, query_tokens.shape[1], passage_tokens.shape[1])
    where = jnp.stack([me, core, tower, span]).astype(jnp.int32)
    swap = plan.along(1)

    def exchange(a, b, *others):
        a, b = (a.reshape(-1, D), b.reshape(-1, D))
        away = jnp.where(tower == 0, b, a)
        return (jnp.where(tower == 0, a, b), send(after(away, *others) if others else away, swap))

    def merged(own, back):
        a = jnp.where(tower == 0, own, back)
        b = jnp.where(tower == 0, back, own)
        return (a.reshape(query_tokens.shape), b.reshape(passage_tokens.shape))
    order = Order(where)
    mine, other, mine2, other2, mine3, other3 = shards_of(plan, order, w_qkv, w_out, jnp.swapaxes(biases, 0, 1), gains, w_up, w_down)
    z1 = gather_line(plan, mine, other)
    both2 = jnp.concatenate([mine2, send(other2, swap)], 0)
    both3 = jnp.concatenate([mine3, send(other3, swap)], 0)
    z2 = gather_steps(plan, both2, z1)
    p1 = gather_plane(plan, z1, z2, both3)
    z3 = gather_steps(plan, both3, z2)
    x_mine, x_got = exchange(query_tokens, passage_tokens, z3)
    w_one = gather_cores(plan, order, p1)
    p2 = gather_plane(plan, z2)
    p3 = gather_plane(plan, after(z3, p2[0]))
    order.done(p2[0])
    first = order.done(attend(order, x_mine, w_one, 0))
    proj, probs, attn, hat1, rstd1, norm, vec, cls_b = order.done(attend(order, x_got, w_one, 1, first[:6]))
    w_two = gather_cores(plan, order, tuple((after(b, first[6]) for b in p2)))
    half_up = order.done(up(order, norm, w_two, vec, 0))
    w_three = gather_cores(plan, order, tuple((after(b, norm) for b in p3)))
    msg = first_rows(order, first[7], cls_b, w_two, w_three, vec, positives)
    cot_mine, cot_got = exchange(query_cot, passage_cot, norm)
    loss = Contrast(plan, order, msg, positives.shape[0])
    act, slope = order.done(up(order, norm, w_two, vec, 1, half_up))
    loss.pack()
    cot = jnp.concatenate([cot_mine, cot_got], 0)
    out_own, out_far, hat2, rstd2 = order.done(down(order, act, w_three, hat1, vec))
    out_back = send(out_far, swap)
    loss.join()
    order.done(cot)
    query_loss, cls_grad = loss.loss()
    second, gs, sums_top, g_down = order.done(top(plan, order, cot, cls_grad, hat2, rstd2, vec, act))
    down_part = Scatter(plan, order, g_down, w_down.shape[1])
    acc, sums_up, g_up = order.done(gelu_back(plan, order, gs, w_three, slope, norm, w_two))
    up_part = Scatter(plan, order, g_up, w_up.shape[1])
    down_part.one()
    order.done(out_back)
    go, ga, sums = order.done(hidden_back(order, acc, second, hat1, rstd1, w_one, vec))
    up_part.one()
    split = 4
    half = ga.shape[0] // 2
    hidden = go
    far_a, far_b, gx_far = order.done(far_back(order, split, ga, proj, probs, w_one, go))
    gx_back = send(gx_far, swap)
    near_a = order.done(attend_back(order, 0, split, ga, proj, probs, half))
    total = wide(3 * split * 128 + D, plan.reps)
    args = (x_mine, x_got, near_a, far_a, stay(attn), go)
    g_a = order.done(weights(plan, order, first_weights_kernel, 'first_weights', 5, total, [], *args))
    a_part = Scatter(plan, order, g_a, w_qkv.shape[1])
    down_part.two()
    up_part.two()
    order.done(gx_back)
    near_b = order.done(attend_back(order, split, PAIRS - split, ga, proj, probs, half))
    down_part.three()
    a_part.one()
    up_part.three()
    total = wide(3 * (D - split * 128) + 128, plan.reps)
    scratch = [pltpu.VMEM((128, D), F32)]
    args = (x_mine, x_got, near_b, far_b, near_a, far_a, sums_up, sums_top, sums)
    kernel = partial(last_weights_kernel, split)
    g_b = order.done(weights(plan, order, kernel, 'last_weights', 4, total, scratch, *args))
    b_part = Scatter(plan, order, g_b, w_qkv.shape[1])
    gx_own = order.done(token_back(order, split, near_a, near_b, w_one, go))
    a_part.two()
    b_part.one()
    down_part.four()
    up_part.four()
    a_part.three()
    b_part.two()
    down_part.last()
    up_part.last()
    b_part.three()
    a_part.four()
    (grad_down,) = finish(plan, order, [down_part], [[(0, D, 0, 0)]], [w_down.shape])
    (grad_up,) = finish(plan, order, [up_part], [[(0, FF, 0, 0)]], [w_up.shape])
    b_part.four()
    a_part.last()
    b_part.last()
    query_out, passage_out = merged(out_own, after(out_back, b_part.out))
    query_grad, passage_grad = merged(gx_own, after(gx_back, b_part.out).astype(F32))
    qa, qb = (split * 128, D - split * 128)
    spans_a = [(0, D, 1, 0)] + [(D + j * qa, qa, 0, j * D) for j in range(3)]
    spans_b = [(j * qb, qb, 0, j * D + qa) for j in range(3)] + [(3 * qb, 128, 2, 0)]
    shapes = [w_qkv.shape, w_out.shape, (biases.shape[1], 2, biases.shape[2]), gains.shape]
    grads = finish(plan, order, [a_part, b_part], [spans_a, spans_b], shapes, 2)
    return (query_out, passage_out, query_grad, passage_grad, query_loss, grads[0], grads[1], grad_up, grad_down, jnp.swapaxes(grads[2], 0, 1), grads[3])


def solution(mesh):
    plan = Plan(mesh.shape['dp'], mesh.shape['rep'])
    rows = P(('dp', 'rep'), None, None)
    shards = P(None, 'dp', None)
    lanes = P(None, None, 'dp')
    return jax.shard_map(partial(on_device, plan), mesh=mesh, in_specs=(rows,) * 4 + (P(('dp', 'rep'), None),) + (shards,) * 4 + (lanes,) * 2, out_specs=(rows,) * 4 + (P(('dp', 'rep')),) + (shards,) * 4 + (lanes,) * 2, check_vma=False)
```
